128 devices in a mesh: ctx: 32 (over z, x, core), tp: 4 (over y).
Axes of the slice: x: 4, y: 4, z: 4, core: 2. Of those that a mesh axis runs over, the one named last changes fastest.
Arguments:
- query: bfloat16 [16384, 8192], P('ctx', 'tp'), may hold values from -12 to 12, as said below
- keys: bfloat16 [16384, 8192], P('ctx', 'tp'), may hold values from -5 to 5
- values: bfloat16 [16384, 8192], P('ctx', 'tp'), may hold values from -18 to 18, as said below
- gate_input: bfloat16 [16384, 8192], P('ctx', 'tp'), may hold values from -6 to 6
- grad_output: bfloat16 [16384, 8192], P('ctx', 'tp'), may hold values from -6 to 6
- norm_gain: float32 [8192], P('tp'), may hold values from 0.1 to 1.9
- segment_ids: int32 [16384], P('ctx'), may hold values from 0 to 5, never falling along the last dimension, each value on 1 to 8192 neighbouring positions
Outputs:
- layer_out: bfloat16 [16384, 8192], P('ctx', 'tp')
- grad_query: bfloat16 [16384, 8192], P('ctx', 'tp')
- grad_keys: bfloat16 [16384, 8192], P('ctx', 'tp')
- grad_values: bfloat16 [16384, 8192], P('ctx', 'tp')
- grad_gate: bfloat16 [16384, 8192], P('ctx', 'tp')
- grad_gain: float32 [8192], P('tp')
The draws below stay inside these ranges and needn't reach their ends.
Inputs may be any that keep to these rules, and one draw needn't show every extreme that they name: `query`: real values. Real values. `segment_ids`: segment ids never fall along the window; each of the 6 documents holds 1 to 8192 tokens, one exactly 8192.
All inputs are finite; a program needn't handle non-finite values.
Results may differ from the reference program's by a relative error of at most 0.013.
Values may be sent and summed in bfloat16 or wider, within the bound.
No kernel may reach another device: no remote copies, remote signals or barrier semaphores. Data moves between devices by JAX's collectives and lax.ppermute only.
A program may use at most 192 MiB of HBM per device.

```python
import math
import jax
import jax.numpy as jnp
import numpy as np
from jax import lax

HEADS = 64
HD = 128
TOK_DEV = 512
SEGS = 6
TOKENS = 16384
ATT = 8192
N_CTX = 32


def draw_query(key, part):
    key = jax.random.fold_in(key, 11)
    base_key, row_key = jax.random.split(key, 2)
    row_scale = jnp.exp(jax.random.uniform(row_key, (TOKENS, 1), jnp.float32, math.log(0.3), math.log(3.0)))
    base = jax.random.normal(base_key, (TOKENS, ATT), jnp.float32)
    return (jnp.clip(base, -4.0, 4.0) * row_scale).astype(jnp.bfloat16)


def draw_values(key, part):
    key = jax.random.fold_in(key, 23)
    base_key, column_key = jax.random.split(key, 2)
    head_index = (jnp.arange(ATT) // HD).astype(jnp.float32)
    ramp = 0.6 * jnp.power(3.0, head_index / (HEADS - 1))
    column_scale = ramp * jnp.exp(jax.random.uniform(column_key, (ATT,), jnp.float32, math.log(0.4), math.log(2.5)))
    base = jax.random.normal(base_key, (TOKENS, ATT), jnp.float32)
    return (jnp.clip(base, -4.0, 4.0) * column_scale[None, :]).astype(jnp.bfloat16)


def level_of(rng, extent, cuts, least, top_value):
    level = 1.0
    for dim, shards_of in cuts:
        steps = jax.random.uniform(jax.random.fold_in(jax.random.fold_in(rng, 6), dim), (shards_of,), jnp.float32, least / len(cuts), top_value / len(cuts))
        level = level * jnp.repeat(jnp.exp(steps), extent[dim] // shards_of).reshape((-1,) + (1,) * (len(extent) - 1 - dim))
    return level


def length_profile(amount, total, most, skew):
    loads = [(1 << 20) // math.isqrt(grade ** skew) + 1 for grade in range(2, amount + 1)]
    surplus, counts = total - most - (amount - 1), [1] * (amount - 1)
    while surplus > 0:
        free = [i for i in range(amount - 1) if counts[i] < most]
        mass, left = sum([loads[i] for i in free]), surplus
        for i in free:
            addition = min(most - counts[i], max(1, left * loads[i] // mass), surplus)
            counts[i] = counts[i] + addition
            surplus = surplus - addition
    return np.array([most] + counts)


def uneven(own_key, count, total, bound, lean):
    if count == 2:
        one = jax.random.randint(own_key, (), max(1, total - bound), min(bound, total - 1) + 1)
        return jnp.stack([one, total - one])
    tallies = jnp.asarray(length_profile(count, total, bound, lean), jnp.int32)
    pairs = (count - 1) // 2
    giver, sink = tallies[1:1 + 2 * pairs:2], tallies[2:2 + 2 * pairs:2]
    margin = jnp.minimum(giver - 1, bound - sink)
    moved = jax.random.randint(jax.random.fold_in(own_key, 1), (pairs,), 0, 1 << 20) % (margin + 1)
    tallies = tallies.at[1:1 + 2 * pairs:2].set(giver - moved).at[2:2 + 2 * pairs:2].set(sink + moved)
    return tallies[jax.random.permutation(jax.random.fold_in(own_key, 2), count)]


def normal_values(own_key, dims, deviation, reach, cuts=(), dtype=jnp.bfloat16):
    factor_of = level_of(own_key, dims, cuts, -0.22, 0.18) if cuts else 1.0
    values = jax.random.normal(own_key, dims, jnp.float32) * deviation * factor_of
    return jnp.minimum(jnp.maximum(values, -reach), reach).astype(dtype)


def setup_inputs(seed: int = 0) -> dict:
    streams_of = jax.random.split(jax.random.key(seed), 8)
    query = draw_query(jax.random.fold_in(streams_of[7], 71), 0)
    keys = normal_values(streams_of[1], (TOKENS, ATT), 1.0, 5.0, ((0, 32), (1, 4)))
    values = draw_values(jax.random.fold_in(streams_of[7], 71), 0)
    gate_input = normal_values(streams_of[3], (TOKENS, ATT), 1.5, 6.0, ((0, 32), (1, 4)))
    grad_output = normal_values(streams_of[4], (TOKENS, ATT), 1.0, 6.0, ((0, 32), (1, 4)))
    norm_gain = jnp.clip(1.0 + 0.18 * jax.random.normal(streams_of[5], (ATT,), jnp.float32), 0.1, 1.9)
    segment_ids = jnp.searchsorted(jnp.cumsum(uneven(streams_of[6], SEGS, TOKENS, TOKENS // 2, 0)), jnp.arange(TOKENS), side="right").astype(jnp.int32)
    return {"query": query, "keys": keys, "values": values, "gate_input": gate_input, "grad_output": grad_output, "norm_gain": norm_gain, "segment_ids": segment_ids}


EPSILON = 1e-06

def doc_mask(segment_ids):
    position = jnp.arange(segment_ids.shape[0])
    causal = position[:, None] >= position[None, :]
    return causal & (segment_ids[:, None] == segment_ids[None, :])

def masked_scores(left_rows, right_rows, allowed):
    scores = jnp.einsum('thd,shd->hts', left_rows.astype(jnp.float32), right_rows.astype(jnp.float32))
    rounded = jnp.where(allowed[None], scores, 0.0).astype(jnp.bfloat16)
    return lax.optimization_barrier(rounded).astype(jnp.float32)

def forward_block(running, block_data):
    state, high_seg = running
    query_blk, keys_blk, values_blk, segment_blk = block_data
    allowed = doc_mask(segment_blk)
    weights = masked_scores(query_blk, keys_blk, allowed)
    intra = jnp.einsum('hts,shd->thd', weights, values_blk.astype(jnp.float32))
    state_bf = state.astype(jnp.bfloat16)
    state_back = lax.optimization_barrier(state_bf).astype(jnp.float32)
    cross = jnp.einsum('thd,hde->the', query_blk.astype(jnp.float32), state_back)
    attn = intra + jnp.where((segment_blk == high_seg)[:, None, None], cross, 0.0)
    last_seg = segment_blk[-1]
    tail_keys = jnp.where((segment_blk == last_seg)[:, None, None], keys_blk, jnp.zeros_like(keys_blk))
    local_state = jnp.einsum('thd,the->hde', tail_keys.astype(jnp.float32), values_blk.astype(jnp.float32))
    joined = (segment_blk[0] == last_seg) & (segment_blk[0] == high_seg)
    new_state = local_state + jnp.where(joined, state, 0.0)
    return ((new_state, last_seg), (attn, state_back, high_seg))

def backward_block(running, block_data):
    later, low_seg = running
    query_blk, keys_blk, values_blk, grad_blk, segment_blk, state_back, high_seg = block_data
    allowed = doc_mask(segment_blk)
    grad_weights = masked_scores(grad_blk, values_blk, allowed)
    weights = masked_scores(query_blk, keys_blk, allowed)
    query_f = query_blk.astype(jnp.float32)
    keys_f = keys_blk.astype(jnp.float32)
    values_f = values_blk.astype(jnp.float32)
    grad_f = grad_blk.astype(jnp.float32)
    from_before = (segment_blk == high_seg)[:, None, None]
    grad_query = jnp.einsum('hts,shd->thd', grad_weights, keys_f)
    grad_query = grad_query + jnp.where(from_before, jnp.einsum('the,hde->thd', grad_f, state_back), 0.0)
    later_back = lax.optimization_barrier(later.astype(jnp.bfloat16)).astype(jnp.float32)
    to_after = (segment_blk == low_seg)[:, None, None]
    grad_keys = jnp.einsum('hts,thd->shd', grad_weights, query_f)
    grad_keys = grad_keys + jnp.where(to_after, jnp.einsum('she,hde->shd', values_f, later_back), 0.0)
    grad_values = jnp.einsum('hts,the->she', weights, grad_f)
    grad_values = grad_values + jnp.where(to_after, jnp.einsum('shd,hde->she', keys_f, later_back), 0.0)
    first_seg = segment_blk[0]
    head_query = jnp.where((segment_blk == first_seg)[:, None, None], query_f, 0.0)
    local_later = jnp.einsum('thd,the->hde', head_query, grad_f)
    joined = (first_seg == segment_blk[-1]) & (segment_blk[-1] == low_seg)
    new_later = local_later + jnp.where(joined, later, 0.0)
    outputs = (grad_query.astype(jnp.bfloat16), grad_keys.astype(jnp.bfloat16), grad_values.astype(jnp.bfloat16))
    return ((new_later, first_seg), outputs)

def reference(query, keys, values, gate_input, grad_output, norm_gain, segment_ids):

    def blocks(array):
        return array.reshape(N_CTX, TOK_DEV, HEADS, HD)
    segment_blocks = segment_ids.reshape(N_CTX, TOK_DEV)
    start_state = jnp.zeros((HEADS, HD, HD), jnp.float32)
    start_seg = jnp.array(-1, jnp.int32)
    carry_out, stacked = lax.scan(forward_block, (start_state, start_seg), (blocks(query), blocks(keys), blocks(values), segment_blocks))
    attn_blocks, state_blocks, high_blocks = stacked
    attn = attn_blocks.reshape(TOKENS, ATT)
    rinv = lax.rsqrt(lax.optimization_barrier(jnp.mean(attn * attn, axis=1)) + EPSILON)
    normed = attn * rinv[:, None]
    sig = jax.nn.sigmoid(gate_input.astype(jnp.float32))
    layer_out = (normed * norm_gain[None, :] * sig).astype(jnp.bfloat16)
    grad_y = grad_output.astype(jnp.float32)
    grad_gain = lax.optimization_barrier(jnp.sum(grad_y * normed * sig, axis=0))
    grad_gate = (grad_y * normed * norm_gain[None, :] * sig * (1.0 - sig)).astype(jnp.bfloat16)
    dnorm = grad_y * norm_gain[None, :] * sig
    inner = lax.optimization_barrier(jnp.mean(dnorm * normed, axis=1))
    grad_attn = (rinv[:, None] * (dnorm - normed * inner[:, None])).astype(jnp.bfloat16)
    carry_back, grads = lax.scan(backward_block, (start_state, start_seg), (blocks(query), blocks(keys), blocks(values), blocks(grad_attn), segment_blocks, state_blocks, high_blocks), reverse=True)
    grad_query, grad_keys, grad_values = grads
    return (layer_out, grad_query.reshape(TOKENS, ATT), grad_keys.reshape(TOKENS, ATT), grad_values.reshape(TOKENS, ATT), grad_gate, grad_gain)
```

```python
import functools

import jax
import jax.numpy as jnp
from jax import lax
from jax.experimental import pallas as pl
from jax.experimental.pallas import tpu as pltpu
from jax.sharding import PartitionSpec as P

HD = 128
ATT = 8192
EPSILON = 1e-06
TOK = 512
HALF = 256
PAIR = 2 * HD
PAIRS = 8
STATE_ROWS = 8 * HD
QUARTER = 2 * HD
TILE = 16
F32 = jnp.float32
BF16 = jnp.bfloat16
VMEM_LIMIT = 48 * 1024 * 1024


def dot(a, b, da, db):
    return lax.dot_general(a, b, (((da,), (db,)), ((), ())), preferred_element_type=F32)


def params():
    return pltpu.CompilerParams(vmem_limit_bytes=VMEM_LIMIT)


def estimate(flops, nbytes):
    return pl.CostEstimate(flops=int(flops), bytes_accessed=int(nbytes), transcendentals=0)


def column_block(first_pair):
    def index(i, ids):
        return (0, lax.rem(i + first_pair + 4 * ids[0], PAIRS))

    return pl.BlockSpec((TOK, PAIR), index)


def gain_block(first_pair):
    def index(i, ids):
        return (0, lax.rem(i + first_pair + 4 * ids[0], PAIRS))

    return pl.BlockSpec((1, PAIR), index)


def whole(shape):
    return pl.BlockSpec(shape, lambda i, ids: (0,) * len(shape))


def state_block(offset):
    return pl.BlockSpec((PAIR, HD), lambda i, ids: (i + offset, 0))


ANY = pl.BlockSpec(memory_space=pl.ANY)


def full(shape):
    return jax.ShapeDtypeStruct(shape, BF16)


def full32(shape):
    return jax.ShapeDtypeStruct(shape, F32)


def ends(seg_ref):
    seg = seg_ref[...].astype(F32)
    return seg, seg[:, 0:1], seg[:, TOK - 1 : TOK]


def count(flags):
    return jnp.sum(flags.astype(F32), axis=1, keepdims=True)


def token_rows(width=HD):
    return lax.broadcasted_iota(jnp.int32, (TOK, width), 0).astype(F32)


def head_mask(seg_ref):
    seg, first, _ = ends(seg_ref)
    return token_rows() < count(seg == first)


def tail_mask(seg_ref):
    seg, _, last = ends(seg_ref)
    return token_rows() >= (TOK - count(seg == last))


def info_tile(low, high):
    row = lax.broadcasted_iota(jnp.int32, (TILE, HD), 0)
    return jnp.where(
        row < 8, jnp.broadcast_to(low, (TILE, HD)), jnp.broadcast_to(high, (TILE, HD))
    ).astype(BF16)


def split_tile(x):
    high = x.astype(BF16).astype(F32)
    return jnp.concatenate([high, x - high], axis=0).astype(BF16)


def joined_tile(tile):
    t = tile.astype(F32)
    return t[0:8] + t[8:16]


def state_kernel(ids, seg_ref, k_ref, v_ref, out_ref, mask):
    i = pl.program_id(0)

    @pl.when(i == 0)
    def _():
        _, first, last = ends(seg_ref)
        mask[...] = tail_mask(seg_ref).astype(F32).astype(BF16)
        out_ref[STATE_ROWS : STATE_ROWS + TILE, :] = info_tile(first, last)

    for j in range(2):
        cols = slice(j * HD, (j + 1) * HD)
        part = dot(k_ref[:, cols] * mask[...], v_ref[:, cols], 0, 0)
        out_ref[pl.ds((2 * i + j) * HD, HD), :] = part.astype(BF16)


def local_state(ids, seg, k, v, first_pair):
    return pl.pallas_call(
        state_kernel,
        grid_spec=pltpu.PrefetchScalarGridSpec(
            num_scalar_prefetch=1,
            grid=(4,),
            in_specs=[whole((1, TOK)), column_block(first_pair), column_block(first_pair)],
            out_specs=whole((STATE_ROWS + TILE, HD)),
            scratch_shapes=[pltpu.VMEM((TOK, HD), BF16)],
        ),
        out_shape=full((STATE_ROWS + TILE, HD)),
        compiler_params=params(),
        cost_estimate=estimate(2.7e8, 2.3e6),
        name="local_state",
    )(ids, seg, k, v)


def pair_masks(seg_ref, m00, m1):
    seg, _, _ = ends(seg_ref)
    col = jnp.transpose(jnp.broadcast_to(seg, (8, TOK)))[:, 0:1]
    for start, ref in ((0, m00), (HALF, m1)):
        width = ref.shape[1]
        same = col[start : start + HALF] == seg[:, 0:width]
        t = lax.broadcasted_iota(jnp.int32, (HALF, width), 0) + start
        s = lax.broadcasted_iota(jnp.int32, (HALF, width), 1)
        ref[...] = jnp.where(same & (s <= t), 1.0, 0.0).astype(BF16)


def masked_pair(left, right, m00, m1):
    w0 = dot(left[0:HALF], right[0:HALF], 1, 1).astype(BF16) * m00[...]
    w1 = dot(left[HALF:TOK], right, 1, 1).astype(BF16) * m1[...]
    return w0, w1


def intra_kernel(ids, seg_ref, q_ref, k_ref, v_ref, *rest):
    out_ref, m00, m1 = rest[-3:]

    @pl.when(pl.program_id(0) == 0)
    def _():
        pair_masks(seg_ref, m00, m1)

    for j in range(2):
        cols = slice(j * HD, (j + 1) * HD)
        v = v_ref[:, cols]
        w0, w1 = masked_pair(q_ref[:, cols], k_ref[:, cols], m00, m1)
        out_ref[0:HALF, cols] = dot(w0, v[0:HALF], 1, 0)
        out_ref[HALF:TOK, cols] = dot(w1, v, 1, 0)


def intra(ids, seg, q, k, v, attn, first_pair, pairs):
    block = column_block(first_pair)
    more = () if attn is None else (attn,)
    return pl.pallas_call(
        intra_kernel,
        grid_spec=pltpu.PrefetchScalarGridSpec(
            num_scalar_prefetch=1,
            grid=(pairs,),
            in_specs=[whole((1, TOK)), block, block, block] + [ANY] * len(more),
            out_specs=block,
            scratch_shapes=[pltpu.VMEM((HALF, HALF), BF16), pltpu.VMEM((HALF, TOK), BF16)],
        ),
        out_shape=full32((TOK, 2048)),
        input_output_aliases={5: 0} if more else {},
        compiler_params=params(),
        cost_estimate=estimate(pairs * 4e8, pairs * 1.3e6),
        name="intra",
    )(ids, seg, q, k, v, *more)


def cross_kernel(ids, seg_ref, attn_in, q_ref, s_ref, go_ref, gi_ref, gain_ref, *rest):
    prev_ref = rest[0] if len(rest) == 5 else None
    attn_ref, sums_ref, squares, inners = rest[-4:]
    i = pl.program_id(0)

    @pl.when(i == 0)
    def _():
        squares[...] = jnp.zeros_like(squares)
        inners[...] = jnp.zeros_like(inners)

    allowed = head_mask(seg_ref)
    for j in range(2):
        cols = slice(j * HD, (j + 1) * HD)
        cross = dot(q_ref[:, cols], s_ref[j * HD : (j + 1) * HD, :], 1, 0)
        attn = attn_in[:, cols] + jnp.where(allowed, cross, 0.0)
        attn_ref[:, cols] = attn
        sig = 0.5 * jnp.tanh(0.5 * gi_ref[:, cols].astype(F32)) + 0.5
        dnorm = go_ref[:, cols].astype(F32) * sig * gain_ref[:, cols]
        squares[...] += attn * attn
        inners[...] += dnorm * attn

    @pl.when(i == pl.num_programs(0) - 1)
    def _():
        ones = jnp.ones((8, HD), F32)
        high = lax.Precision.HIGHEST
        dims = (((1,), (1,)), ((), ()))
        ss = lax.dot_general(ones, squares[...], dims, precision=high, preferred_element_type=F32)
        dd = lax.dot_general(ones, inners[...], dims, precision=high, preferred_element_type=F32)
        total = jnp.where(lax.broadcasted_iota(jnp.int32, (8, TOK), 0) < 4, ss, dd)
        if prev_ref is not None:
            total = total + prev_ref[...]
        sums_ref[...] = total


def cross(ids, seg, attn, q, state, go, gi, gain, prev, first_pair):
    block = column_block(first_pair)
    more = () if prev is None else (prev,)
    return pl.pallas_call(
        cross_kernel,
        grid_spec=pltpu.PrefetchScalarGridSpec(
            num_scalar_prefetch=1,
            grid=(4,),
            in_specs=[whole((1, TOK)), block, block, state_block(0), block, block]
            + [gain_block(first_pair)]
            + [whole((8, TOK))] * len(more),
            out_specs=[block, whole((8, TOK))],
            scratch_shapes=[pltpu.VMEM((TOK, HD), F32), pltpu.VMEM((TOK, HD), F32)],
        ),
        out_shape=[full32((TOK, 2048)), full32((8, TOK))],
        input_output_aliases={2: 0},
        compiler_params=params(),
        cost_estimate=estimate(2e8, 7e6),
        name="cross",
    )(ids, seg, attn, q, state, go, gi, gain, *more)


def scales(sums, rinv_ref, back_ref):
    own, one, two, three = [r[...] for r in sums]
    total = (own + one) + (two + three)
    rinv = lax.rsqrt(total * (1.0 / ATT) + EPSILON)
    rinv = rinv[0:1]
    back = rinv * rinv * rinv * total[4:5] * (1.0 / ATT)
    row = lax.broadcasted_iota(jnp.int32, (8, TOK), 0)
    both = jnp.where(
        row < 4, jnp.broadcast_to(rinv, (8, TOK)), jnp.broadcast_to(back, (8, TOK))
    )
    cols = jnp.transpose(both)
    rinv_ref[...] = jnp.broadcast_to(cols[:, 0:1], (TOK, HD))
    back_ref[...] = jnp.broadcast_to(cols[:, 4:5], (TOK, HD))


def grad_kernel(ids, seg_ref, s0, s1, s2, s3, attn_ref, q_ref, go_ref, gi_ref, gain_ref, *rest):
    g_ref, out_ref, mask, rinv, back, gains = rest[-6:]
    i = pl.program_id(0)

    @pl.when(i == 0)
    def _():
        _, first, last = ends(seg_ref)
        mask[...] = head_mask(seg_ref).astype(F32).astype(BF16)
        out_ref[STATE_ROWS : STATE_ROWS + TILE, :] = info_tile(8.0 - last, 8.0 - first)
        scales((s0, s1, s2, s3), rinv, back)

    for j in range(2):
        cols = slice(j * HD, (j + 1) * HD)
        attn = attn_ref[:, cols]
        sig = 0.5 * jnp.tanh(0.5 * gi_ref[:, cols].astype(F32)) + 0.5
        gated = go_ref[:, cols].astype(F32) * sig * rinv[...]
        gains[pl.ds(2 * i + j, 1), :] = jnp.sum(gated * attn, axis=0, keepdims=True)
        g = (gated * gain_ref[:, cols] - attn * back[...]).astype(BF16)
        g_ref[:, cols] = g
        part = dot(q_ref[:, cols] * mask[...], g, 0, 0)
        out_ref[pl.ds((2 * i + j) * HD, HD), :] = part.astype(BF16)

    @pl.when(i == pl.num_programs(0) - 1)
    def _():
        out_ref[STATE_ROWS + TILE : STATE_ROWS + 2 * TILE, :] = split_tile(gains[...])


def grad_attn(ids, seg, sums, attn, q, go, gi, gain, g, first_pair):
    block = column_block(first_pair)
    more = () if g is None else (g,)
    rows = STATE_ROWS + 2 * TILE
    return pl.pallas_call(
        grad_kernel,
        grid_spec=pltpu.PrefetchScalarGridSpec(
            num_scalar_prefetch=1,
            grid=(4,),
            in_specs=[whole((1, TOK))]
            + [whole((8, TOK))] * 4
            + [block] * 4
            + [gain_block(first_pair)]
            + [ANY] * len(more),
            out_specs=[block, whole((rows, HD))],
            scratch_shapes=[
                pltpu.VMEM((TOK, HD), BF16),
                pltpu.VMEM((TOK, HD), F32),
                pltpu.VMEM((TOK, HD), F32),
                pltpu.VMEM((8, HD), F32),
            ],
        ),
        out_shape=[full((TOK, 2048)), full((rows, HD))],
        input_output_aliases={11: 0} if more else {},
        compiler_params=params(),
        cost_estimate=estimate(2.7e8, 6e6),
        name="grad_attn",
    )(ids, seg, *sums, attn, q, go, gi, gain, *more)


def local_grads_kernel(
    ids, seg_ref, s0, s1, s2, s3, q_ref, k_ref, v_ref, g_ref, go_ref, gi_ref, attn_ref, gain_ref,
    state_ref, *rest
):
    lo_ref, gg_ref, dq_ref, dk_ref, dv_ref, m00, m1, rinv, back = rest[-9:]

    @pl.when(pl.program_id(0) == 0)
    def _():
        pair_masks(seg_ref, m00, m1)
        scales((s0, s1, s2, s3), rinv, back)

    allowed = head_mask(seg_ref)
    for j in range(2):
        cols = slice(j * HD, (j + 1) * HD)
        q, k, v, g = q_ref[:, cols], k_ref[:, cols], v_ref[:, cols], g_ref[:, cols]
        w0, w1 = masked_pair(q, k, m00, m1)
        dw0, dw1 = masked_pair(g, v, m00, m1)
        hop = jnp.where(allowed, dot(g, state_ref[j * HD : (j + 1) * HD, :], 1, 1), 0.0)
        dq_ref[0:HALF, cols] = (dot(dw0, k[0:HALF], 1, 0) + hop[0:HALF]).astype(BF16)
        dq_ref[HALF:TOK, cols] = (dot(dw1, k, 1, 0) + hop[HALF:TOK]).astype(BF16)
        for ref, a0, a1, rows in ((dk_ref, dw0, dw1, q), (dv_ref, w0, w1, g)):
            late = dot(a1, rows[HALF:TOK], 0, 0)
            ref[0:HALF, cols] = late[0:HALF] + dot(a0, rows[0:HALF], 0, 0)
            ref[HALF:TOK, cols] = late[HALF:TOK]
        bend = 0.5 * jnp.tanh(0.5 * gi_ref[:, cols].astype(F32))
        gated = attn_ref[:, cols] * rinv[...] * gain_ref[:, cols] * (0.5 + bend)
        lo_ref[:, cols] = gated.astype(BF16)
        gg_ref[:, cols] = (go_ref[:, cols].astype(F32) * gated * (0.5 - bend)).astype(BF16)


def local_grads(ids, seg, sums, q, k, v, g, go, gi, attn, gain, state, outs, first_pair, pairs):
    block = column_block(first_pair)
    more = () if outs is None else tuple(outs)
    return pl.pallas_call(
        local_grads_kernel,
        grid_spec=pltpu.PrefetchScalarGridSpec(
            num_scalar_prefetch=1,
            grid=(pairs,),
            in_specs=[whole((1, TOK))]
            + [whole((8, TOK))] * 4
            + [block] * 7
            + [gain_block(first_pair), state_block(first_pair % 4)]
            + [ANY] * len(more),
            out_specs=[block] * 5,
            scratch_shapes=[
                pltpu.VMEM((HALF, HALF), BF16),
                pltpu.VMEM((HALF, TOK), BF16),
                pltpu.VMEM((TOK, HD), F32),
                pltpu.VMEM((TOK, HD), F32),
            ],
        ),
        out_shape=[full((TOK, 2048))] * 3 + [full32((TOK, 2048))] * 2,
        input_output_aliases={15 + n: n for n in range(5)} if more else {},
        compiler_params=params(),
        cost_estimate=estimate(pairs * 1.1e9, pairs * 3.9e6),
        name="local_grads",
    )(ids, seg, *sums, q, k, v, g, go, gi, attn, gain, state, *more)


def finish_kernel(ids, seg_ref, dk_in, dv_in, k_ref, v_ref, l_ref, *rest):
    dk_ref, dv_ref = rest[-2:]
    allowed = tail_mask(seg_ref)
    for j in range(2):
        cols = slice(j * HD, (j + 1) * HD)
        later = l_ref[j * HD : (j + 1) * HD, :]
        dk = dot(v_ref[:, cols], later, 1, 1)
        dv = dot(k_ref[:, cols], later, 1, 0)
        dk_ref[:, cols] = (dk_in[:, cols] + jnp.where(allowed, dk, 0.0)).astype(BF16)
        dv_ref[:, cols] = (dv_in[:, cols] + jnp.where(allowed, dv, 0.0)).astype(BF16)


def finish(ids, seg, dk, dv, k, v, later, outs, first_pair):
    block = column_block(first_pair)
    more = () if outs is None else tuple(outs)
    return pl.pallas_call(
        finish_kernel,
        grid_spec=pltpu.PrefetchScalarGridSpec(
            num_scalar_prefetch=1,
            grid=(4,),
            in_specs=[whole((1, TOK))] + [block] * 4 + [state_block(0)] + [ANY] * len(more),
            out_specs=[block] * 2,
        ),
        out_shape=[full((TOK, 2048))] * 2,
        input_output_aliases={7 + n: n for n in range(2)} if more else {},
        compiler_params=params(),
        cost_estimate=estimate(2.7e8, 8e6),
        name="finish",
    )(ids, seg, dk, dv, k, v, later, *more)


def place(ids, reverse):
    core, x, z = ids[0], ids[1], ids[2]
    return (1 - core, 3 - x, 3 - z) if reverse else (core, x, z)


def info_rows(ref, at):
    tile = ref[at : at + TILE, :].astype(F32)
    return tile[0:1], tile[8:9]


def flag(cond):
    return jnp.where(cond, 1.0, 0.0)


def sorted_cores(first_core, own, other):
    return jnp.where(first_core, own, other), jnp.where(first_core, other, own)


def chip_kernel(reverse, gain, ids, own_ref, other_ref, *outs):
    vcore, _, _ = place(ids, reverse)
    first_core = vcore == 0
    low_own, high_own = info_rows(own_ref, STATE_ROWS)
    low_other, high_other = info_rows(other_ref, STATE_ROWS)
    low_a, _ = sorted_cores(first_core, low_own, low_other)
    high_a, high_b = sorted_cores(first_core, high_own, high_other)
    join = flag(high_a == high_b)
    own_weight = jnp.where(first_core, join, 1.0)
    other_weight = jnp.where(first_core, 1.0, join)
    for m, out in enumerate(outs):
        rows = pl.ds(pl.multiple_of((ids[1] ^ m) * QUARTER, QUARTER), QUARTER)
        total = own_ref[rows, :].astype(F32) * own_weight
        total = total + other_ref[rows, :].astype(F32) * other_weight
        out[0:QUARTER, :] = total.astype(BF16)
        out[QUARTER : QUARTER + TILE, :] = info_tile(low_a, high_b)
        if gain:
            at = slice(STATE_ROWS + TILE, STATE_ROWS + 2 * TILE)
            both = joined_tile(own_ref[at, :]) + joined_tile(other_ref[at, :])
            out[QUARTER + TILE : QUARTER + 2 * TILE, :] = split_tile(both)


def row_kernel(gain, ids, p0, p1, p2, p3, out):
    parts = (p0, p1, p2, p3)
    info = [info_rows(p, QUARTER) for p in parts]
    low = jnp.minimum(jnp.minimum(info[0][0], info[1][0]), jnp.minimum(info[2][0], info[3][0]))
    high = jnp.maximum(jnp.maximum(info[0][1], info[1][1]), jnp.maximum(info[2][1], info[3][1]))
    total = None
    for p, (_, own_high) in zip(parts, info):
        term = p[0:QUARTER, :].astype(F32) * flag(own_high == high)
        total = term if total is None else total + term
    out[0:QUARTER, :] = total.astype(BF16)
    out[QUARTER : QUARTER + TILE, :] = info_tile(low, high)
    if gain:
        g = [joined_tile(p[QUARTER + TILE : QUARTER + 2 * TILE, :]) for p in parts]
        out[QUARTER + TILE : QUARTER + 2 * TILE, :] = split_tile((g[0] + g[1]) + (g[2] + g[3]))


def entry_kernel(reverse, gain, ids, p0, p1, p2, p3, t0, t1, t2, t3, *outs):
    _, vx, vz = place(ids, reverse)
    parts = (p0, p1, p2, p3)
    rows = (t0, t1, t2, t3)
    info = [info_rows(p, QUARTER) for p in parts]
    row_high = [info_rows(t, QUARTER)[1] for t in rows]
    for m in range(4):
        low = info[m][0]
        total = jnp.zeros((QUARTER, HD), F32)
        for n in range(4):
            if n != m:
                before = flag((vx ^ n) < (vx ^ m))
                total = total + parts[n][0:QUARTER, :].astype(F32) * (flag(info[n][1] == low) * before)
        for n in range(1, 4):
            before = flag((vz ^ n) < vz)
            total = total + rows[n][0:QUARTER, :].astype(F32) * (flag(row_high[n] == low) * before)
        outs[m][...] = total.astype(BF16)
    if gain:
        g = [joined_tile(t[QUARTER + TILE : QUARTER + 2 * TILE, :]) for t in rows]
        outs[4][...] = split_tile((g[0] + g[1]) + (g[2] + g[3]))


def device_kernel(reverse, gain, ids, own_ref, other_ref, e0, e1, e2, e3, *rest):
    keep, send = rest[-2:]
    vcore, _, _ = place(ids, reverse)
    first_core = vcore == 0
    low_own, high_own = info_rows(own_ref, STATE_ROWS)
    low_other, high_other = info_rows(other_ref, STATE_ROWS)
    low_a, low_b = sorted_cores(first_core, low_own, low_other)
    high_a, _ = sorted_cores(first_core, high_own, high_other)
    from_a = flag(high_a == low_b)
    from_chip = flag(low_a == low_b)
    for m, ref in enumerate((e0, e1, e2, e3)):
        rows = pl.ds(pl.multiple_of((ids[1] ^ m) * QUARTER, QUARTER), QUARTER)
        entry = ref[...].astype(F32)
        a = jnp.where(first_core, own_ref[rows, :].astype(F32), other_ref[rows, :].astype(F32))
        second = a * from_a + entry * from_chip
        keep[rows, :] = jnp.where(first_core, entry, second).astype(BF16)
        send[rows, :] = jnp.where(first_core, second, entry).astype(BF16)
    if gain:
        send[STATE_ROWS : STATE_ROWS + TILE, :] = rest[0][...]


def small(kernel, out_rows, nbytes, name, ids, *args):
    block = pl.BlockSpec(memory_space=pltpu.VMEM)
    return pl.pallas_call(
        kernel,
        in_specs=[pl.BlockSpec(memory_space=pltpu.SMEM)] + [block] * len(args),
        out_specs=[block] * len(out_rows),
        out_shape=[full((r, HD)) for r in out_rows],
        compiler_params=params(),
        cost_estimate=estimate(1e6, nbytes),
        name=name,
    )(ids, *args)


def swap(x, axis, size, bits):
    return lax.ppermute(x, axis, [(i, i ^ bits) for i in range(size)])


def chip_swap(x):
    return swap(x, "ctx", 32, 1)


def row_swap(x, m):
    return swap(x, "ctx", 32, m << 1)


def plane_swap(x, m):
    return swap(x, "ctx", 32, m << 3)


def scan(ids, own, other, reverse, gain):
    extra = TILE if gain else 0
    rows = QUARTER + TILE + extra
    parts = small(
        functools.partial(chip_kernel, reverse, gain), [rows] * 4, 1.1e6, "chip_sum", ids, own, other
    )
    parts = [parts[0]] + [row_swap(parts[m], m) for m in range(1, 4)]
    total = small(functools.partial(row_kernel, gain), [rows], 3e5, "row_sum", ids, *parts)[0]
    totals = [total] + [plane_swap(total, m) for m in range(1, 4)]
    entries = small(
        functools.partial(entry_kernel, reverse, gain),
        [QUARTER] * 4 + ([TILE] if gain else []),
        8e5,
        "entry",
        ids,
        *parts,
        *totals,
    )
    tail = entries[4:]
    entries = [entries[0]] + [row_swap(entries[m], m) for m in range(1, 4)]
    keep, send = small(
        functools.partial(device_kernel, reverse, gain),
        [STATE_ROWS, STATE_ROWS + extra],
        1.3e6,
        "device_entry",
        ids,
        own,
        other,
        *entries,
        *tail,
    )
    return keep, chip_swap(send), tail


def on_device(query, keys, values, gate_input, grad_output, norm_gain, segment_ids):
    where = lax.axis_index("ctx")
    core = where & 1
    ids = jnp.stack([core, (where >> 1) & 3, where >> 3]).astype(jnp.int32)
    seg = segment_ids.reshape(1, TOK)
    gain = norm_gain.reshape(1, -1)

    sent = local_state(ids, seg, keys, values, 4)
    other = chip_swap(sent)
    own = local_state(ids, seg, keys, values, 0)
    attn = intra(ids, seg, query, keys, values, None, 0, 4)
    attn = intra(ids, seg, query, keys, values, attn, 4, 4)
    keep, received, _ = scan(ids, own, other, False, False)
    attn, sums = cross(
        ids, seg, attn, query, keep, grad_output, gate_input, gain, None, 0
    )
    attn, sums = cross(
        ids, seg, attn, query, received, grad_output, gate_input, gain, sums, 4
    )
    sums = [sums] + [swap(sums, "tp", 4, m) for m in range(1, 4)]

    g, sent = grad_attn(ids, seg, sums, attn, query, grad_output, gate_input, gain, None, 4)
    other = chip_swap(sent)
    g, own = grad_attn(ids, seg, sums, attn, query, grad_output, gate_input, gain, g, 0)
    outs = None
    for first_pair, state in ((0, keep), (2, keep), (4, received), (6, received)):
        outs = local_grads(
            ids, seg, sums, query, keys, values, g, grad_output, gate_input, attn, gain, state,
            outs, first_pair, 2,
        )
    layer_out, grad_gate, grad_query, grad_keys, grad_values = outs
    later_keep, later_received, tail = scan(ids, own, other, True, True)
    done = finish(ids, seg, grad_keys, grad_values, keys, values, later_keep, None, 0)
    grad_keys, grad_values = finish(
        ids, seg, grad_keys, grad_values, keys, values, later_received, done, 4
    )
    gain_keep = joined_tile(tail[0])
    gain_other = joined_tile(later_received[STATE_ROWS : STATE_ROWS + TILE])
    grad_gain = jnp.where(
        core == 0,
        jnp.concatenate([gain_keep, gain_other]),
        jnp.concatenate([gain_other, gain_keep]),
    ).reshape(-1)
    return layer_out, grad_query, grad_keys, grad_values, grad_gate, grad_gain


def solution(mesh):
    in_specs = (P("ctx", "tp"),) * 5 + (P("tp"), P("ctx"))
    out_specs = (P("ctx", "tp"),) * 5 + (P("tp"),)
    return jax.shard_map(
        on_device, mesh=mesh, in_specs=in_specs, out_specs=out_specs, check_vma=False
    )
```

```python
import functools

import jax
import jax.numpy as jnp
from jax import lax
from jax.experimental import pallas as pl
from jax.experimental.pallas import tpu as pltpu
from jax.sharding import PartitionSpec as P

HD = 128
ATT = 8192
EPSILON = 1e-06
TOK = 512
BLOCK = 256
HEADS = 8
WIDE = HEADS * HD
GROUP = 4
GROUPS = HEADS // GROUP
SPAN = GROUP * HD
STATE_ROWS = HEADS * HD
QUARTER = 2 * HD
TILE = 16
F32 = jnp.float32
BF16 = jnp.bfloat16
VMEM_LIMIT = 16 * 1024 * 1024
VM = pl.BlockSpec(memory_space=pltpu.VMEM)
SM = pl.BlockSpec(memory_space=pltpu.SMEM)
ANY = pl.BlockSpec(memory_space=pl.ANY)


def dot(a, b, da, db):
    return lax.dot_general(a, b, (((da,), (db,)), ((), ())), preferred_element_type=F32)


def vmem(shape, dtype):
    return pltpu.VMEM(shape, dtype)


def half_shape(dtype):
    return vmem((TOK, WIDE), dtype)


def far(dtype=BF16):
    return jax.ShapeDtypeStruct((TOK, 2 * WIDE), dtype)


def call(kernel, name, flops, near, outs, distant=(), scratch=(), aliases=None):
    near = [pltpu.with_memory_space_constraint(a, pltpu.VMEM) for a in near]
    distant = [pltpu.with_memory_space_constraint(a, pltpu.HBM) for a in distant]
    out_specs = [ANY if isinstance(o, jax.ShapeDtypeStruct) else VM for o in outs]

    def placed(*refs):
        where = lax.axis_index("ctx")
        kernel((where & 1, (where >> 1) & 3, where >> 3), *refs)

    return pl.pallas_call(
        placed,
        in_specs=[VM] * len(near) + [ANY] * len(distant),
        out_specs=out_specs,
        out_shape=list(outs),
        scratch_shapes=list(scratch),
        input_output_aliases=aliases or {},
        compiler_params=pltpu.CompilerParams(vmem_limit_bytes=VMEM_LIMIT),
        cost_estimate=pl.CostEstimate(
            flops=int(flops), bytes_accessed=int(flops / 300), transcendentals=0
        ),
        name=name,
    )(*near, *distant)


def base_column(ids, flip):
    return pl.multiple_of((ids[0] ^ flip) * WIDE, WIDE)


def each_group(body):
    def step(g, carry):
        body(g)
        return carry

    lax.fori_loop(0, GROUPS, step, 0)


def head_columns(g, j):
    return pl.ds(pl.multiple_of(g * SPAN + j * HD, HD), HD)


def head_rows(g, j, rows=HD):
    return pl.ds(pl.multiple_of((g * GROUP + j) * rows, rows), rows)


def group_columns(g):
    return pl.ds(pl.multiple_of(g * SPAN, SPAN), SPAN)


def far_columns(base, g):
    return pl.ds(pl.multiple_of(base + g * SPAN, SPAN), SPAN)


def load(source, base, g, target, sem):
    return pltpu.make_async_copy(
        source.at[:, far_columns(base, g)], target.at[:, group_columns(g)], sem
    )


def store(source, base, g, target, sem):
    return pltpu.make_async_copy(
        source.at[:, group_columns(g)], target.at[:, far_columns(base, g)], sem
    )


def load_all(base, pairs, sems):
    for g in range(GROUPS):
        for n, (source, target) in enumerate(pairs):
            load(source, base, g, target, sems.at[n, g]).start()


def ends(seg_ref):
    seg = seg_ref[...].astype(F32)
    return seg, seg[:, 0:1], seg[:, TOK - 1 : TOK]


def count(flags):
    return jnp.sum(flags.astype(F32), axis=1, keepdims=True)


def info_tile(low, high):
    row = lax.broadcasted_iota(jnp.int32, (TILE, HD), 0)
    return jnp.where(
        row < 8, jnp.broadcast_to(low, (TILE, HD)), jnp.broadcast_to(high, (TILE, HD))
    ).astype(BF16)


def split_tile(x):
    high = x.astype(BF16).astype(F32)
    return jnp.concatenate([high, x - high], axis=0).astype(BF16)


def joined_tile(tile):
    t = tile.astype(F32)
    return t[0:8] + t[8:16]


def state_kernel(flip, ids, *refs):
    if flip:
        k_far, v_far, seg_far, k, v, out, seg, head, tail, sems, seg_sem, mask = refs
    else:
        seg, tail, k_far, v_far, k, v, out, sems, mask = refs
    base = base_column(ids, flip)
    load_all(base, ((k_far, k), (v_far, v)), sems)
    if flip:
        copy = pltpu.make_async_copy(seg_far, seg, seg_sem)
        copy.start()
        copy.wait()
        row, first, last = ends(seg)
        token = lax.broadcasted_iota(jnp.int32, (TOK, HD), 0).astype(F32)
        head[...] = jnp.where(token < count(row == first), 1.0, 0.0)
        tail[...] = jnp.where(token >= TOK - count(row == last), 1.0, 0.0)
    _, first, last = ends(seg)
    mask[...] = tail[...].astype(BF16)
    out[STATE_ROWS : STATE_ROWS + TILE, :] = info_tile(first, last)

    def body(g):
        load(k_far, base, g, k, sems.at[0, g]).wait()
        load(v_far, base, g, v, sems.at[1, g]).wait()
        for j in range(GROUP):
            c = head_columns(g, j)
            out[head_rows(g, j), :] = dot(k[:, c] * mask[...], v[:, c], 0, 0).astype(BF16)

    each_group(body)


def local_state(k, v, seg, seg_vmem=None, tail=None):
    flip = seg_vmem is None
    outs = [half_shape(BF16), half_shape(BF16), vmem((STATE_ROWS + TILE, HD), BF16)]
    scratch = [pltpu.SemaphoreType.DMA((2, GROUPS))]
    near, distant = [seg_vmem, tail], [k, v]
    if flip:
        outs += [vmem((1, TOK), jnp.int32), vmem((TOK, HD), F32), vmem((TOK, HD), F32)]
        scratch += [pltpu.SemaphoreType.DMA]
        near, distant = [], [k, v, seg]
    return call(
        functools.partial(state_kernel, int(flip)), "local_state", 1e9, near, outs, distant,
        scratch + [pltpu.VMEM((TOK, HD), BF16)],
    )


def fill_masks(seg_ref, m0, m1):
    seg, _, _ = ends(seg_ref)
    col = jnp.transpose(jnp.broadcast_to(seg, (8, TOK)))[:, 0:1]
    for start, ref in ((0, m0), (BLOCK, m1)):
        width = ref.shape[1]
        same = col[start : start + BLOCK] == seg[:, 0:width]
        t = lax.broadcasted_iota(jnp.int32, (BLOCK, width), 0) + start
        s = lax.broadcasted_iota(jnp.int32, (BLOCK, width), 1)
        ref[...] = jnp.where(same & (s <= t), 1.0, 0.0).astype(BF16)


def masked_pair(left, right, m0, m1):
    w0 = dot(left[0:BLOCK], right[0:BLOCK], 1, 1).astype(BF16) * m0[...]
    w1 = dot(left[BLOCK:TOK], right, 1, 1).astype(BF16) * m1[...]
    return w0, w1


def intra_kernel(flip, ids, *refs):
    if flip:
        k, v, m0, m1, _, q_far, q, attn, w0, w1, token, sems = refs
    else:
        k, v, seg, _, q_far, q, attn, w0, w1, token, m0, m1, sems = refs
    base = base_column(ids, flip)
    load_all(base, ((q_far, q),), sems)
    if not flip:
        fill_masks(seg, m0, m1)
    token[...] = jnp.zeros_like(token)

    def body(g):
        load(q_far, base, g, q, sems.at[0, g]).wait()
        for j in range(GROUP):
            c = head_columns(g, j)
            value = v[:, c]
            a0, a1 = masked_pair(q[:, c], k[:, c], m0, m1)
            w0[head_rows(g, j, BLOCK), :] = a0
            w1[head_rows(g, j, BLOCK), :] = a1
            attn[0:BLOCK, c] = dot(a0, value[0:BLOCK], 1, 0)
            attn[BLOCK:TOK, c] = dot(a1, value, 1, 0)

    each_group(body)


TOKEN = vmem((8, HD), F32)


def intra(k, v, q, after, seg=None, masks=None):
    outs = [
        half_shape(BF16),
        half_shape(F32),
        vmem((HEADS * BLOCK, BLOCK), BF16),
        vmem((HEADS * BLOCK, TOK), BF16),
        TOKEN,
    ]
    if masks is None:
        near = [k, v, seg, after]
        outs += [vmem((BLOCK, BLOCK), BF16), vmem((BLOCK, TOK), BF16)]
    else:
        near = [k, v, *masks, after]
    return call(
        functools.partial(intra_kernel, int(masks is not None)), "intra", 3e9, near, outs, [q],
        [pltpu.SemaphoreType.DMA((1, GROUPS))],
    )


def sigmoid_parts(gi):
    bend = 0.5 * jnp.tanh(0.5 * gi.astype(F32))
    return 0.5 + bend, 0.5 - bend


def prepare_kernel(flip, ids, q, head, _, go_far, gi_far, w, gi, qt, token, go, sems, mask):
    base = base_column(ids, flip)
    load_all(base, ((go_far, go), (gi_far, gi)), sems)
    mask[...] = head[...].astype(BF16)
    token[...] = jnp.zeros_like(token)

    def body(g):
        for j in range(GROUP):
            qt[head_rows(g, j), :] = jnp.transpose(q[:, head_columns(g, j)] * mask[...])
        load(go_far, base, g, go, sems.at[0, g]).wait()
        load(gi_far, base, g, gi, sems.at[1, g]).wait()
        for j in range(GROUP):
            c = head_columns(g, j)
            w[:, c] = go[:, c].astype(F32) * sigmoid_parts(gi[:, c])[0]

    each_group(body)


def prepare(flip, q, head, after, go, gi):
    return call(
        functools.partial(prepare_kernel, flip), "prepare", 1.5e9, [q, head, after],
        [half_shape(F32), half_shape(BF16), vmem((STATE_ROWS, TOK), BF16), TOKEN], [go, gi],
        [
            pltpu.VMEM((TOK, WIDE), BF16),
            pltpu.SemaphoreType.DMA((2, GROUPS)),
            pltpu.VMEM((TOK, HD), BF16),
        ],
    )


def cross_kernel(flip, ids, attn_in, q, s, w, head, gain, *rest):
    previous = rest[0] if flip else None
    attn, sums, squares, inners = rest[-4:]
    base = base_column(ids, flip)
    squares[...] = jnp.zeros_like(squares)
    inners[...] = jnp.zeros_like(inners)

    def body(g):
        for j in range(GROUP):
            c = head_columns(g, j)
            a = attn_in[:, c] + dot(q[:, c], s[head_rows(g, j), :], 1, 0) * head[...]
            attn[:, c] = a
            squares[...] += a * a
            scale = gain[:, pl.ds(pl.multiple_of(base + g * SPAN + j * HD, HD), HD)]
            inners[...] += w[:, c] * a * scale

    each_group(body)
    ones = jnp.ones((8, HD), F32)
    dims = (((1,), (1,)), ((), ()))
    ss, dd = [
        lax.dot_general(
            ones, x[...], dims, precision=lax.Precision.HIGHEST, preferred_element_type=F32
        )
        for x in (squares, inners)
    ]
    total = jnp.where(lax.broadcasted_iota(jnp.int32, (8, TOK), 0) < 4, ss, dd)
    if flip:
        total = total + previous[...]
    sums[...] = total


def cross(flip, attn, q, state, w, head, gain, previous=()):
    return call(
        functools.partial(cross_kernel, flip), "cross", 1.2e9,
        [attn, q, state, w, head, gain, *previous], [half_shape(F32), vmem((8, TOK), F32)], (),
        [pltpu.VMEM((TOK, HD), F32), pltpu.VMEM((TOK, HD), F32)],
    )


def scales(sums, rinv_ref, back_ref):
    own, one, two, three = [r[...] for r in sums]
    total = (own + one) + (two + three)
    rinv = lax.rsqrt(total[0:1] * (1.0 / ATT) + EPSILON)
    back = rinv * rinv * rinv * total[4:5] * (1.0 / ATT)
    row = lax.broadcasted_iota(jnp.int32, (8, TOK), 0)
    both = jnp.where(
        row < 4, jnp.broadcast_to(rinv, (8, TOK)), jnp.broadcast_to(back, (8, TOK))
    )
    cols = jnp.transpose(both)
    rinv_ref[...] = jnp.broadcast_to(cols[:, 0:1], (TOK, HD))
    back_ref[...] = jnp.broadcast_to(cols[:, 4:5], (TOK, HD))


def grad_kernel(flip, ids, seg, attn, w, qt, gain, *rest):
    if flip:
        s0, s1, s2, s3, grad, out, rinv, back, gains = rest
        scales((s0, s1, s2, s3), rinv, back)
    else:
        rinv, back, grad, out, gains = rest
    base = base_column(ids, flip)
    _, first, last = ends(seg)
    out[STATE_ROWS : STATE_ROWS + TILE, :] = info_tile(8.0 - last, 8.0 - first)

    def body(g):
        for j in range(GROUP):
            c = head_columns(g, j)
            a = attn[:, c]
            gated = w[:, c] * rinv[...]
            gains[pl.ds(g * GROUP + j, 1), :] = jnp.sum(gated * a, axis=0, keepdims=True)
            scale = gain[:, pl.ds(pl.multiple_of(base + g * SPAN + j * HD, HD), HD)]
            x = (gated * scale - a * back[...]).astype(BF16)
            grad[:, c] = x
            out[head_rows(g, j), :] = dot(qt[head_rows(g, j), :], x, 1, 0).astype(BF16)

    each_group(body)
    out[STATE_ROWS + TILE : STATE_ROWS + 2 * TILE, :] = split_tile(gains[...])


def grad_attn(flip, seg, attn, w, qt, gain, extra):
    outs = [half_shape(BF16), vmem((STATE_ROWS + 2 * TILE, HD), BF16)]
    if flip:
        outs += [vmem((TOK, HD), F32), vmem((TOK, HD), F32)]
    return call(
        functools.partial(grad_kernel, flip), "grad_attn", 1.2e9,
        [seg, attn, w, qt, gain, *extra], outs, (), [pltpu.VMEM((8, HD), F32)],
    )


def local_grads_kernel(flip, ids, q, k, v, grad, s, w0, w1, m0, m1, head, _, *rest):
    dq_far, dk, dv, token, dq, sems = rest[-6:]
    base = base_column(ids, flip)
    token[...] = jnp.zeros_like(token)

    def body(g):
        for j in range(GROUP):
            c = head_columns(g, j)
            qh, kh, vh, gh = q[:, c], k[:, c], v[:, c], grad[:, c]
            d0, d1 = masked_pair(gh, vh, m0, m1)
            hop = dot(gh, s[head_rows(g, j), :], 1, 1) * head[...]
            dq[0:BLOCK, c] = (dot(d0, kh[0:BLOCK], 1, 0) + hop[0:BLOCK]).astype(BF16)
            dq[BLOCK:TOK, c] = (dot(d1, kh, 1, 0) + hop[BLOCK:TOK]).astype(BF16)
            a0, a1 = w0[head_rows(g, j, BLOCK), :], w1[head_rows(g, j, BLOCK), :]
            for ref, b0, b1, rows in ((dk, d0, d1, qh), (dv, a0, a1, gh)):
                late = dot(b1, rows[BLOCK:TOK], 0, 0)
                ref[0:BLOCK, c] = late[0:BLOCK] + dot(b0, rows[0:BLOCK], 0, 0)
                ref[BLOCK:TOK, c] = late[BLOCK:TOK]
        store(dq, base, g, dq_far, sems.at[g]).start()

    each_group(body)
    for g in range(GROUPS):
        store(dq, base, g, dq_far, sems.at[g]).wait()


def local_grads(flip, q, k, v, g, state, w0, w1, masks, head, after, before=()):
    return call(
        functools.partial(local_grads_kernel, flip), "local_grads", 5e9,
        [q, k, v, g, state, w0, w1, *masks, head, after],
        [far(), half_shape(F32), half_shape(F32), TOKEN], before,
        [pltpu.VMEM((TOK, WIDE), BF16), pltpu.SemaphoreType.DMA((GROUPS,))],
        {11: 0} if before else None,
    )


def gates_kernel(flip, ids, attn, gi, w, rinv, gain, _, *rest):
    lo_far, gg_far, token, lo, gg, sems = rest[-6:]
    base = base_column(ids, flip)
    token[...] = jnp.zeros_like(token)

    def body(g):
        for j in range(GROUP):
            c = head_columns(g, j)
            sig, other = sigmoid_parts(gi[:, c])
            scale = gain[:, pl.ds(pl.multiple_of(base + g * SPAN + j * HD, HD), HD)]
            scaled = attn[:, c] * rinv[...] * scale
            lo[:, c] = (scaled * sig).astype(BF16)
            gg[:, c] = (scaled * w[:, c] * other).astype(BF16)
        store(lo, base, g, lo_far, sems.at[0, g]).start()
        store(gg, base, g, gg_far, sems.at[1, g]).start()

    each_group(body)
    for g in range(GROUPS):
        store(lo, base, g, lo_far, sems.at[0, g]).wait()
        store(gg, base, g, gg_far, sems.at[1, g]).wait()


def gates(flip, attn, gi, w, rinv, gain, after, before=()):
    return call(
        functools.partial(gates_kernel, flip), "gates", 1.2e9, [attn, gi, w, rinv, gain, after],
        [far(), far(), TOKEN], before,
        [
            pltpu.VMEM((TOK, WIDE), BF16),
            pltpu.VMEM((TOK, WIDE), BF16),
            pltpu.SemaphoreType.DMA((2, GROUPS)),
        ],
        {6: 0, 7: 1} if before else None,
    )


def finish_kernel(flip, ids, dk_in, dv_in, k, v, later, tail, *rest):
    if flip:
        total, _, _, dk_far, dv_far, gain_far, dk, dv, sems, gain, gain_sem = rest
        core = ids[0]
        at = [pl.ds(pl.multiple_of(n * 8, 8), 8) for n in (core, 1 - core)]
        gain[at[0], :] = joined_tile(total[...])
        gain[at[1], :] = joined_tile(later[STATE_ROWS : STATE_ROWS + TILE, :])
        gain_copy = pltpu.make_async_copy(gain, gain_far, gain_sem)
        gain_copy.start()
    else:
        dk_far, dv_far, dk, dv, sems = rest
    base = base_column(ids, flip)

    def body(g):
        for j in range(GROUP):
            c = head_columns(g, j)
            m = later[head_rows(g, j), :]
            dk[:, c] = (dk_in[:, c] + dot(v[:, c], m, 1, 1) * tail[...]).astype(BF16)
            dv[:, c] = (dv_in[:, c] + dot(k[:, c], m, 1, 0) * tail[...]).astype(BF16)
        store(dk, base, g, dk_far, sems.at[0, g]).start()
        store(dv, base, g, dv_far, sems.at[1, g]).start()

    each_group(body)
    for g in range(GROUPS):
        store(dk, base, g, dk_far, sems.at[0, g]).wait()
        store(dv, base, g, dv_far, sems.at[1, g]).wait()
    if flip:
        gain_copy.wait()


def finish(flip, dk, dv, k, v, later, tail, total=(), before=()):
    near = [dk, dv, k, v, later, tail, *total]
    outs = [far(), far()]
    scratch = [
        pltpu.VMEM((TOK, WIDE), BF16),
        pltpu.VMEM((TOK, WIDE), BF16),
        pltpu.SemaphoreType.DMA((2, GROUPS)),
    ]
    if flip:
        outs += [jax.ShapeDtypeStruct((TILE, HD), F32)]
        scratch += [pltpu.VMEM((TILE, HD), F32), pltpu.SemaphoreType.DMA]
    return call(
        functools.partial(finish_kernel, flip), "finish", 1.2e9, near, outs, before, scratch,
        {len(near): 0, len(near) + 1: 1} if flip else None,
    )


def place(ids, reverse):
    core, x, z = ids[0], ids[1], ids[2]
    return (1 - core, 3 - x, 3 - z) if reverse else (core, x, z)


def info_rows(ref, at):
    tile = ref[at : at + TILE, :].astype(F32)
    return tile[0:1], tile[8:9]


def flag(cond):
    return jnp.where(cond, 1.0, 0.0)


def sorted_cores(first_core, own, other):
    return jnp.where(first_core, own, other), jnp.where(first_core, other, own)


def quarter_rows(ids, m):
    return pl.ds(pl.multiple_of((ids[1] ^ m) * QUARTER, QUARTER), QUARTER)


def chip_kernel(reverse, gain, ids, own_ref, other_ref, *outs):
    vcore, _, _ = place(ids, reverse)
    first_core = vcore == 0
    low_own, high_own = info_rows(own_ref, STATE_ROWS)
    low_other, high_other = info_rows(other_ref, STATE_ROWS)
    low_a, _ = sorted_cores(first_core, low_own, low_other)
    high_a, high_b = sorted_cores(first_core, high_own, high_other)
    join = flag(high_a == high_b)
    own_weight = jnp.where(first_core, join, 1.0)
    other_weight = jnp.where(first_core, 1.0, join)
    for m, out in enumerate(outs):
        rows = quarter_rows(ids, m)
        total = own_ref[rows, :].astype(F32) * own_weight
        total = total + other_ref[rows, :].astype(F32) * other_weight
        out[0:QUARTER, :] = total.astype(BF16)
        out[QUARTER : QUARTER + TILE, :] = info_tile(low_a, high_b)
        if gain:
            at = slice(STATE_ROWS + TILE, STATE_ROWS + 2 * TILE)
            both = joined_tile(own_ref[at, :]) + joined_tile(other_ref[at, :])
            out[QUARTER + TILE : QUARTER + 2 * TILE, :] = split_tile(both)


def row_kernel(gain, ids, p0, p1, p2, p3, _, out):
    parts = (p0, p1, p2, p3)
    info = [info_rows(p, QUARTER) for p in parts]
    low = jnp.minimum(jnp.minimum(info[0][0], info[1][0]), jnp.minimum(info[2][0], info[3][0]))
    high = jnp.maximum(jnp.maximum(info[0][1], info[1][1]), jnp.maximum(info[2][1], info[3][1]))
    total = None
    for p, (_, own_high) in zip(parts, info):
        term = p[0:QUARTER, :].astype(F32) * flag(own_high == high)
        total = term if total is None else total + term
    out[0:QUARTER, :] = total.astype(BF16)
    out[QUARTER : QUARTER + TILE, :] = info_tile(low, high)
    if gain:
        g = [joined_tile(p[QUARTER + TILE : QUARTER + 2 * TILE, :]) for p in parts]
        out[QUARTER + TILE : QUARTER + 2 * TILE, :] = split_tile((g[0] + g[1]) + (g[2] + g[3]))


def entry_kernel(reverse, gain, ids, p0, p1, p2, p3, t0, t1, t2, t3, _, *outs):
    _, vx, vz = place(ids, reverse)
    parts = (p0, p1, p2, p3)
    rows = (t0, t1, t2, t3)
    info = [info_rows(p, QUARTER) for p in parts]
    row_high = [info_rows(t, QUARTER)[1] for t in rows]
    for m in range(4):
        low = info[m][0]
        total = jnp.zeros((QUARTER, HD), F32)
        for n in range(4):
            if n != m:
                weight = flag(info[n][1] == low) * flag((vx ^ n) < (vx ^ m))
                total = total + parts[n][0:QUARTER, :].astype(F32) * weight
        for n in range(1, 4):
            weight = flag(row_high[n] == low) * flag((vz ^ n) < vz)
            total = total + rows[n][0:QUARTER, :].astype(F32) * weight
        outs[m][...] = total.astype(BF16)
    if gain:
        g = [joined_tile(t[QUARTER + TILE : QUARTER + 2 * TILE, :]) for t in rows]
        outs[4][...] = split_tile((g[0] + g[1]) + (g[2] + g[3]))


def device_kernel(reverse, gain, ids, own_ref, other_ref, e0, e1, e2, e3, _, *rest):
    keep, send = rest[-2:]
    vcore, _, _ = place(ids, reverse)
    first_core = vcore == 0
    low_own, high_own = info_rows(own_ref, STATE_ROWS)
    low_other, high_other = info_rows(other_ref, STATE_ROWS)
    low_a, low_b = sorted_cores(first_core, low_own, low_other)
    high_a, _ = sorted_cores(first_core, high_own, high_other)
    from_a = flag(high_a == low_b)
    from_chip = flag(low_a == low_b)
    for m, ref in enumerate((e0, e1, e2, e3)):
        rows = quarter_rows(ids, m)
        entry = ref[...].astype(F32)
        a = jnp.where(first_core, own_ref[rows, :].astype(F32), other_ref[rows, :].astype(F32))
        second = a * from_a + entry * from_chip
        keep[rows, :] = jnp.where(first_core, entry, second).astype(BF16)
        send[rows, :] = jnp.where(first_core, second, entry).astype(BF16)
    if gain:
        send[STATE_ROWS : STATE_ROWS + TILE, :] = rest[0][...]


def glue(kernel, name, rows, *args):
    return call(kernel, name, 5e8, args, [vmem((r, HD), BF16) for r in rows])


def swap(x, axis, size, bits):
    return lax.ppermute(x, axis, [(i, i ^ bits) for i in range(size)])


def chip_swap(x):
    return swap(x, "ctx", 32, 1)


def row_swap(x, m):
    return swap(x, "ctx", 32, m << 1)


def plane_swap(x, m):
    return swap(x, "ctx", 32, m << 3)


def scan(own, other, reverse, gain, beside_x, beside_z, beside_back):
    extra = TILE if gain else 0
    rows = QUARTER + TILE + extra
    sent = glue(
        functools.partial(chip_kernel, reverse, gain), "chip_sum", [rows] * 4, own, other
    )
    parts = [sent[0]] + [row_swap(sent[m], m) for m in range(1, 4)]
    token = beside_x(sent[0])
    total = glue(functools.partial(row_kernel, gain), "row_sum", [rows], *parts, token)[0]
    totals = [total] + [plane_swap(total, m) for m in range(1, 4)]
    token = beside_z(total)
    entries = glue(
        functools.partial(entry_kernel, reverse, gain),
        "entry",
        [QUARTER] * 4 + ([TILE] if gain else []),
        *parts,
        *totals,
        token,
    )
    tail = entries[4:]
    back = [entries[0]] + [row_swap(entries[m], m) for m in range(1, 4)]
    token = beside_back(entries[0])
    keep, send = glue(
        functools.partial(device_kernel, reverse, gain),
        "device_entry",
        [STATE_ROWS, STATE_ROWS + extra],
        own,
        other,
        *back,
        token,
        *tail,
    )
    return keep, chip_swap(send), tail


def on_device(query, keys, values, gate_input, grad_output, norm_gain, segment_ids):
    gain = norm_gain.reshape(1, -1)

    k_send, v_send, sent, seg, head, tail = local_state(keys, values, segment_ids.reshape(1, TOK)
    )
    other = chip_swap(sent)
    k_keep, v_keep, own = local_state(keys, values, None, seg, tail)
    made = {}

    def intra_keep(after):
        made["keep"] = intra(k_keep, v_keep, query, after, seg=seg)
        return made["keep"][4]

    def intra_send(after):
        made["send"] = intra(k_send, v_send, query, after, masks=made["keep"][5:7])
        return made["send"][4]

    def prepare_both(after):
        made["pk"] = prepare(0, made["keep"][0], head, after, grad_output, gate_input)
        made["ps"] = prepare(1, made["send"][0], head, made["pk"][3], grad_output, gate_input
        )
        return made["ps"][3]

    state_keep, state_send, _ = scan(own, other, False, False, intra_keep, intra_send, prepare_both
    )
    q_keep, attn_keep, w0_keep, w1_keep, _, m0, m1 = made["keep"]
    q_send, attn_send, w0_send, w1_send, _ = made["send"]
    gated_keep, gi_keep, qt_keep, _ = made["pk"]
    gated_send, gi_send, qt_send, _ = made["ps"]

    attn_keep, sums = cross(0, attn_keep, q_keep, state_keep, gated_keep, head, gain
    )
    attn_send, sums = cross(1, attn_send, q_send, state_send, gated_send, head, gain, (sums,)
    )
    sums = [sums] + [swap(sums, "tp", 4, m) for m in range(1, 4)]

    g_send, sent, rinv, back = grad_attn(1, seg, attn_send, gated_send, qt_send, gain, sums
    )
    other = chip_swap(sent)
    g_keep, own = grad_attn(0, seg, attn_keep, gated_keep, qt_keep, gain, (rinv, back)
    )

    def grads_keep(after):
        made["gk"] = local_grads(0, q_keep, k_keep, v_keep, g_keep, state_keep, w0_keep, w1_keep, (m0, m1),
            head, after,
        )
        return made["gk"][3]

    def grads_send(after):
        made["gs"] = local_grads(1, q_send, k_send, v_send, g_send, state_send, w0_send, w1_send, (m0, m1),
            head, after, (made["gk"][0],),
        )
        return made["gs"][3]

    def gates_both(after):
        first = gates(0, attn_keep, gi_keep, gated_keep, rinv, gain, after)
        made["out"] = gates(1, attn_send, gi_send, gated_send, rinv, gain, first[2], tuple(first[:2])
        )
        return made["out"][2]

    later_keep, later_send, total = scan(own, other, True, True, grads_keep, grads_send, gates_both
    )
    _, dk_keep, dv_keep, _ = made["gk"]
    grad_query, dk_send, dv_send, _ = made["gs"]
    layer_out, grad_gate, _ = made["out"]
    done = finish(0, dk_keep, dv_keep, k_keep, v_keep, later_keep, tail)
    grad_keys, grad_values, grad_gain = finish(
        1, dk_send, dv_send, k_send, v_send, later_send, tail, (total[0],), tuple(done)
    )
    grad_gain = grad_gain.reshape(-1)
    return layer_out, grad_query, grad_keys, grad_values, grad_gate, grad_gain


def solution(mesh):
    in_specs = (P("ctx", "tp"),) * 5 + (P("tp"), P("ctx"))
    out_specs = (P("ctx", "tp"),) * 5 + (P("tp"),)
    return jax.shard_map(
        on_device, mesh=mesh, in_specs=in_specs, out_specs=out_specs, check_vma=False
    )
```

```python
import functools

import jax
import jax.numpy as jnp
from jax import lax
from jax.experimental import pallas as pl
from jax.experimental.pallas import tpu as pltpu
from jax.sharding import PartitionSpec as P

HD = 128
ATT = 8192
EPSILON = 1e-06
TOK = 512
BLOCK = 256
HEADS = 8
WIDE = HEADS * HD
GROUP = 4
GROUPS = HEADS // GROUP
SPAN = GROUP * HD
STATE_ROWS = HEADS * HD
QUARTER = 2 * HD
TILE = 16
F32 = jnp.float32
BF16 = jnp.bfloat16
VMEM_LIMIT = 16 * 1024 * 1024
VM = pl.BlockSpec(memory_space=pltpu.VMEM)
SM = pl.BlockSpec(memory_space=pltpu.SMEM)
ANY = pl.BlockSpec(memory_space=pl.ANY)


def dot(a, b, da, db):
    return lax.dot_general(a, b, (((da,), (db,)), ((), ())), preferred_element_type=F32)


def vmem(shape, dtype):
    return pltpu.VMEM(shape, dtype)


def half_shape(dtype):
    return vmem((TOK, WIDE), dtype)


def far(dtype=BF16):
    return jax.ShapeDtypeStruct((TOK, 2 * WIDE), dtype)


def call(kernel, name, flops, near, outs, distant=(), scratch=(), aliases=None):
    near = [pltpu.with_memory_space_constraint(a, pltpu.VMEM) for a in near]
    distant = [pltpu.with_memory_space_constraint(a, pltpu.HBM) for a in distant]
    out_specs = [ANY if isinstance(o, jax.ShapeDtypeStruct) else VM for o in outs]

    def placed(*refs):
        where = lax.axis_index("ctx")
        kernel((where & 1, (where >> 1) & 3, where >> 3), *refs)

    return pl.pallas_call(
        placed,
        in_specs=[VM] * len(near) + [ANY] * len(distant),
        out_specs=out_specs,
        out_shape=list(outs),
        scratch_shapes=list(scratch),
        input_output_aliases=aliases or {},
        compiler_params=pltpu.CompilerParams(vmem_limit_bytes=VMEM_LIMIT),
        cost_estimate=pl.CostEstimate(
            flops=int(flops), bytes_accessed=int(flops / 300), transcendentals=0
        ),
        name=name,
    )(*near, *distant)


def base_column(ids, flip):
    return pl.multiple_of((ids[0] ^ flip) * WIDE, WIDE)


def each_group(body, groups=GROUPS):
    def step(g, carry):
        body(g)
        return carry

    lax.fori_loop(0, groups, step, 0)


def head_columns(h):
    return pl.ds(pl.multiple_of(h * HD, HD), HD)


def head_rows(h, rows=HD):
    return pl.ds(pl.multiple_of(h * rows, rows), rows)


def span(start, width):
    return pl.ds(pl.multiple_of(start, width), width)


def load(source, base, at, target, sem, width=SPAN):
    return pltpu.make_async_copy(
        source.at[:, span(base + at, width)], target.at[:, span(at, width)], sem
    )


def store(source, at, base, target, sem, width=SPAN):
    return pltpu.make_async_copy(
        source.at[:, span(at, width)], target.at[:, span(base, width)], sem
    )


def info_tile(low, high):
    row = lax.broadcasted_iota(jnp.int32, (TILE, HD), 0)
    return jnp.where(
        row < 8, jnp.broadcast_to(low, (TILE, HD)), jnp.broadcast_to(high, (TILE, HD))
    ).astype(BF16)


def split_tile(x):
    high = x.astype(BF16).astype(F32)
    return jnp.concatenate([high, x - high], axis=0).astype(BF16)


def joined_tile(tile):
    t = tile.astype(F32)
    return t[0:8] + t[8:16]


def split_ends(seg_ref):
    seg = seg_ref[...].astype(F32)
    return seg[:, 0:1], seg[:, BLOCK - 1 : BLOCK], seg[:, BLOCK : BLOCK + 1], seg[:, TOK - 1 : TOK]


def flag(cond):
    return jnp.where(cond, 1.0, 0.0)


def fill_token_masks(seg_ref, before, after, last, first):
    start0, end0, start1, end1 = split_ends(seg_ref)
    col = jnp.transpose(jnp.broadcast_to(seg_ref[...].astype(F32), (8, TOK)))[:, 0:1]
    col = jnp.broadcast_to(col, (TOK, HD))
    for ref, id0, id1 in (
        (last, end0, end1), (before, start0, end0), (after, start1, end1), (first, start0, start1)
    ):
        ref[0:BLOCK, :] = flag(col[0:BLOCK] == id0).astype(BF16)
        ref[BLOCK:TOK, :] = flag(col[BLOCK:TOK] == id1).astype(BF16)


FINE = 2
FINE_SPAN = FINE * HD


def state_kernel(flip, ids, *refs):
    if flip:
        k_far, v_far, seg_far, k, v, out, early, seg, before, after, last, first, sems, seg_sem = refs
    else:
        seg, last, k_far, v_far, k, v, out, early, sems = refs
    base = base_column(ids, flip)
    groups = HEADS // FINE
    copies = [
        [
            load(far_ref, base, g * FINE_SPAN, ref, sems.at[n, g], FINE_SPAN)
            for n, (far_ref, ref) in enumerate(((k_far, k), (v_far, v)))
        ]
        for g in range(groups)
    ]
    if flip:
        copy = pltpu.make_async_copy(seg_far, seg, seg_sem)
        copy.start()
    for pair in copies:
        for c in pair:
            c.start()
    if flip:
        copy.wait()
        fill_token_masks(seg, before, after, last, first)
    start0, end0, _, end1 = split_ends(seg)
    join = flag(end0 == end1)
    out[STATE_ROWS : STATE_ROWS + TILE, :] = info_tile(start0, end1)
    for g in range(groups):
        for c in copies[g]:
            c.wait()
        for h in range(g * FINE, (g + 1) * FINE):
            kh = k[:, head_columns(h)] * last[...]
            vh = v[:, head_columns(h)]
            one = dot(kh[0:BLOCK], vh[0:BLOCK], 0, 0)
            two = dot(kh[BLOCK:TOK], vh[BLOCK:TOK], 0, 0)
            early[head_rows(h), :] = one
            out[head_rows(h), :] = (two + one * join).astype(BF16)


def local_state(k, v, seg, seg_vmem=None, last=None):
    flip = seg_vmem is None
    outs = [
        half_shape(BF16), half_shape(BF16), vmem((STATE_ROWS + TILE, HD), BF16),
        vmem((STATE_ROWS, HD), F32),
    ]
    scratch = [pltpu.SemaphoreType.DMA((2, HEADS // FINE))]
    near, distant = [seg_vmem, last], [k, v]
    if flip:
        outs += [vmem((1, TOK), jnp.int32)] + [vmem((TOK, HD), BF16)] * 4
        scratch += [pltpu.SemaphoreType.DMA]
        near, distant = [], [k, v, seg]
    return call(
        functools.partial(state_kernel, int(flip)), "local_state", 1e9, near, outs, distant, scratch
    )


def fill_masks(seg_ref, m0, m1):
    seg = seg_ref[...].astype(F32)
    col = jnp.transpose(jnp.broadcast_to(seg, (8, TOK)))[:, 0:1]
    t = lax.broadcasted_iota(jnp.int32, (BLOCK, BLOCK), 0)
    s = lax.broadcasted_iota(jnp.int32, (BLOCK, BLOCK), 1)
    for start, ref in ((0, m0), (BLOCK, m1)):
        same = col[start : start + BLOCK] == seg[:, start : start + BLOCK]
        ref[...] = flag(same & (s <= t)).astype(BF16)


def masked(left, right, mask):
    return dot(left, right, 1, 1).astype(BF16) * mask[...]


BLOCKS = ((0, slice(0, BLOCK)), (1, slice(BLOCK, TOK)))


def intra_kernel(flip, ids, *refs):
    if flip:
        k, v, first, m0, m1, _, q_far, q, attn, w0, w1, qt, token, sems = refs
    else:
        k, v, first, seg, _, q_far, q, attn, w0, w1, qt, token, m0, m1, sems = refs
    base = base_column(ids, flip)
    for g in range(GROUPS):
        load(q_far, base, g * SPAN, q, sems.at[g]).start()
    if not flip:
        fill_masks(seg, m0, m1)
    token[...] = jnp.zeros_like(token)

    def body(g):
        load(q_far, base, g * SPAN, q, sems.at[g]).wait()
        for j in range(GROUP):
            h = g * GROUP + j
            c = head_columns(h)
            qh, kh, vh = q[:, c], k[:, c], v[:, c]
            for n, t in BLOCKS:
                w = masked(qh[t], kh[t], (m0, m1)[n])
                (w0, w1)[n][head_rows(h, BLOCK), :] = w
                attn[t, c] = dot(w, vh[t], 1, 0)
            qt[head_rows(h), :] = jnp.transpose(qh * first[...])

    each_group(body)


TOKEN = vmem((8, HD), F32)


def intra(k, v, first, q, after, seg=None, masks=None):
    outs = [
        half_shape(BF16),
        half_shape(F32),
        vmem((HEADS * BLOCK, BLOCK), BF16),
        vmem((HEADS * BLOCK, BLOCK), BF16),
        vmem((STATE_ROWS, TOK), BF16),
        TOKEN,
    ]
    if masks is None:
        near = [k, v, first, seg, after]
        outs += [vmem((BLOCK, BLOCK), BF16), vmem((BLOCK, BLOCK), BF16)]
    else:
        near = [k, v, first, *masks, after]
    return call(
        functools.partial(intra_kernel, int(masks is not None)), "intra", 3e9, near, outs, [q],
        [pltpu.SemaphoreType.DMA((GROUPS,))],
    )


def sigmoid_parts(gi):
    bend = 0.5 * jnp.tanh(0.5 * gi.astype(F32))
    return 0.5 + bend, 0.5 - bend


def prepare_kernel(ids, _, go_far, gi_far, w, gi, token, go, sems):
    pairs = ((go_far, go), (gi_far, gi))
    for g in range(2 * GROUPS):
        for n, (far_ref, ref) in enumerate(pairs):
            load(far_ref, 0, g * SPAN, ref, sems.at[n, g]).start()
    token[...] = jnp.zeros_like(token)

    def body(g):
        for n, (far_ref, ref) in enumerate(pairs):
            load(far_ref, 0, g * SPAN, ref, sems.at[n, g]).wait()
        for j in range(GROUP):
            c = head_columns(g * GROUP + j)
            w[:, c] = go[:, c].astype(F32) * sigmoid_parts(gi[:, c])[0]

    each_group(body, 2 * GROUPS)


def prepare(after, go, gi):
    return call(
        prepare_kernel, "prepare", 3e9, [after],
        [vmem((TOK, 2 * WIDE), F32), vmem((TOK, 2 * WIDE), BF16), TOKEN], [go, gi],
        [pltpu.VMEM((TOK, 2 * WIDE), BF16), pltpu.SemaphoreType.DMA((2, 2 * GROUPS))],
    )


def cross_kernel(flip, ids, attn_in, q, s, early, w, before, seg, gain, *rest):
    previous = rest[0] if flip else None
    attn, second, sums, squares, inners = rest[-5:]
    base = base_column(ids, flip)
    squares[...] = jnp.zeros_like(squares)
    inners[...] = jnp.zeros_like(inners)
    start0, end0, _, _ = split_ends(seg)
    join = flag(start0 == end0)

    def body(g):
        for j in range(GROUP):
            h = g * GROUP + j
            c, rows = head_columns(h), head_rows(h)
            far_c = span(base + h * HD, HD)
            one = s[rows, :]
            two = (early[rows, :] + one.astype(F32) * join).astype(BF16)
            second[rows, :] = two
            qh = q[:, c] * before[...]
            scale = gain[:, far_c]
            for n, t in BLOCKS:
                a = attn_in[t, c] + dot(qh[t], (one, two)[n], 1, 0)
                attn[t, c] = a
                squares[t, :] += a * a
                inners[t, :] += w[t, far_c] * a * scale

    each_group(body)
    ones = jnp.ones((8, HD), F32)
    dims = (((1,), (1,)), ((), ()))
    ss, dd = [
        lax.dot_general(
            ones, x[...], dims, precision=lax.Precision.HIGHEST, preferred_element_type=F32
        )
        for x in (squares, inners)
    ]
    total = jnp.where(lax.broadcasted_iota(jnp.int32, (8, TOK), 0) < 4, ss, dd)
    if flip:
        total = total + previous[...]
    sums[...] = total


def cross(flip, attn, q, state, early, w, before, seg, gain, previous=()):
    return call(
        functools.partial(cross_kernel, flip), "cross", 1.2e9,
        [attn, q, state, early, w, before, seg, gain, *previous],
        [half_shape(F32), vmem((STATE_ROWS, HD), BF16), vmem((8, TOK), F32)], (),
        [pltpu.VMEM((TOK, HD), F32), pltpu.VMEM((TOK, HD), F32)],
    )


def scales(sums, rinv_ref, back_ref):
    own, one, two, three = [r[...] for r in sums]
    total = (own + one) + (two + three)
    rinv = lax.rsqrt(total[0:1] * (1.0 / ATT) + EPSILON)
    back = rinv * rinv * rinv * total[4:5] * (1.0 / ATT)
    row = lax.broadcasted_iota(jnp.int32, (8, TOK), 0)
    both = jnp.where(
        row < 4, jnp.broadcast_to(rinv, (8, TOK)), jnp.broadcast_to(back, (8, TOK))
    )
    cols = jnp.transpose(both)
    rinv_ref[...] = jnp.broadcast_to(cols[:, 0:1], (TOK, HD))
    back_ref[...] = jnp.broadcast_to(cols[:, 4:5], (TOK, HD))


def grad_kernel(flip, ids, seg, attn, w, qt, gain, *rest):
    if flip:
        s0, s1, s2, s3, grad, out, late, rinv, back, gains = rest
        scales((s0, s1, s2, s3), rinv, back)
    else:
        rinv, back, grad, out, late, gains = rest
    base = base_column(ids, flip)
    start0, _, start1, end1 = split_ends(seg)
    join = flag(start0 == start1)
    out[STATE_ROWS : STATE_ROWS + TILE, :] = info_tile(8.0 - end1, 8.0 - start0)

    def body(g):
        for j in range(GROUP):
            h = g * GROUP + j
            c, rows = head_columns(h), head_rows(h)
            far_c = span(base + h * HD, HD)
            a = attn[:, c]
            gated = w[:, far_c] * rinv[...]
            gains[pl.ds(h, 1), :] = jnp.sum(gated * a, axis=0, keepdims=True)
            x = (gated * gain[:, far_c] - a * back[...]).astype(BF16)
            grad[:, c] = x
            one = dot(qt[rows, 0:BLOCK], x[0:BLOCK], 1, 0)
            two = dot(qt[rows, BLOCK:TOK], x[BLOCK:TOK], 1, 0)
            late[rows, :] = two
            out[rows, :] = (one + two * join).astype(BF16)

    each_group(body)
    out[STATE_ROWS + TILE : STATE_ROWS + 2 * TILE, :] = split_tile(gains[...])


def grad_attn(flip, seg, attn, w, qt, gain, extra):
    outs = [
        half_shape(BF16), vmem((STATE_ROWS + 2 * TILE, HD), BF16), vmem((STATE_ROWS, HD), F32)
    ]
    if flip:
        outs += [vmem((TOK, HD), F32), vmem((TOK, HD), F32)]
    return call(
        functools.partial(grad_kernel, flip), "grad_attn", 1.2e9,
        [seg, attn, w, qt, gain, *extra], outs, (), [pltpu.VMEM((8, HD), F32)],
    )


def local_grads_kernel(flip, ids, q, k, v, grad, s0, s1, w0, w1, m0, m1, before, _, *rest):
    dq_far, dk, dv, token, dq, sems = rest[-6:]
    base = base_column(ids, flip)
    token[...] = jnp.zeros_like(token)

    def body(g):
        for j in range(GROUP):
            h = g * GROUP + j
            c = head_columns(h)
            qh, kh, vh, gh = q[:, c], k[:, c], v[:, c], grad[:, c]
            cut = gh * before[...]
            for n, t in BLOCKS:
                d = masked(gh[t], vh[t], (m0, m1)[n])
                w = (w0, w1)[n][head_rows(h, BLOCK), :]
                hop = dot(cut[t], (s0, s1)[n][head_rows(h), :], 1, 1)
                dq[t, c] = (dot(d, kh[t], 1, 0) + hop).astype(BF16)
                dk[t, c] = dot(d, qh[t], 0, 0)
                dv[t, c] = dot(w, gh[t], 0, 0)
        store(dq, g * SPAN, base + g * SPAN, dq_far, sems.at[g]).start()

    each_group(body)
    for g in range(GROUPS):
        store(dq, g * SPAN, base + g * SPAN, dq_far, sems.at[g]).wait()


def local_grads(flip, q, k, v, g, states, weights, masks, before, after, done=()):
    near = [q, k, v, g, *states, *weights, *masks, before, after]
    return call(
        functools.partial(local_grads_kernel, flip), "local_grads", 5e9, near,
        [far(), half_shape(F32), half_shape(F32), TOKEN], done,
        [pltpu.VMEM((TOK, WIDE), BF16), pltpu.SemaphoreType.DMA((GROUPS,))],
        {len(near): 0} if done else None,
    )


def gates_kernel(ids, keep, send, gi, w, rinv, gain, _, lo_far, gg_far, token, lo, gg, sems):
    token[...] = jnp.zeros_like(token)
    copies = []
    for flip, attn in enumerate((keep, send)):
        base = base_column(ids, flip)

        def body(g, flip=flip, attn=attn, base=base):
            for j in range(GROUP):
                h = g * GROUP + j
                far_c = span(base + h * HD, HD)
                out_c = head_columns(flip * HEADS + h)
                sig, other = sigmoid_parts(gi[:, far_c])
                scaled = attn[:, head_columns(h)] * rinv[...] * gain[:, far_c]
                lo[:, out_c] = (scaled * sig).astype(BF16)
                gg[:, out_c] = (scaled * w[:, far_c] * other).astype(BF16)
            at, to = flip * WIDE + g * SPAN, base + g * SPAN
            store(lo, at, to, lo_far, sems.at[0, flip, g]).start()
            store(gg, at, to, gg_far, sems.at[1, flip, g]).start()

        each_group(body)
        for g in range(GROUPS):
            at, to = flip * WIDE + g * SPAN, base + g * SPAN
            copies.append(store(lo, at, to, lo_far, sems.at[0, flip, g]))
            copies.append(store(gg, at, to, gg_far, sems.at[1, flip, g]))
    for copy in copies:
        copy.wait()


def gates(keep, send, gi, w, rinv, gain, after):
    return call(
        gates_kernel, "gates", 3e9, [keep, send, gi, w, rinv, gain, after],
        [far(), far(), TOKEN], (),
        [
            pltpu.VMEM((TOK, 2 * WIDE), BF16),
            pltpu.VMEM((TOK, 2 * WIDE), BF16),
            pltpu.SemaphoreType.DMA((2, 2, GROUPS)),
        ],
    )


def finish_kernel(flip, ids, dk_in, dv_in, k, v, later, late, seg, after, *rest):
    if flip:
        total, _, _, dk_far, dv_far, gain_far, dk, dv, sems, gain, gain_sem = rest
        core = ids[0]
        at = [pl.ds(pl.multiple_of(n * 8, 8), 8) for n in (core, 1 - core)]
        gain[at[0], :] = joined_tile(total[...])
        gain[at[1], :] = joined_tile(later[STATE_ROWS : STATE_ROWS + TILE, :])
        gain_copy = pltpu.make_async_copy(gain, gain_far, gain_sem)
        gain_copy.start()
    else:
        dk_far, dv_far, dk, dv, sems = rest
    base = base_column(ids, flip)
    _, _, start1, end1 = split_ends(seg)
    join = flag(start1 == end1)
    copies = []
    for g in range(HEADS // FINE):
        for h in range(g * FINE, (g + 1) * FINE):
            c, rows = head_columns(h), head_rows(h)
            one = later[rows, :]
            both = ((late[rows, :] + one.astype(F32) * join).astype(BF16), one)
            kh, vh = k[:, c] * after[...], v[:, c] * after[...]
            for n, t in BLOCKS:
                dk[t, c] = (dk_in[t, c] + dot(vh[t], both[n], 1, 1)).astype(BF16)
                dv[t, c] = (dv_in[t, c] + dot(kh[t], both[n], 1, 0)).astype(BF16)
        for n, (ref, far_ref) in enumerate(((dk, dk_far), (dv, dv_far))):
            at = g * FINE_SPAN
            copy = store(ref, at, base + at, far_ref, sems.at[n, g], FINE_SPAN)
            copy.start()
            copies.append(copy)
    for copy in copies:
        copy.wait()
    if flip:
        gain_copy.wait()


def finish(flip, dk, dv, k, v, later, late, seg, after, total=(), done=()):
    near = [dk, dv, k, v, later, late, seg, after, *total]
    outs = [far(), far()]
    scratch = [
        pltpu.VMEM((TOK, WIDE), BF16),
        pltpu.VMEM((TOK, WIDE), BF16),
        pltpu.SemaphoreType.DMA((2, HEADS // FINE)),
    ]
    if flip:
        outs += [jax.ShapeDtypeStruct((TILE, HD), F32)]
        scratch += [pltpu.VMEM((TILE, HD), F32), pltpu.SemaphoreType.DMA]
    return call(
        functools.partial(finish_kernel, flip), "finish", 1.2e9, near, outs, done, scratch,
        {len(near): 0, len(near) + 1: 1} if flip else None,
    )


def place(ids, reverse):
    core, x, z = ids[0], ids[1], ids[2]
    return (1 - core, 3 - x, 3 - z) if reverse else (core, x, z)


def info_rows(ref, at):
    tile = ref[at : at + TILE, :].astype(F32)
    return tile[0:1], tile[8:9]


def sorted_cores(first_core, own, other):
    return jnp.where(first_core, own, other), jnp.where(first_core, other, own)


def quarter_rows(ids, m):
    return pl.ds(pl.multiple_of((ids[1] ^ m) * QUARTER, QUARTER), QUARTER)


def chip_kernel(reverse, gain, ids, own_ref, other_ref, *outs):
    vcore, _, _ = place(ids, reverse)
    first_core = vcore == 0
    low_own, high_own = info_rows(own_ref, STATE_ROWS)
    low_other, high_other = info_rows(other_ref, STATE_ROWS)
    low_a, _ = sorted_cores(first_core, low_own, low_other)
    high_a, high_b = sorted_cores(first_core, high_own, high_other)
    join = flag(high_a == high_b)
    own_weight = jnp.where(first_core, join, 1.0)
    other_weight = jnp.where(first_core, 1.0, join)
    for m, out in enumerate(outs):
        rows = quarter_rows(ids, m)
        total = own_ref[rows, :].astype(F32) * own_weight
        total = total + other_ref[rows, :].astype(F32) * other_weight
        out[0:QUARTER, :] = total.astype(BF16)
        out[QUARTER : QUARTER + TILE, :] = info_tile(low_a, high_b)
        if gain:
            at = slice(STATE_ROWS + TILE, STATE_ROWS + 2 * TILE)
            both = joined_tile(own_ref[at, :]) + joined_tile(other_ref[at, :])
            out[QUARTER + TILE : QUARTER + 2 * TILE, :] = split_tile(both)


def row_kernel(gain, ids, p0, p1, p2, p3, _, out):
    parts = (p0, p1, p2, p3)
    info = [info_rows(p, QUARTER) for p in parts]
    low = jnp.minimum(jnp.minimum(info[0][0], info[1][0]), jnp.minimum(info[2][0], info[3][0]))
    high = jnp.maximum(jnp.maximum(info[0][1], info[1][1]), jnp.maximum(info[2][1], info[3][1]))
    total = None
    for p, (_, own_high) in zip(parts, info):
        term = p[0:QUARTER, :].astype(F32) * flag(own_high == high)
        total = term if total is None else total + term
    out[0:QUARTER, :] = total.astype(BF16)
    out[QUARTER : QUARTER + TILE, :] = info_tile(low, high)
    if gain:
        g = [joined_tile(p[QUARTER + TILE : QUARTER + 2 * TILE, :]) for p in parts]
        out[QUARTER + TILE : QUARTER + 2 * TILE, :] = split_tile((g[0] + g[1]) + (g[2] + g[3]))


def entry_kernel(reverse, gain, ids, p0, p1, p2, p3, *rest):
    _, vx, vz = place(ids, reverse)
    parts = (p0, p1, p2, p3)
    outs = rest[-5 if gain else -4 :]
    if gain:
        rows = rest[1:4]
        earlier = [(vz ^ n) < vz for n in range(1, 4)]
    else:
        rows = rest[1:3]
        earlier = [vz >= 1, vz >= 2]
    info = [info_rows(p, QUARTER) for p in parts]
    row_high = [info_rows(t, QUARTER)[1] for t in rows]
    for m in range(4):
        low = info[m][0]
        total = jnp.zeros((QUARTER, HD), F32)
        for n in range(4):
            if n != m:
                weight = flag(info[n][1] == low) * flag((vx ^ n) < (vx ^ m))
                total = total + parts[n][0:QUARTER, :].astype(F32) * weight
        for row, high, before in zip(rows, row_high, earlier):
            weight = flag(high == low) * flag(before)
            total = total + row[0:QUARTER, :].astype(F32) * weight
        outs[m][...] = total.astype(BF16)
    if gain:
        g = [joined_tile(t[QUARTER + TILE : QUARTER + 2 * TILE, :]) for t in rest[0:4]]
        outs[4][...] = split_tile((g[0] + g[1]) + (g[2] + g[3]))


def device_kernel(reverse, gain, ids, own_ref, other_ref, e0, e1, e2, e3, _, *rest):
    keep, send = rest[-2:]
    vcore, _, _ = place(ids, reverse)
    first_core = vcore == 0
    low_own, high_own = info_rows(own_ref, STATE_ROWS)
    low_other, high_other = info_rows(other_ref, STATE_ROWS)
    low_a, low_b = sorted_cores(first_core, low_own, low_other)
    high_a, _ = sorted_cores(first_core, high_own, high_other)
    from_a = flag(high_a == low_b)
    from_chip = flag(low_a == low_b)
    for m, ref in enumerate((e0, e1, e2, e3)):
        rows = quarter_rows(ids, m)
        entry = ref[...].astype(F32)
        a = jnp.where(first_core, own_ref[rows, :].astype(F32), other_ref[rows, :].astype(F32))
        second = a * from_a + entry * from_chip
        keep[rows, :] = jnp.where(first_core, entry, second).astype(BF16)
        send[rows, :] = jnp.where(first_core, second, entry).astype(BF16)
    if gain:
        send[STATE_ROWS : STATE_ROWS + TILE, :] = rest[0][...]


def glue(kernel, name, rows, *args):
    return call(kernel, name, 5e8, args, [vmem((r, HD), BF16) for r in rows])


def swap(x, axis, size, bits):
    return lax.ppermute(x, axis, [(i, i ^ bits) for i in range(size)])


def chip_swap(x):
    return swap(x, "ctx", 32, 1)


def row_swap(x, m):
    return swap(x, "ctx", 32, m << 1)


def plane_swap(x, m):
    return swap(x, "ctx", 32, m << 3)


def plane_shift(x):
    return lax.ppermute(x, "ctx", [(i, (i + 8) % 32) for i in range(32)])


def scan(own, other, reverse, gain, beside_x, beside_z, beside_back):
    extra = TILE if gain else 0
    rows = QUARTER + TILE + extra
    sent = glue(
        functools.partial(chip_kernel, reverse, gain), "chip_sum", [rows] * 4, own, other
    )
    parts = [sent[0]] + [row_swap(sent[m], m) for m in range(1, 4)]
    token = beside_x(sent[0])
    total = glue(functools.partial(row_kernel, gain), "row_sum", [rows], *parts, token)[0]
    if gain:
        totals = [total] + [plane_swap(total, m) for m in range(1, 4)]
    else:
        totals = [total, plane_shift(total), plane_swap(total, 2)]
    token = beside_z(total)
    entries = glue(
        functools.partial(entry_kernel, reverse, gain),
        "entry",
        [QUARTER] * 4 + ([TILE] if gain else []),
        *parts,
        *totals,
        token,
    )
    tail = entries[4:]
    back = [entries[0]] + [row_swap(entries[m], m) for m in range(1, 4)]
    token = beside_back(entries[0])
    keep, send = glue(
        functools.partial(device_kernel, reverse, gain),
        "device_entry",
        [STATE_ROWS, STATE_ROWS + extra],
        own,
        other,
        *back,
        token,
        *tail,
    )
    return keep, chip_swap(send), tail


def on_device(query, keys, values, gate_input, grad_output, norm_gain, segment_ids):
    gain = norm_gain.reshape(1, -1)

    k_send, v_send, sent, early_send, seg, before, after, last, first = local_state(
        keys, values, segment_ids.reshape(1, TOK)
    )
    other = chip_swap(sent)
    k_keep, v_keep, own, early_keep = local_state(keys, values, None, seg, last)
    made = {}

    def intra_keep(token):
        made["keep"] = intra(k_keep, v_keep, first, query, token, seg=seg)
        return made["keep"][5]

    def intra_send(token):
        made["send"] = intra(k_send, v_send, first, query, token, masks=made["keep"][6:8])
        return made["send"][5]

    def prepare_both(token):
        made["gate"] = prepare(token, grad_output, gate_input)
        return made["gate"][2]

    state_keep, state_send, _ = scan(own, other, False, False, intra_keep, intra_send, prepare_both)
    q_keep, attn_keep, w0_keep, w1_keep, qt_keep, _, *masks = made["keep"]
    q_send, attn_send, w0_send, w1_send, qt_send, _ = made["send"]
    gated, gate, _ = made["gate"]

    attn_keep, second_keep, sums = cross(
        0, attn_keep, q_keep, state_keep, early_keep, gated, before, seg, gain
    )
    attn_send, second_send, sums = cross(
        1, attn_send, q_send, state_send, early_send, gated, before, seg, gain, (sums,)
    )
    sums = [sums] + [swap(sums, "tp", 4, m) for m in range(1, 4)]

    g_send, sent, late_send, rinv, back = grad_attn(
        1, seg, attn_send, gated, qt_send, gain, sums
    )
    other = chip_swap(sent)
    g_keep, own, late_keep = grad_attn(0, seg, attn_keep, gated, qt_keep, gain, (rinv, back))

    def grads_keep(token):
        made["gk"] = local_grads(
            0, q_keep, k_keep, v_keep, g_keep, (state_keep, second_keep), (w0_keep, w1_keep),
            masks, before, token,
        )
        return made["gk"][3]

    def grads_send(token):
        made["gs"] = local_grads(
            1, q_send, k_send, v_send, g_send, (state_send, second_send), (w0_send, w1_send),
            masks, before, token, (made["gk"][0],),
        )
        return made["gs"][3]

    def gates_both(token):
        made["out"] = gates(attn_keep, attn_send, gate, gated, rinv, gain, token)
        return made["out"][2]

    later_keep, later_send, total = scan(
        own, other, True, True, grads_keep, grads_send, gates_both
    )
    _, dk_keep, dv_keep, _ = made["gk"]
    grad_query, dk_send, dv_send, _ = made["gs"]
    layer_out, grad_gate, _ = made["out"]
    done = finish(0, dk_keep, dv_keep, k_keep, v_keep, later_keep, late_keep, seg, after)
    grad_keys, grad_values, grad_gain = finish(
        1, dk_send, dv_send, k_send, v_send, later_send, late_send, seg, after, (total[0],),
        tuple(done),
    )
    grad_gain = grad_gain.reshape(-1)
    return layer_out, grad_query, grad_keys, grad_values, grad_gate, grad_gain


def solution(mesh):
    in_specs = (P("ctx", "tp"),) * 5 + (P("tp"), P("ctx"))
    out_specs = (P("ctx", "tp"),) * 5 + (P("tp"),)
    return jax.shard_map(
        on_device, mesh=mesh, in_specs=in_specs, out_specs=out_specs, check_vma=False
    )
```

```python
import functools

import jax
import jax.numpy as jnp
from jax import lax
from jax.experimental import pallas as pl
from jax.experimental.pallas import tpu as pltpu
from jax.sharding import PartitionSpec as P

HD = 128
ATT = 8192
EPSILON = 1e-06
TOK = 512
BLOCK = 256
HEADS = 8
WIDE = HEADS * HD
GROUP = 4
GROUPS = HEADS // GROUP
SPAN = GROUP * HD
STATE_ROWS = HEADS * HD
QUARTER = 2 * HD
TILE = 16
F32 = jnp.float32
BF16 = jnp.bfloat16
VMEM_LIMIT = 16 * 1024 * 1024
VM = pl.BlockSpec(memory_space=pltpu.VMEM)
SM = pl.BlockSpec(memory_space=pltpu.SMEM)
ANY = pl.BlockSpec(memory_space=pl.ANY)


def dot(a, b, da, db):
    return lax.dot_general(a, b, (((da,), (db,)), ((), ())), preferred_element_type=F32)


def vmem(shape, dtype):
    return pltpu.VMEM(shape, dtype)


def half_shape(dtype):
    return vmem((TOK, WIDE), dtype)


def far(dtype=BF16):
    return jax.ShapeDtypeStruct((TOK, 2 * WIDE), dtype)


def call(kernel, name, flops, near, outs, distant=(), scratch=(), aliases=None):
    near = [pltpu.with_memory_space_constraint(a, pltpu.VMEM) for a in near]
    distant = [pltpu.with_memory_space_constraint(a, pltpu.HBM) for a in distant]
    out_specs = [ANY if isinstance(o, jax.ShapeDtypeStruct) else VM for o in outs]

    def placed(*refs):
        where = lax.axis_index("ctx")
        kernel((where & 1, (where >> 1) & 3, where >> 3), *refs)

    return pl.pallas_call(
        placed,
        in_specs=[VM] * len(near) + [ANY] * len(distant),
        out_specs=out_specs,
        out_shape=list(outs),
        scratch_shapes=list(scratch),
        input_output_aliases=aliases or {},
        compiler_params=pltpu.CompilerParams(vmem_limit_bytes=VMEM_LIMIT),
        cost_estimate=pl.CostEstimate(
            flops=int(flops), bytes_accessed=int(flops / 300), transcendentals=0
        ),
        name=name,
    )(*near, *distant)


def base_column(ids, flip):
    return pl.multiple_of((ids[0] ^ flip) * WIDE, WIDE)


def each_group(body, groups=GROUPS):
    def step(g, carry):
        body(g)
        return carry

    lax.fori_loop(0, groups, step, 0)


def head_columns(h):
    return pl.ds(pl.multiple_of(h * HD, HD), HD)


def head_rows(h, rows=HD):
    return pl.ds(pl.multiple_of(h * rows, rows), rows)


def span(start, width):
    return pl.ds(pl.multiple_of(start, width), width)


def load(source, base, at, target, sem, width=SPAN):
    return pltpu.make_async_copy(
        source.at[:, span(base + at, width)], target.at[:, span(at, width)], sem
    )


def store(source, at, base, target, sem, width=SPAN):
    return pltpu.make_async_copy(
        source.at[:, span(at, width)], target.at[:, span(base, width)], sem
    )


def info_tile(low, high):
    row = lax.broadcasted_iota(jnp.int32, (TILE, HD), 0)
    return jnp.where(
        row < 8, jnp.broadcast_to(low, (TILE, HD)), jnp.broadcast_to(high, (TILE, HD))
    ).astype(BF16)


def split_tile(x):
    high = x.astype(BF16).astype(F32)
    return jnp.concatenate([high, x - high], axis=0).astype(BF16)


def joined_tile(tile):
    t = tile.astype(F32)
    return t[0:8] + t[8:16]


def split_ends(seg_ref):
    seg = seg_ref[...].astype(F32)
    return seg[:, 0:1], seg[:, BLOCK - 1 : BLOCK], seg[:, BLOCK : BLOCK + 1], seg[:, TOK - 1 : TOK]


def flag(cond):
    return jnp.where(cond, 1.0, 0.0)


def fill_last_mask(seg_ref, ref):
    seg = seg_ref[...].astype(F32)
    row = lax.broadcasted_iota(jnp.int32, (BLOCK, HD), 0).astype(F32)
    for _, t in BLOCKS:
        block = seg[:, t]
        same = jnp.sum(flag(block == block[:, BLOCK - 1 : BLOCK]), axis=1, keepdims=True)
        ref[t, :] = flag(row >= BLOCK - same).astype(BF16)


def fill_token_masks(seg_ref, col, before, after, first):
    start0, end0, start1, end1 = split_ends(seg_ref)
    wide = jnp.broadcast_to(col, (TOK, HD))
    for ref, ids in ((before, (start0, end0)), (after, (start1, end1)), (first, (start0, start1))):
        for n, t in BLOCKS:
            ref[t, :] = flag(wide[t] == ids[n]).astype(BF16)


BLOCKS = ((0, slice(0, BLOCK)), (1, slice(BLOCK, TOK)))
FINE = 2
FINE_SPAN = FINE * HD


def state_kernel(flip, ids, *refs):
    if flip:
        k_far, v_far, seg_far, k, v, out, early, seg, last, sems, seg_sem = refs
    else:
        seg, last, k_far, v_far, k, v, out, early, sems = refs
    base = base_column(ids, flip)
    groups = HEADS // FINE
    copies = [
        [
            load(far_ref, base, g * FINE_SPAN, ref, sems.at[n, g], FINE_SPAN)
            for n, (far_ref, ref) in enumerate(((k_far, k), (v_far, v)))
        ]
        for g in range(groups)
    ]
    if flip:
        copy = pltpu.make_async_copy(seg_far, seg, seg_sem)
        copy.start()
    for pair in copies:
        for c in pair:
            c.start()
    if flip:
        copy.wait()
        fill_last_mask(seg, last)
    start0, end0, _, end1 = split_ends(seg)
    join = flag(end0 == end1)
    out[STATE_ROWS : STATE_ROWS + TILE, :] = info_tile(start0, end1)
    for g in range(groups):
        for c in copies[g]:
            c.wait()
        group = range(g * FINE, (g + 1) * FINE)
        rows = [(k[:, head_columns(h)] * last[...], v[:, head_columns(h)]) for h in group]
        parts = [[dot(kh[t], vh[t], 0, 0) for _, t in BLOCKS] for kh, vh in rows]
        for h, (one, two) in zip(group, parts):
            early[head_rows(h), :] = one
            out[head_rows(h), :] = (two + one * join).astype(BF16)


def local_state(k, v, seg, seg_vmem=None, last=None):
    flip = seg_vmem is None
    outs = [
        half_shape(BF16), half_shape(BF16), vmem((STATE_ROWS + TILE, HD), BF16),
        vmem((STATE_ROWS, HD), F32),
    ]
    scratch = [pltpu.SemaphoreType.DMA((2, HEADS // FINE))]
    near, distant = [seg_vmem, last], [k, v]
    if flip:
        outs += [vmem((1, TOK), jnp.int32), vmem((TOK, HD), BF16)]
        scratch += [pltpu.SemaphoreType.DMA]
        near, distant = [], [k, v, seg]
    return call(
        functools.partial(state_kernel, int(flip)), "local_state", 1e9, near, outs, distant, scratch
    )


def fill_masks(seg_ref, m0, m1, *masks):
    seg = seg_ref[...].astype(F32)
    col = jnp.transpose(jnp.broadcast_to(seg, (8, TOK)))[:, 0:1]
    fill_token_masks(seg_ref, col, *masks)
    t = lax.broadcasted_iota(jnp.int32, (BLOCK, BLOCK), 0)
    s = lax.broadcasted_iota(jnp.int32, (BLOCK, BLOCK), 1)
    for start, ref in ((0, m0), (BLOCK, m1)):
        same = col[start : start + BLOCK] == seg[:, start : start + BLOCK]
        ref[...] = flag(same & (s <= t)).astype(BF16)


def masked(left, right, mask):
    return dot(left, right, 1, 1).astype(BF16) * mask[...]


def intra_kernel(flip, ids, *refs):
    if flip:
        k, v, m0, m1, first, _, q_far, q, attn, w0, w1, qt, token, sems = refs
    else:
        k, v, seg, _, q_far, q, attn, w0, w1, qt, token, m0, m1, before, after, first, sems = refs
    base = base_column(ids, flip)
    for g in range(GROUPS):
        load(q_far, base, g * SPAN, q, sems.at[g]).start()
    if not flip:
        fill_masks(seg, m0, m1, before, after, first)
    token[...] = jnp.zeros_like(token)

    def body(g):
        load(q_far, base, g * SPAN, q, sems.at[g]).wait()
        group = [g * GROUP + j for j in range(GROUP)]
        rows = [[ref[:, head_columns(h)] for ref in (q, k, v)] for h in group]
        flipped = [jnp.transpose(qh * first[...]) for qh, _, _ in rows]
        weights = [[masked(qh[t], kh[t], (m0, m1)[n]) for n, t in BLOCKS] for qh, kh, _ in rows]
        sums = [
            [dot(w[n], vh[t], 1, 0) for n, t in BLOCKS] for w, (_, _, vh) in zip(weights, rows)
        ]
        for h, turned, w, a in zip(group, flipped, weights, sums):
            qt[head_rows(h), :] = turned
            for n, t in BLOCKS:
                (w0, w1)[n][head_rows(h, BLOCK), :] = w[n]
                attn[t, head_columns(h)] = a[n]

    each_group(body)


TOKEN = vmem((8, HD), F32)


def intra(k, v, q, after, seg=None, masks=None):
    outs = [
        half_shape(BF16),
        half_shape(F32),
        vmem((HEADS * BLOCK, BLOCK), BF16),
        vmem((HEADS * BLOCK, BLOCK), BF16),
        vmem((STATE_ROWS, TOK), BF16),
        TOKEN,
    ]
    if masks is None:
        near = [k, v, seg, after]
        outs += [vmem((BLOCK, BLOCK), BF16)] * 2 + [vmem((TOK, HD), BF16)] * 3
    else:
        near = [k, v, *masks, after]
    return call(
        functools.partial(intra_kernel, int(masks is not None)), "intra", 3e9, near, outs, [q],
        [pltpu.SemaphoreType.DMA((GROUPS,))],
    )


def sigmoid_parts(gi):
    bend = 0.5 * jnp.tanh(0.5 * gi.astype(F32))
    return 0.5 + bend, 0.5 - bend


def prepare_kernel(ids, _, go_far, gi_far, w, gi, token, go, sems):
    pairs = ((go_far, go), (gi_far, gi))
    for g in range(2 * GROUPS):
        for n, (far_ref, ref) in enumerate(pairs):
            load(far_ref, 0, g * SPAN, ref, sems.at[n, g]).start()
    token[...] = jnp.zeros_like(token)

    def body(g):
        for n, (far_ref, ref) in enumerate(pairs):
            load(far_ref, 0, g * SPAN, ref, sems.at[n, g]).wait()
        for j in range(GROUP):
            c = head_columns(g * GROUP + j)
            w[:, c] = go[:, c].astype(F32) * sigmoid_parts(gi[:, c])[0]

    each_group(body, 2 * GROUPS)


def prepare(after, go, gi):
    return call(
        prepare_kernel, "prepare", 3e9, [after],
        [vmem((TOK, 2 * WIDE), F32), vmem((TOK, 2 * WIDE), BF16), TOKEN], [go, gi],
        [pltpu.VMEM((TOK, 2 * WIDE), BF16), pltpu.SemaphoreType.DMA((2, 2 * GROUPS))],
    )


def cross_kernel(flip, ids, attn_in, q, s, early, w, before, seg, gain, *rest):
    previous = rest[0] if flip else None
    attn, second, sums, squares, inners = rest[-5:]
    base = base_column(ids, flip)
    squares[...] = jnp.zeros_like(squares)
    inners[...] = jnp.zeros_like(inners)
    start0, end0, _, _ = split_ends(seg)
    join = flag(start0 == end0)

    def body(g):
        group = [g * GROUP + j for j in range(GROUP)]
        ones = [s[head_rows(h), :] for h in group]
        twos = [
            (early[head_rows(h), :] + one.astype(F32) * join).astype(BF16)
            for h, one in zip(group, ones)
        ]
        rows = [q[:, head_columns(h)] * before[...] for h in group]
        for n, t in BLOCKS:
            hops = [dot(qh[t], pair[n], 1, 0) for qh, pair in zip(rows, zip(ones, twos))]
            sums = [attn_in[t, head_columns(h)] + hop for h, hop in zip(group, hops)]
            square, inner = squares[t, :], inners[t, :]
            for h, a in zip(group, sums):
                far_c = span(base + h * HD, HD)
                square = square + a * a
                inner = inner + w[t, far_c] * a * gain[:, far_c]
            squares[t, :] = square
            inners[t, :] = inner
            for h, a in zip(group, sums):
                attn[t, head_columns(h)] = a
        for h, two in zip(group, twos):
            second[head_rows(h), :] = two

    each_group(body)
    ones = jnp.ones((8, HD), F32)
    dims = (((1,), (1,)), ((), ()))
    ss, dd = [
        lax.dot_general(
            ones, x[...], dims, precision=lax.Precision.HIGHEST, preferred_element_type=F32
        )
        for x in (squares, inners)
    ]
    total = jnp.where(lax.broadcasted_iota(jnp.int32, (8, TOK), 0) < 4, ss, dd)
    if flip:
        total = total + previous[...]
    sums[...] = total


def cross(flip, attn, q, state, early, w, before, seg, gain, previous=()):
    return call(
        functools.partial(cross_kernel, flip), "cross", 1.2e9,
        [attn, q, state, early, w, before, seg, gain, *previous],
        [half_shape(F32), vmem((STATE_ROWS, HD), BF16), vmem((8, TOK), F32)], (),
        [pltpu.VMEM((TOK, HD), F32), pltpu.VMEM((TOK, HD), F32)],
    )


def scales(sums, rinv_ref, back_ref):
    own, one, two, three = [r[...] for r in sums]
    total = (own + one) + (two + three)
    rinv = lax.rsqrt(total[0:1] * (1.0 / ATT) + EPSILON)
    back = rinv * rinv * rinv * total[4:5] * (1.0 / ATT)
    row = lax.broadcasted_iota(jnp.int32, (8, TOK), 0)
    both = jnp.where(
        row < 4, jnp.broadcast_to(rinv, (8, TOK)), jnp.broadcast_to(back, (8, TOK))
    )
    cols = jnp.transpose(both)
    rinv_ref[...] = jnp.broadcast_to(cols[:, 0:1], (TOK, HD))
    back_ref[...] = jnp.broadcast_to(cols[:, 4:5], (TOK, HD))


def grad_kernel(flip, ids, seg, attn, w, qt, gain, *rest):
    if flip:
        s0, s1, s2, s3, grad, out, late, rinv, back, gains = rest
        scales((s0, s1, s2, s3), rinv, back)
    else:
        rinv, back, grad, out, late, gains = rest
    base = base_column(ids, flip)
    start0, _, start1, end1 = split_ends(seg)
    join = flag(start0 == start1)
    out[STATE_ROWS : STATE_ROWS + TILE, :] = info_tile(8.0 - end1, 8.0 - start0)

    def body(g):
        group = [g * GROUP + j for j in range(GROUP)]
        turned = [qt[head_rows(h), :] for h in group]
        totals, rows = [], []
        for h in group:
            far_c = span(base + h * HD, HD)
            a = attn[:, head_columns(h)]
            gated = w[:, far_c] * rinv[...]
            totals.append(jnp.sum(gated * a, axis=0, keepdims=True))
            rows.append((gated * gain[:, far_c] - a * back[...]).astype(BF16))
        parts = [[dot(qh[:, t], x[t], 1, 0) for _, t in BLOCKS] for qh, x in zip(turned, rows)]
        for h, total, x, (one, two) in zip(group, totals, rows, parts):
            gains[pl.ds(h, 1), :] = total
            grad[:, head_columns(h)] = x
            late[head_rows(h), :] = two
            out[head_rows(h), :] = (one + two * join).astype(BF16)

    each_group(body)
    out[STATE_ROWS + TILE : STATE_ROWS + 2 * TILE, :] = split_tile(gains[...])


def grad_attn(flip, seg, attn, w, qt, gain, extra):
    outs = [
        half_shape(BF16), vmem((STATE_ROWS + 2 * TILE, HD), BF16), vmem((STATE_ROWS, HD), F32)
    ]
    if flip:
        outs += [vmem((TOK, HD), F32), vmem((TOK, HD), F32)]
    return call(
        functools.partial(grad_kernel, flip), "grad_attn", 1.2e9,
        [seg, attn, w, qt, gain, *extra], outs, (), [pltpu.VMEM((8, HD), F32)],
    )


def local_grads_kernel(flip, ids, q, k, v, grad, s0, s1, w0, w1, m0, m1, before, _, *rest):
    dq_far, dk, dv, token, dq, sems = rest[-6:]
    base = base_column(ids, flip)
    token[...] = jnp.zeros_like(token)

    def body(g):
        group = [g * GROUP + j for j in range(GROUP)]
        rows = [[ref[:, head_columns(h)] for ref in (q, k, v, grad)] for h in group]
        states = [[ref[head_rows(h), :] for ref in (s0, s1)] for h in group]
        weights = [[ref[head_rows(h, BLOCK), :] for ref in (w0, w1)] for h in group]
        inner = [
            [masked(gh[t], vh[t], (m0, m1)[n]) for n, t in BLOCKS] for _, _, vh, gh in rows
        ]
        outs = []
        for (qh, kh, _, gh), state, w, d in zip(rows, states, weights, inner):
            cut = gh * before[...]
            outs.append(
                [
                    (
                        dot(d[n], kh[t], 1, 0) + dot(cut[t], state[n], 1, 1),
                        dot(d[n], qh[t], 0, 0),
                        dot(w[n], gh[t], 0, 0),
                    )
                    for n, t in BLOCKS
                ]
            )
        for h, blocks in zip(group, outs):
            c = head_columns(h)
            for (n, t), (x, y, z) in zip(BLOCKS, blocks):
                dq[t, c] = x.astype(BF16)
                dk[t, c] = y
                dv[t, c] = z
        store(dq, g * SPAN, base + g * SPAN, dq_far, sems.at[g]).start()

    each_group(body)
    for g in range(GROUPS):
        store(dq, g * SPAN, base + g * SPAN, dq_far, sems.at[g]).wait()


def local_grads(flip, q, k, v, g, states, weights, masks, before, after, done=()):
    near = [q, k, v, g, *states, *weights, *masks, before, after]
    return call(
        functools.partial(local_grads_kernel, flip), "local_grads", 5e9, near,
        [far(), half_shape(F32), half_shape(F32), TOKEN], done,
        [pltpu.VMEM((TOK, WIDE), BF16), pltpu.SemaphoreType.DMA((GROUPS,))],
        {len(near): 0} if done else None,
    )


def gates_kernel(ids, keep, send, gi, w, rinv, gain, _, lo_far, gg_far, token, lo, gg, sems):
    token[...] = jnp.zeros_like(token)
    copies = []
    for flip, attn in enumerate((keep, send)):
        base = base_column(ids, flip)

        def body(g, flip=flip, attn=attn, base=base):
            for j in range(GROUP):
                h = g * GROUP + j
                far_c = span(base + h * HD, HD)
                out_c = head_columns(flip * HEADS + h)
                sig, other = sigmoid_parts(gi[:, far_c])
                scaled = attn[:, head_columns(h)] * rinv[...] * gain[:, far_c]
                lo[:, out_c] = (scaled * sig).astype(BF16)
                gg[:, out_c] = (scaled * w[:, far_c] * other).astype(BF16)
            at, to = flip * WIDE + g * SPAN, base + g * SPAN
            store(lo, at, to, lo_far, sems.at[0, flip, g]).start()
            store(gg, at, to, gg_far, sems.at[1, flip, g]).start()

        each_group(body)
        for g in range(GROUPS):
            at, to = flip * WIDE + g * SPAN, base + g * SPAN
            copies.append(store(lo, at, to, lo_far, sems.at[0, flip, g]))
            copies.append(store(gg, at, to, gg_far, sems.at[1, flip, g]))
    for copy in copies:
        copy.wait()


def gates(keep, send, gi, w, rinv, gain, after):
    return call(
        gates_kernel, "gates", 3e9, [keep, send, gi, w, rinv, gain, after],
        [far(), far(), TOKEN], (),
        [
            pltpu.VMEM((TOK, 2 * WIDE), BF16),
            pltpu.VMEM((TOK, 2 * WIDE), BF16),
            pltpu.SemaphoreType.DMA((2, 2, GROUPS)),
        ],
    )


def finish_kernel(flip, ids, dk_in, dv_in, k, v, later, late, seg, after, *rest):
    if flip:
        total, _, _, dk_far, dv_far, gain_far, dk, dv, sems, gain, gain_sem = rest
        core = ids[0]
        at = [pl.ds(pl.multiple_of(n * 8, 8), 8) for n in (core, 1 - core)]
        gain[at[0], :] = joined_tile(total[...])
        gain[at[1], :] = joined_tile(later[STATE_ROWS : STATE_ROWS + TILE, :])
        gain_copy = pltpu.make_async_copy(gain, gain_far, gain_sem)
        gain_copy.start()
    else:
        dk_far, dv_far, dk, dv, sems = rest
    base = base_column(ids, flip)
    _, _, start1, end1 = split_ends(seg)
    join = flag(start1 == end1)
    copies = []
    for g in range(HEADS // FINE):
        group = range(g * FINE, (g + 1) * FINE)
        states = []
        for h in group:
            one = later[head_rows(h), :]
            states.append(
                ((late[head_rows(h), :] + one.astype(F32) * join).astype(BF16), one)
            )
        rows = [
            (k[:, head_columns(h)] * after[...], v[:, head_columns(h)] * after[...]) for h in group
        ]
        hops = [
            [(dot(vh[t], state[n], 1, 1), dot(kh[t], state[n], 1, 0)) for n, t in BLOCKS]
            for (kh, vh), state in zip(rows, states)
        ]
        sums = [
            [
                (dk_in[t, head_columns(h)] + hop[n][0], dv_in[t, head_columns(h)] + hop[n][1])
                for n, t in BLOCKS
            ]
            for h, hop in zip(group, hops)
        ]
        for h, blocks in zip(group, sums):
            for (_, t), (x, y) in zip(BLOCKS, blocks):
                dk[t, head_columns(h)] = x.astype(BF16)
                dv[t, head_columns(h)] = y.astype(BF16)
        for n, (ref, far_ref) in enumerate(((dk, dk_far), (dv, dv_far))):
            at = g * FINE_SPAN
            copy = store(ref, at, base + at, far_ref, sems.at[n, g], FINE_SPAN)
            copy.start()
            copies.append(copy)
    for copy in copies:
        copy.wait()
    if flip:
        gain_copy.wait()


def finish(flip, dk, dv, k, v, later, late, seg, after, total=(), done=()):
    near = [dk, dv, k, v, later, late, seg, after, *total]
    outs = [far(), far()]
    scratch = [
        pltpu.VMEM((TOK, WIDE), BF16),
        pltpu.VMEM((TOK, WIDE), BF16),
        pltpu.SemaphoreType.DMA((2, HEADS // FINE)),
    ]
    if flip:
        outs += [jax.ShapeDtypeStruct((TILE, HD), F32)]
        scratch += [pltpu.VMEM((TILE, HD), F32), pltpu.SemaphoreType.DMA]
    return call(
        functools.partial(finish_kernel, flip), "finish", 1.2e9, near, outs, done, scratch,
        {len(near): 0, len(near) + 1: 1} if flip else None,
    )


def place(ids, reverse):
    core, x, z = ids[0], ids[1], ids[2]
    return (1 - core, 3 - x, 3 - z) if reverse else (core, x, z)


def info_rows(ref, at):
    tile = ref[at : at + TILE, :].astype(F32)
    return tile[0:1], tile[8:9]


def sorted_cores(first_core, own, other):
    return jnp.where(first_core, own, other), jnp.where(first_core, other, own)


def quarter_rows(ids, m):
    return pl.ds(pl.multiple_of((ids[1] ^ m) * QUARTER, QUARTER), QUARTER)


def chip_kernel(reverse, gain, ids, own_ref, other_ref, *outs):
    vcore, _, _ = place(ids, reverse)
    first_core = vcore == 0
    low_own, high_own = info_rows(own_ref, STATE_ROWS)
    low_other, high_other = info_rows(other_ref, STATE_ROWS)
    low_a, _ = sorted_cores(first_core, low_own, low_other)
    high_a, high_b = sorted_cores(first_core, high_own, high_other)
    join = flag(high_a == high_b)
    own_weight = jnp.where(first_core, join, 1.0)
    other_weight = jnp.where(first_core, 1.0, join)
    for m, out in enumerate(outs):
        rows = quarter_rows(ids, m)
        total = own_ref[rows, :].astype(F32) * own_weight
        total = total + other_ref[rows, :].astype(F32) * other_weight
        out[0:QUARTER, :] = total.astype(BF16)
        out[QUARTER : QUARTER + TILE, :] = info_tile(low_a, high_b)
        if gain:
            at = slice(STATE_ROWS + TILE, STATE_ROWS + 2 * TILE)
            both = joined_tile(own_ref[at, :]) + joined_tile(other_ref[at, :])
            out[QUARTER + TILE : QUARTER + 2 * TILE, :] = split_tile(both)


def row_kernel(gain, ids, p0, p1, p2, p3, _, out):
    parts = (p0, p1, p2, p3)
    info = [info_rows(p, QUARTER) for p in parts]
    low = jnp.minimum(jnp.minimum(info[0][0], info[1][0]), jnp.minimum(info[2][0], info[3][0]))
    high = jnp.maximum(jnp.maximum(info[0][1], info[1][1]), jnp.maximum(info[2][1], info[3][1]))
    total = None
    for p, (_, own_high) in zip(parts, info):
        term = p[0:QUARTER, :].astype(F32) * flag(own_high == high)
        total = term if total is None else total + term
    out[0:QUARTER, :] = total.astype(BF16)
    out[QUARTER : QUARTER + TILE, :] = info_tile(low, high)
    if gain:
        g = [joined_tile(p[QUARTER + TILE : QUARTER + 2 * TILE, :]) for p in parts]
        out[QUARTER + TILE : QUARTER + 2 * TILE, :] = split_tile((g[0] + g[1]) + (g[2] + g[3]))


def entry_kernel(reverse, gain, ids, p0, p1, p2, p3, *rest):
    _, vx, vz = place(ids, reverse)
    parts = (p0, p1, p2, p3)
    outs = rest[-5 if gain else -4 :]
    if gain:
        rows = rest[1:4]
        earlier = [(vz ^ n) < vz for n in range(1, 4)]
    else:
        rows = rest[1:3]
        earlier = [vz >= 1, vz >= 2]
    info = [info_rows(p, QUARTER) for p in parts]
    row_high = [info_rows(t, QUARTER)[1] for t in rows]
    for m in range(4):
        low = info[m][0]
        total = jnp.zeros((QUARTER, HD), F32)
        for n in range(4):
            if n != m:
                weight = flag(info[n][1] == low) * flag((vx ^ n) < (vx ^ m))
                total = total + parts[n][0:QUARTER, :].astype(F32) * weight
        for row, high, before in zip(rows, row_high, earlier):
            weight = flag(high == low) * flag(before)
            total = total + row[0:QUARTER, :].astype(F32) * weight
        outs[m][...] = total.astype(BF16)
    if gain:
        g = [joined_tile(t[QUARTER + TILE : QUARTER + 2 * TILE, :]) for t in rest[0:4]]
        outs[4][...] = split_tile((g[0] + g[1]) + (g[2] + g[3]))


def device_kernel(reverse, gain, ids, own_ref, other_ref, e0, e1, e2, e3, _, *rest):
    keep, send = rest[-2:]
    vcore, _, _ = place(ids, reverse)
    first_core = vcore == 0
    low_own, high_own = info_rows(own_ref, STATE_ROWS)
    low_other, high_other = info_rows(other_ref, STATE_ROWS)
    low_a, low_b = sorted_cores(first_core, low_own, low_other)
    high_a, _ = sorted_cores(first_core, high_own, high_other)
    from_a = flag(high_a == low_b)
    from_chip = flag(low_a == low_b)
    for m, ref in enumerate((e0, e1, e2, e3)):
        rows = quarter_rows(ids, m)
        entry = ref[...].astype(F32)
        a = jnp.where(first_core, own_ref[rows, :].astype(F32), other_ref[rows, :].astype(F32))
        second = a * from_a + entry * from_chip
        keep[rows, :] = jnp.where(first_core, entry, second).astype(BF16)
        send[rows, :] = jnp.where(first_core, second, entry).astype(BF16)
    if gain:
        send[STATE_ROWS : STATE_ROWS + TILE, :] = rest[0][...]


def glue(kernel, name, rows, *args):
    return call(kernel, name, 5e8, args, [vmem((r, HD), BF16) for r in rows])


def swap(x, axis, size, bits):
    return lax.ppermute(x, axis, [(i, i ^ bits) for i in range(size)])


def chip_swap(x):
    return swap(x, "ctx", 32, 1)


def row_swap(x, m):
    return swap(x, "ctx", 32, m << 1)


def plane_swap(x, m):
    return swap(x, "ctx", 32, m << 3)


def plane_shift(x):
    return lax.ppermute(x, "ctx", [(i, (i + 8) % 32) for i in range(32)])


def scan(own, other, reverse, gain, beside_x, beside_z, beside_back):
    extra = TILE if gain else 0
    rows = QUARTER + TILE + extra
    sent = glue(
        functools.partial(chip_kernel, reverse, gain), "chip_sum", [rows] * 4, own, other
    )
    parts = [sent[0]] + [row_swap(sent[m], m) for m in range(1, 4)]
    token = beside_x(sent[0])
    total = glue(functools.partial(row_kernel, gain), "row_sum", [rows], *parts, token)[0]
    if gain:
        totals = [total] + [plane_swap(total, m) for m in range(1, 4)]
    else:
        totals = [total, plane_shift(total), plane_swap(total, 2)]
    token = beside_z(total)
    entries = glue(
        functools.partial(entry_kernel, reverse, gain),
        "entry",
        [QUARTER] * 4 + ([TILE] if gain else []),
        *parts,
        *totals,
        token,
    )
    tail = entries[4:]
    back = [entries[0]] + [row_swap(entries[m], m) for m in range(1, 4)]
    token = beside_back(entries[0])
    keep, send = glue(
        functools.partial(device_kernel, reverse, gain),
        "device_entry",
        [STATE_ROWS, STATE_ROWS + extra],
        own,
        other,
        *back,
        token,
        *tail,
    )
    return keep, chip_swap(send), tail


def on_device(query, keys, values, gate_input, grad_output, norm_gain, segment_ids):
    gain = norm_gain.reshape(1, -1)

    k_send, v_send, sent, early_send, seg, last = local_state(
        keys, values, segment_ids.reshape(1, TOK)
    )
    other = chip_swap(sent)
    k_keep, v_keep, own, early_keep = local_state(keys, values, None, seg, last)
    made = {}

    def intra_keep(token):
        made["keep"] = intra(k_keep, v_keep, query, token, seg=seg)
        return made["keep"][5]

    def intra_send(token):
        m0, m1, _, _, first = made["keep"][6:]
        made["send"] = intra(k_send, v_send, query, token, masks=(m0, m1, first))
        return made["send"][5]

    def prepare_both(token):
        made["gate"] = prepare(token, grad_output, gate_input)
        return made["gate"][2]

    state_keep, state_send, _ = scan(own, other, False, False, intra_keep, intra_send, prepare_both)
    q_keep, attn_keep, w0_keep, w1_keep, qt_keep, _, *masks, before, after, _ = made["keep"]
    q_send, attn_send, w0_send, w1_send, qt_send, _ = made["send"]
    gated, gate, _ = made["gate"]

    attn_keep, second_keep, sums = cross(
        0, attn_keep, q_keep, state_keep, early_keep, gated, before, seg, gain
    )
    attn_send, second_send, sums = cross(
        1, attn_send, q_send, state_send, early_send, gated, before, seg, gain, (sums,)
    )
    sums = [sums] + [swap(sums, "tp", 4, m) for m in range(1, 4)]

    g_send, sent, late_send, rinv, back = grad_attn(
        1, seg, attn_send, gated, qt_send, gain, sums
    )
    other = chip_swap(sent)
    g_keep, own, late_keep = grad_attn(0, seg, attn_keep, gated, qt_keep, gain, (rinv, back))

    def grads_keep(token):
        made["gk"] = local_grads(
            0, q_keep, k_keep, v_keep, g_keep, (state_keep, second_keep), (w0_keep, w1_keep),
            masks, before, token,
        )
        return made["gk"][3]

    def grads_send(token):
        made["gs"] = local_grads(
            1, q_send, k_send, v_send, g_send, (state_send, second_send), (w0_send, w1_send),
            masks, before, token, (made["gk"][0],),
        )
        return made["gs"][3]

    def gates_both(token):
        made["out"] = gates(attn_keep, attn_send, gate, gated, rinv, gain, token)
        return made["out"][2]

    later_keep, later_send, total = scan(
        own, other, True, True, grads_keep, grads_send, gates_both
    )
    _, dk_keep, dv_keep, _ = made["gk"]
    grad_query, dk_send, dv_send, _ = made["gs"]
    layer_out, grad_gate, _ = made["out"]
    done = finish(0, dk_keep, dv_keep, k_keep, v_keep, later_keep, late_keep, seg, after)
    grad_keys, grad_values, grad_gain = finish(
        1, dk_send, dv_send, k_send, v_send, later_send, late_send, seg, after, (total[0],),
        tuple(done),
    )
    grad_gain = grad_gain.reshape(-1)
    return layer_out, grad_query, grad_keys, grad_values, grad_gate, grad_gain


def solution(mesh):
    in_specs = (P("ctx", "tp"),) * 5 + (P("tp"), P("ctx"))
    out_specs = (P("ctx", "tp"),) * 5 + (P("tp"),)
    return jax.shard_map(
        on_device, mesh=mesh, in_specs=in_specs, out_specs=out_specs, check_vma=False
    )
```

```python
import functools

import jax
import jax.numpy as jnp
from jax import lax
from jax.experimental import pallas as pl
from jax.experimental.pallas import tpu as pltpu
from jax.sharding import PartitionSpec as P

HD = 128
ATT = 8192
EPSILON = 1e-06
TOK = 512
BLOCK = 256
HEADS = 8
WIDE = HEADS * HD
GROUP = 4
GROUPS = HEADS // GROUP
SPAN = GROUP * HD
STATE_ROWS = HEADS * HD
QUARTER = 2 * HD
TILE = 16
F32 = jnp.float32
BF16 = jnp.bfloat16
VMEM_LIMIT = 16 * 1024 * 1024
VM = pl.BlockSpec(memory_space=pltpu.VMEM)
SM = pl.BlockSpec(memory_space=pltpu.SMEM)
ANY = pl.BlockSpec(memory_space=pl.ANY)


def dot(a, b, da, db):
    return lax.dot_general(a, b, (((da,), (db,)), ((), ())), preferred_element_type=F32)


def vmem(shape, dtype):
    return pltpu.VMEM(shape, dtype)


def half_shape(dtype):
    return vmem((TOK, WIDE), dtype)


def far(dtype=BF16):
    return jax.ShapeDtypeStruct((TOK, 2 * WIDE), dtype)


def call(kernel, name, flops, near, outs, distant=(), scratch=(), aliases=None):
    near = [pltpu.with_memory_space_constraint(a, pltpu.VMEM) for a in near]
    distant = [pltpu.with_memory_space_constraint(a, pltpu.HBM) for a in distant]
    out_specs = [ANY if isinstance(o, jax.ShapeDtypeStruct) else VM for o in outs]

    def placed(*refs):
        where = lax.axis_index("ctx")
        kernel((where & 1, (where >> 1) & 3, where >> 3), *refs)

    return pl.pallas_call(
        placed,
        in_specs=[VM] * len(near) + [ANY] * len(distant),
        out_specs=out_specs,
        out_shape=list(outs),
        scratch_shapes=list(scratch),
        input_output_aliases=aliases or {},
        compiler_params=pltpu.CompilerParams(vmem_limit_bytes=VMEM_LIMIT),
        cost_estimate=pl.CostEstimate(
            flops=int(flops), bytes_accessed=int(flops / 300), transcendentals=0
        ),
        name=name,
    )(*near, *distant)


def base_column(ids, flip):
    return pl.multiple_of((ids[0] ^ flip) * WIDE, WIDE)


def each_group(body, groups=GROUPS):
    def step(g, carry):
        body(g)
        return carry

    lax.fori_loop(0, groups, step, 0)


def head_columns(h):
    return pl.ds(pl.multiple_of(h * HD, HD), HD)


def head_rows(h, rows=HD):
    return pl.ds(pl.multiple_of(h * rows, rows), rows)


def span(start, width):
    return pl.ds(pl.multiple_of(start, width), width)


def store_half(source, base, target, sem):
    return pltpu.make_async_copy(source, target.at[:, span(base, WIDE)], sem)


def load(source, base, at, target, sem, width=SPAN):
    return pltpu.make_async_copy(
        source.at[:, span(base + at, width)], target.at[:, span(at, width)], sem
    )


def store(source, at, base, target, sem, width=SPAN):
    return pltpu.make_async_copy(
        source.at[:, span(at, width)], target.at[:, span(base, width)], sem
    )


def info_tile(low, high):
    row = lax.broadcasted_iota(jnp.int32, (TILE, HD), 0)
    return jnp.where(
        row < 8, jnp.broadcast_to(low, (TILE, HD)), jnp.broadcast_to(high, (TILE, HD))
    ).astype(BF16)


def split_tile(x):
    high = x.astype(BF16).astype(F32)
    return jnp.concatenate([high, x - high], axis=0).astype(BF16)


def joined_tile(tile):
    t = tile.astype(F32)
    return t[0:8] + t[8:16]


def split_ends(seg_ref):
    seg = seg_ref[...].astype(F32)
    return seg[:, 0:1], seg[:, BLOCK - 1 : BLOCK], seg[:, BLOCK : BLOCK + 1], seg[:, TOK - 1 : TOK]


def flag(cond):
    return jnp.where(cond, 1.0, 0.0)


def fill_last_mask(seg_ref, ref):
    seg = seg_ref[...].astype(F32)
    row = lax.broadcasted_iota(jnp.int32, (BLOCK, HD), 0).astype(F32)
    for _, t in BLOCKS:
        block = seg[:, t]
        same = jnp.sum(flag(block == block[:, BLOCK - 1 : BLOCK]), axis=1, keepdims=True)
        ref[t, :] = flag(row >= BLOCK - same).astype(BF16)


def fill_token_masks(seg_ref, col, before, after, first):
    start0, end0, start1, end1 = split_ends(seg_ref)
    wide = jnp.broadcast_to(col, (TOK, HD))
    for ref, ids in ((before, (start0, end0)), (after, (start1, end1)), (first, (start0, start1))):
        for n, t in BLOCKS:
            ref[t, :] = flag(wide[t] == ids[n]).astype(BF16)


BLOCKS = ((0, slice(0, BLOCK)), (1, slice(BLOCK, TOK)))
FINE = 2
FINE_SPAN = FINE * HD


def state_kernel(flip, ids, *refs):
    if flip:
        k_far, v_far, seg_far, k, v, out, early, seg, last, sems, seg_sem = refs
    else:
        seg, last, k_far, v_far, k, v, out, early, sems = refs
    base = base_column(ids, flip)
    copies = [
        [
            pltpu.make_async_copy(far_ref.at[t, span(base, WIDE)], ref.at[t, :], sems.at[m, n])
            for m, (far_ref, ref) in enumerate(((k_far, k), (v_far, v)))
        ]
        for n, t in BLOCKS
    ]
    for pair in copies:
        for c in pair:
            c.start()
    if flip:
        copy = pltpu.make_async_copy(seg_far, seg, seg_sem)
        copy.start()
        copy.wait()
        fill_last_mask(seg, last)
    start0, end0, _, end1 = split_ends(seg)
    join = flag(end0 == end1)
    out[STATE_ROWS : STATE_ROWS + TILE, :] = info_tile(start0, end1)
    for n, t in BLOCKS:
        for c in copies[n]:
            c.wait()
        rows = [(k[t, head_columns(h)] * last[t, :], v[t, head_columns(h)]) for h in range(HEADS)]
        parts = [dot(kh, vh, 0, 0) for kh, vh in rows]
        if n == 1:
            parts = [two + early[head_rows(h), :] * join for h, two in enumerate(parts)]
        for h, part in enumerate(parts):
            if n == 0:
                early[head_rows(h), :] = part
            else:
                out[head_rows(h), :] = part.astype(BF16)


def local_state(k, v, seg, seg_vmem=None, last=None):
    flip = seg_vmem is None
    outs = [
        half_shape(BF16), half_shape(BF16), vmem((STATE_ROWS + TILE, HD), BF16),
        vmem((STATE_ROWS, HD), F32),
    ]
    scratch = [pltpu.SemaphoreType.DMA((2, 2))]
    near, distant = [seg_vmem, last], [k, v]
    if flip:
        outs += [vmem((1, TOK), jnp.int32), vmem((TOK, HD), BF16)]
        scratch += [pltpu.SemaphoreType.DMA]
        near, distant = [], [k, v, seg]
    return call(
        functools.partial(state_kernel, int(flip)), "local_state", 1e9, near, outs, distant, scratch
    )


def fill_masks(seg_ref, m0, m1, *masks):
    seg = seg_ref[...].astype(F32)
    col = jnp.transpose(jnp.broadcast_to(seg, (8, TOK)))[:, 0:1]
    fill_token_masks(seg_ref, col, *masks)
    t = lax.broadcasted_iota(jnp.int32, (BLOCK, BLOCK), 0)
    s = lax.broadcasted_iota(jnp.int32, (BLOCK, BLOCK), 1)
    for start, ref in ((0, m0), (BLOCK, m1)):
        same = col[start : start + BLOCK] == seg[:, start : start + BLOCK]
        ref[...] = flag(same & (s <= t)).astype(BF16)


def masked(left, right, mask):
    return dot(left, right, 1, 1).astype(BF16) * mask[...]


def intra_kernel(flip, ids, *refs):
    if flip:
        k, v, m0, m1, first, _, q_far, q, attn, w0, w1, qt, token, sems = refs
    else:
        k, v, seg, _, q_far, q, attn, w0, w1, qt, token, m0, m1, before, after, first, sems = refs
    base = base_column(ids, flip)
    for g in range(GROUPS):
        load(q_far, base, g * SPAN, q, sems.at[g]).start()
    if not flip:
        fill_masks(seg, m0, m1, before, after, first)
    token[...] = jnp.zeros_like(token)

    def body(g):
        load(q_far, base, g * SPAN, q, sems.at[g]).wait()
        group = [g * GROUP + j for j in range(GROUP)]
        rows = [[ref[:, head_columns(h)] for ref in (q, k, v)] for h in group]
        flipped = [jnp.transpose(qh * first[...]) for qh, _, _ in rows]
        weights = [[masked(qh[t], kh[t], (m0, m1)[n]) for n, t in BLOCKS] for qh, kh, _ in rows]
        sums = [
            [dot(w[n], vh[t], 1, 0) for n, t in BLOCKS] for w, (_, _, vh) in zip(weights, rows)
        ]
        for h, turned, w, a in zip(group, flipped, weights, sums):
            qt[head_rows(h), :] = turned
            for n, t in BLOCKS:
                (w0, w1)[n][head_rows(h, BLOCK), :] = w[n]
                attn[t, head_columns(h)] = a[n]

    each_group(body)


TOKEN = vmem((8, HD), F32)


def intra(k, v, q, after, seg=None, masks=None):
    outs = [
        half_shape(BF16),
        half_shape(F32),
        vmem((HEADS * BLOCK, BLOCK), BF16),
        vmem((HEADS * BLOCK, BLOCK), BF16),
        vmem((STATE_ROWS, TOK), BF16),
        TOKEN,
    ]
    if masks is None:
        near = [k, v, seg, after]
        outs += [vmem((BLOCK, BLOCK), BF16)] * 2 + [vmem((TOK, HD), BF16)] * 3
    else:
        near = [k, v, *masks, after]
    return call(
        functools.partial(intra_kernel, int(masks is not None)), "intra", 3e9, near, outs, [q],
        [pltpu.SemaphoreType.DMA((GROUPS,))],
    )


def sigmoid_parts(gi):
    bend = 0.5 * jnp.tanh(0.5 * gi.astype(F32))
    return 0.5 + bend, 0.5 - bend


def prepare_kernel(ids, _, go_far, gi_far, w, gi, token, go, sems):
    pairs = ((go_far, go), (gi_far, gi))
    for g in range(2 * GROUPS):
        for n, (far_ref, ref) in enumerate(pairs):
            load(far_ref, 0, g * SPAN, ref, sems.at[n, g]).start()
    token[...] = jnp.zeros_like(token)

    def body(g):
        for n, (far_ref, ref) in enumerate(pairs):
            load(far_ref, 0, g * SPAN, ref, sems.at[n, g]).wait()
        for j in range(GROUP):
            c = head_columns(g * GROUP + j)
            w[:, c] = go[:, c].astype(F32) * sigmoid_parts(gi[:, c])[0]

    each_group(body, 2 * GROUPS)


def prepare(after, go, gi):
    return call(
        prepare_kernel, "prepare", 3e9, [after],
        [vmem((TOK, 2 * WIDE), F32), vmem((TOK, 2 * WIDE), BF16), TOKEN], [go, gi],
        [pltpu.VMEM((TOK, 2 * WIDE), BF16), pltpu.SemaphoreType.DMA((2, 2 * GROUPS))],
    )


def cross_kernel(flip, ids, attn_in, q, s, early, w, before, seg, gain, *rest):
    if flip:
        squares_in, inners_in, attn, second, sums, squares, inners = rest
        squares[...] = squares_in[...]
        inners[...] = inners_in[...]
    else:
        attn, second, squares, inners = rest
        squares[...] = jnp.zeros_like(squares)
        inners[...] = jnp.zeros_like(inners)
    base = base_column(ids, flip)
    start0, end0, _, _ = split_ends(seg)
    join = flag(start0 == end0)

    def body(g):
        group = [g * GROUP + j for j in range(GROUP)]
        ones = [s[head_rows(h), :] for h in group]
        twos = [
            (early[head_rows(h), :] + one.astype(F32) * join).astype(BF16)
            for h, one in zip(group, ones)
        ]
        rows = [q[:, head_columns(h)] * before[...] for h in group]
        for n, t in BLOCKS:
            hops = [dot(qh[t], pair[n], 1, 0) for qh, pair in zip(rows, zip(ones, twos))]
            sums = [attn_in[t, head_columns(h)] + hop for h, hop in zip(group, hops)]
            square, inner = squares[t, :], inners[t, :]
            for h, a in zip(group, sums):
                far_c = span(base + h * HD, HD)
                square = square + a * a
                inner = inner + w[t, far_c] * a * gain[:, far_c]
            squares[t, :] = square
            inners[t, :] = inner
            for h, a in zip(group, sums):
                attn[t, head_columns(h)] = a
        for h, two in zip(group, twos):
            second[head_rows(h), :] = two

    each_group(body)
    if flip:
        ones = jnp.ones((8, HD), BF16)
        totals = []
        for x in (squares[...], inners[...]):
            high = x.astype(BF16)
            low = (x - high.astype(F32)).astype(BF16)
            totals.append(dot(ones, high, 1, 1) + dot(ones, low, 1, 1))
        row = lax.broadcasted_iota(jnp.int32, (8, TOK), 0)
        sums[...] = jnp.where(row < 4, totals[0], totals[1])


def cross(flip, attn, q, state, early, w, before, seg, gain, previous=()):
    total = vmem((TOK, HD), F32)
    outs = [half_shape(F32), vmem((STATE_ROWS, HD), BF16)]
    return call(
        functools.partial(cross_kernel, flip), "cross", 1.2e9,
        [attn, q, state, early, w, before, seg, gain, *previous],
        outs + ([vmem((8, TOK), F32)] if flip else [total, total]), (),
        [pltpu.VMEM((TOK, HD), F32)] * 2 if flip else [],
    )


def scales(sums, rinv_ref, back_ref):
    own, one, two, three = [r[...] for r in sums]
    total = (own + one) + (two + three)
    rinv = lax.rsqrt(total[0:1] * (1.0 / ATT) + EPSILON)
    back = rinv * rinv * rinv * total[4:5] * (1.0 / ATT)
    row = lax.broadcasted_iota(jnp.int32, (8, TOK), 0)
    both = jnp.where(
        row < 4, jnp.broadcast_to(rinv, (8, TOK)), jnp.broadcast_to(back, (8, TOK))
    )
    cols = jnp.transpose(both)
    rinv_ref[...] = jnp.broadcast_to(cols[:, 0:1], (TOK, HD))
    back_ref[...] = jnp.broadcast_to(cols[:, 4:5], (TOK, HD))


def grad_kernel(flip, ids, seg, attn, w, qt, gain, *rest):
    if flip:
        s0, s1, s2, s3, grad, out, late, rinv, back, gains = rest
        scales((s0, s1, s2, s3), rinv, back)
    else:
        rinv, back, grad, out, late, gains = rest
    base = base_column(ids, flip)
    start0, _, start1, end1 = split_ends(seg)
    join = flag(start0 == start1)
    out[STATE_ROWS : STATE_ROWS + TILE, :] = info_tile(8.0 - end1, 8.0 - start0)

    def body(g):
        group = [g * GROUP + j for j in range(GROUP)]
        turned = [qt[head_rows(h), :] for h in group]
        totals, rows = [], []
        for h in group:
            far_c = span(base + h * HD, HD)
            a = attn[:, head_columns(h)]
            gated = w[:, far_c] * rinv[...]
            totals.append(jnp.sum(gated * a, axis=0, keepdims=True))
            rows.append((gated * gain[:, far_c] - a * back[...]).astype(BF16))
        parts = [[dot(qh[:, t], x[t], 1, 0) for _, t in BLOCKS] for qh, x in zip(turned, rows)]
        for h, total, x, (one, two) in zip(group, totals, rows, parts):
            gains[pl.ds(h, 1), :] = total
            grad[:, head_columns(h)] = x
            late[head_rows(h), :] = two
            out[head_rows(h), :] = (one + two * join).astype(BF16)

    each_group(body)
    out[STATE_ROWS + TILE : STATE_ROWS + 2 * TILE, :] = split_tile(gains[...])


def grad_attn(flip, seg, attn, w, qt, gain, extra):
    outs = [
        half_shape(BF16), vmem((STATE_ROWS + 2 * TILE, HD), BF16), vmem((STATE_ROWS, HD), F32)
    ]
    if flip:
        outs += [vmem((TOK, HD), F32), vmem((TOK, HD), F32)]
    return call(
        functools.partial(grad_kernel, flip), "grad_attn", 1.2e9,
        [seg, attn, w, qt, gain, *extra], outs, (), [pltpu.VMEM((8, HD), F32)],
    )


def local_grads_kernel(flip, ids, q, k, v, grad, s0, s1, w0, w1, m0, m1, before, _, *rest):
    if flip:
        dq_keep, dq_far, dq, dk, dv, token, sems = rest
        keep_copy = store_half(dq_keep, base_column(ids, 0), dq_far, sems.at[1])
        keep_copy.start()
        first_copy = store(dq, 0, base_column(ids, 1), dq_far, sems.at[0])
    else:
        dq, dk, dv, token = rest
    token[...] = jnp.zeros_like(token)

    def body(g):
        group = [g * GROUP + j for j in range(GROUP)]
        rows = [[ref[:, head_columns(h)] for ref in (q, k, v, grad)] for h in group]
        states = [[ref[head_rows(h), :] for ref in (s0, s1)] for h in group]
        weights = [[ref[head_rows(h, BLOCK), :] for ref in (w0, w1)] for h in group]
        inner = [
            [masked(gh[t], vh[t], (m0, m1)[n]) for n, t in BLOCKS] for _, _, vh, gh in rows
        ]
        outs = []
        for (qh, kh, _, gh), state, w, d in zip(rows, states, weights, inner):
            cut = gh * before[...]
            outs.append(
                [
                    (
                        dot(d[n], kh[t], 1, 0) + dot(cut[t], state[n], 1, 1),
                        dot(d[n], qh[t], 0, 0),
                        dot(w[n], gh[t], 0, 0),
                    )
                    for n, t in BLOCKS
                ]
            )
        for h, blocks in zip(group, outs):
            c = head_columns(h)
            for (n, t), (x, y, z) in zip(BLOCKS, blocks):
                dq[t, c] = x.astype(BF16)
                dk[t, c] = y
                dv[t, c] = z
        if flip:
            pl.when(g == 0)(first_copy.start)

    each_group(body)
    if flip:
        first_copy.wait()
        keep_copy.wait()


def local_grads(flip, q, k, v, g, states, weights, masks, before, after, dq_keep=()):
    near = [q, k, v, g, *states, *weights, *masks, before, after, *dq_keep]
    outs = [half_shape(BF16), half_shape(F32), half_shape(F32), TOKEN]
    return call(
        functools.partial(local_grads_kernel, flip), "local_grads", 5e9, near,
        [far()] * flip + outs, (), [pltpu.SemaphoreType.DMA((2,))] * flip,
    )


def gates_kernel(
    ids, keep, send, gi, w, rinv, gain, dq, _, dq_in, lo_far, gg_far, dq_far, token, lo, gg, sems,
    dq_sem
):
    token[...] = jnp.zeros_like(token)
    at = (GROUPS - 1) * SPAN
    copies = [store(dq, at, base_column(ids, 1) + at, dq_far, dq_sem)]
    copies[0].start()
    for flip, attn in enumerate((keep, send)):
        base = base_column(ids, flip)

        def body(g, flip=flip, attn=attn, base=base):
            for j in range(GROUP):
                h = g * GROUP + j
                far_c = span(base + h * HD, HD)
                out_c = head_columns(flip * HEADS + h)
                sig, other = sigmoid_parts(gi[:, far_c])
                scaled = attn[:, head_columns(h)] * rinv[...] * gain[:, far_c]
                lo[:, out_c] = (scaled * sig).astype(BF16)
                gg[:, out_c] = (scaled * w[:, far_c] * other).astype(BF16)
            at, to = flip * WIDE + g * SPAN, base + g * SPAN
            store(lo, at, to, lo_far, sems.at[0, flip, g]).start()
            store(gg, at, to, gg_far, sems.at[1, flip, g]).start()

        each_group(body)
        for g in range(GROUPS):
            at, to = flip * WIDE + g * SPAN, base + g * SPAN
            copies.append(store(lo, at, to, lo_far, sems.at[0, flip, g]))
            copies.append(store(gg, at, to, gg_far, sems.at[1, flip, g]))
    for copy in copies:
        copy.wait()


def gates(keep, send, gi, w, rinv, gain, dq, after, dq_far):
    near = [keep, send, gi, w, rinv, gain, dq, after]
    return call(
        gates_kernel, "gates", 3e9, near, [far(), far(), far(), TOKEN], [dq_far],
        [
            pltpu.VMEM((TOK, 2 * WIDE), BF16),
            pltpu.VMEM((TOK, 2 * WIDE), BF16),
            pltpu.SemaphoreType.DMA((2, 2, GROUPS)),
            pltpu.SemaphoreType.DMA,
        ],
        {len(near): 2},
    )


def finish_kernel(flip, ids, dk_in, dv_in, k, v, later, late, seg, after, *rest):
    if flip:
        total, _, _, dk_far, dv_far, gain_far, dk, dv, sems, gain, gain_sem = rest
        core = ids[0]
        at = [pl.ds(pl.multiple_of(n * 8, 8), 8) for n in (core, 1 - core)]
        gain[at[0], :] = joined_tile(total[...])
        gain[at[1], :] = joined_tile(later[STATE_ROWS : STATE_ROWS + TILE, :])
        gain_copy = pltpu.make_async_copy(gain, gain_far, gain_sem)
        gain_copy.start()
    else:
        dk_far, dv_far, dk, dv, sems = rest
    base = base_column(ids, flip)
    _, _, start1, end1 = split_ends(seg)
    join = flag(start1 == end1)
    copies = []
    for g in range(HEADS // FINE):
        group = range(g * FINE, (g + 1) * FINE)
        states = []
        for h in group:
            one = later[head_rows(h), :]
            states.append(
                ((late[head_rows(h), :] + one.astype(F32) * join).astype(BF16), one)
            )
        rows = [
            (k[:, head_columns(h)] * after[...], v[:, head_columns(h)] * after[...]) for h in group
        ]
        hops = [
            [(dot(vh[t], state[n], 1, 1), dot(kh[t], state[n], 1, 0)) for n, t in BLOCKS]
            for (kh, vh), state in zip(rows, states)
        ]
        sums = [
            [
                (dk_in[t, head_columns(h)] + hop[n][0], dv_in[t, head_columns(h)] + hop[n][1])
                for n, t in BLOCKS
            ]
            for h, hop in zip(group, hops)
        ]
        for h, blocks in zip(group, sums):
            for (_, t), (x, y) in zip(BLOCKS, blocks):
                dk[t, head_columns(h)] = x.astype(BF16)
                dv[t, head_columns(h)] = y.astype(BF16)
        for n, (ref, far_ref) in enumerate(((dk, dk_far), (dv, dv_far))):
            at = g * FINE_SPAN
            copy = store(ref, at, base + at, far_ref, sems.at[n, g], FINE_SPAN)
            copy.start()
            copies.append(copy)
    for copy in copies:
        copy.wait()
    if flip:
        gain_copy.wait()


def finish(flip, dk, dv, k, v, later, late, seg, after, total=(), done=()):
    near = [dk, dv, k, v, later, late, seg, after, *total]
    outs = [far(), far()]
    scratch = [
        pltpu.VMEM((TOK, WIDE), BF16),
        pltpu.VMEM((TOK, WIDE), BF16),
        pltpu.SemaphoreType.DMA((2, HEADS // FINE)),
    ]
    if flip:
        outs += [jax.ShapeDtypeStruct((TILE, HD), F32)]
        scratch += [pltpu.VMEM((TILE, HD), F32), pltpu.SemaphoreType.DMA]
    return call(
        functools.partial(finish_kernel, flip), "finish", 1.2e9, near, outs, done, scratch,
        {len(near): 0, len(near) + 1: 1} if flip else None,
    )


def place(ids, reverse):
    core, x, z = ids[0], ids[1], ids[2]
    return (1 - core, 3 - x, 3 - z) if reverse else (core, x, z)


def info_rows(ref, at):
    tile = ref[at : at + TILE, :].astype(F32)
    return tile[0:1], tile[8:9]


def sorted_cores(first_core, own, other):
    return jnp.where(first_core, own, other), jnp.where(first_core, other, own)


def quarter_rows(ids, m):
    return pl.ds(pl.multiple_of((ids[1] ^ m) * QUARTER, QUARTER), QUARTER)


def chip_kernel(reverse, gain, ids, own_ref, other_ref, *outs):
    vcore, _, _ = place(ids, reverse)
    first_core = vcore == 0
    low_own, high_own = info_rows(own_ref, STATE_ROWS)
    low_other, high_other = info_rows(other_ref, STATE_ROWS)
    low_a, _ = sorted_cores(first_core, low_own, low_other)
    high_a, high_b = sorted_cores(first_core, high_own, high_other)
    join = flag(high_a == high_b)
    own_weight = jnp.where(first_core, join, 1.0)
    other_weight = jnp.where(first_core, 1.0, join)
    for m, out in enumerate(outs):
        rows = quarter_rows(ids, m)
        total = own_ref[rows, :].astype(F32) * own_weight
        total = total + other_ref[rows, :].astype(F32) * other_weight
        out[0:QUARTER, :] = total.astype(BF16)
        out[QUARTER : QUARTER + TILE, :] = info_tile(low_a, high_b)
        if gain:
            at = slice(STATE_ROWS + TILE, STATE_ROWS + 2 * TILE)
            both = joined_tile(own_ref[at, :]) + joined_tile(other_ref[at, :])
            out[QUARTER + TILE : QUARTER + 2 * TILE, :] = split_tile(both)


def row_kernel(gain, ids, p0, p1, p2, p3, _, out):
    parts = (p0, p1, p2, p3)
    info = [info_rows(p, QUARTER) for p in parts]
    low = jnp.minimum(jnp.minimum(info[0][0], info[1][0]), jnp.minimum(info[2][0], info[3][0]))
    high = jnp.maximum(jnp.maximum(info[0][1], info[1][1]), jnp.maximum(info[2][1], info[3][1]))
    total = None
    for p, (_, own_high) in zip(parts, info):
        term = p[0:QUARTER, :].astype(F32) * flag(own_high == high)
        total = term if total is None else total + term
    out[0:QUARTER, :] = total.astype(BF16)
    out[QUARTER : QUARTER + TILE, :] = info_tile(low, high)
    if gain:
        g = [joined_tile(p[QUARTER + TILE : QUARTER + 2 * TILE, :]) for p in parts]
        out[QUARTER + TILE : QUARTER + 2 * TILE, :] = split_tile((g[0] + g[1]) + (g[2] + g[3]))


def entry_kernel(reverse, gain, ids, p0, p1, p2, p3, *rest):
    _, vx, vz = place(ids, reverse)
    parts = (p0, p1, p2, p3)
    outs = rest[-5 if gain else -4 :]
    if gain:
        rows = rest[1:4]
        earlier = [(vz ^ n) < vz for n in range(1, 4)]
    else:
        rows = rest[1:3]
        earlier = [vz >= 1, vz >= 2]
    info = [info_rows(p, QUARTER) for p in parts]
    row_high = [info_rows(t, QUARTER)[1] for t in rows]
    for m in range(4):
        low = info[m][0]
        total = jnp.zeros((QUARTER, HD), F32)
        for n in range(4):
            if n != m:
                weight = flag(info[n][1] == low) * flag((vx ^ n) < (vx ^ m))
                total = total + parts[n][0:QUARTER, :].astype(F32) * weight
        for row, high, before in zip(rows, row_high, earlier):
            weight = flag(high == low) * flag(before)
            total = total + row[0:QUARTER, :].astype(F32) * weight
        outs[m][...] = total.astype(BF16)
    if gain:
        g = [joined_tile(t[QUARTER + TILE : QUARTER + 2 * TILE, :]) for t in rest[0:4]]
        outs[4][...] = split_tile((g[0] + g[1]) + (g[2] + g[3]))


def device_kernel(reverse, gain, ids, own_ref, other_ref, e0, e1, e2, e3, _, *rest):
    keep, send = rest[-2:]
    vcore, _, _ = place(ids, reverse)
    first_core = vcore == 0
    low_own, high_own = info_rows(own_ref, STATE_ROWS)
    low_other, high_other = info_rows(other_ref, STATE_ROWS)
    low_a, low_b = sorted_cores(first_core, low_own, low_other)
    high_a, _ = sorted_cores(first_core, high_own, high_other)
    from_a = flag(high_a == low_b)
    from_chip = flag(low_a == low_b)
    for m, ref in enumerate((e0, e1, e2, e3)):
        rows = quarter_rows(ids, m)
        entry = ref[...].astype(F32)
        a = jnp.where(first_core, own_ref[rows, :].astype(F32), other_ref[rows, :].astype(F32))
        second = a * from_a + entry * from_chip
        keep[rows, :] = jnp.where(first_core, entry, second).astype(BF16)
        send[rows, :] = jnp.where(first_core, second, entry).astype(BF16)
    if gain:
        send[STATE_ROWS : STATE_ROWS + TILE, :] = rest[0][...]


def glue(kernel, name, rows, *args):
    return call(kernel, name, 5e8, args, [vmem((r, HD), BF16) for r in rows])


def swap(x, axis, size, bits):
    return lax.ppermute(x, axis, [(i, i ^ bits) for i in range(size)])


def chip_swap(x):
    return swap(x, "ctx", 32, 1)


def row_swap(x, m):
    return swap(x, "ctx", 32, m << 1)


def plane_swap(x, m):
    return swap(x, "ctx", 32, m << 3)


def plane_shift(x):
    return lax.ppermute(x, "ctx", [(i, (i + 8) % 32) for i in range(32)])


def scan(own, other, reverse, gain, beside_x, beside_z, beside_back):
    extra = TILE if gain else 0
    rows = QUARTER + TILE + extra
    sent = glue(
        functools.partial(chip_kernel, reverse, gain), "chip_sum", [rows] * 4, own, other
    )
    parts = [sent[0]] + [row_swap(sent[m], m) for m in range(1, 4)]
    token = beside_x(sent[0])
    total = glue(functools.partial(row_kernel, gain), "row_sum", [rows], *parts, token)[0]
    if gain:
        totals = [total] + [plane_swap(total, m) for m in range(1, 4)]
    else:
        totals = [total, plane_shift(total), plane_swap(total, 2)]
    token = beside_z(total)
    entries = glue(
        functools.partial(entry_kernel, reverse, gain),
        "entry",
        [QUARTER] * 4 + ([TILE] if gain else []),
        *parts,
        *totals,
        token,
    )
    tail = entries[4:]
    back = [entries[0]] + [row_swap(entries[m], m) for m in range(1, 4)]
    token = beside_back(entries[0])
    keep, send = glue(
        functools.partial(device_kernel, reverse, gain),
        "device_entry",
        [STATE_ROWS, STATE_ROWS + extra],
        own,
        other,
        *back,
        token,
        *tail,
    )
    return keep, chip_swap(send), tail


def on_device(query, keys, values, gate_input, grad_output, norm_gain, segment_ids):
    gain = norm_gain.reshape(1, -1)

    k_send, v_send, sent, early_send, seg, last = local_state(
        keys, values, segment_ids.reshape(1, TOK)
    )
    other = chip_swap(sent)
    k_keep, v_keep, own, early_keep = local_state(keys, values, None, seg, last)
    made = {}

    def intra_keep(token):
        made["keep"] = intra(k_keep, v_keep, query, token, seg=seg)
        return made["keep"][5]

    def intra_send(token):
        m0, m1, _, _, first = made["keep"][6:]
        made["send"] = intra(k_send, v_send, query, token, masks=(m0, m1, first))
        return made["send"][5]

    def prepare_both(token):
        made["gate"] = prepare(token, grad_output, gate_input)
        return made["gate"][2]

    state_keep, state_send, _ = scan(own, other, False, False, intra_keep, intra_send, prepare_both)
    q_keep, attn_keep, w0_keep, w1_keep, qt_keep, _, *masks, before, after, _ = made["keep"]
    q_send, attn_send, w0_send, w1_send, qt_send, _ = made["send"]
    gated, gate, _ = made["gate"]

    attn_keep, second_keep, *sums = cross(
        0, attn_keep, q_keep, state_keep, early_keep, gated, before, seg, gain
    )
    attn_send, second_send, sums = cross(
        1, attn_send, q_send, state_send, early_send, gated, before, seg, gain, sums
    )
    sums = [sums] + [swap(sums, "tp", 4, m) for m in range(1, 4)]

    g_send, sent, late_send, rinv, back = grad_attn(
        1, seg, attn_send, gated, qt_send, gain, sums
    )
    other = chip_swap(sent)
    g_keep, own, late_keep = grad_attn(0, seg, attn_keep, gated, qt_keep, gain, (rinv, back))

    def grads_keep(token):
        made["gk"] = local_grads(
            0, q_keep, k_keep, v_keep, g_keep, (state_keep, second_keep), (w0_keep, w1_keep),
            masks, before, token,
        )
        return made["gk"][3]

    def grads_send(token):
        made["gs"] = local_grads(
            1, q_send, k_send, v_send, g_send, (state_send, second_send), (w0_send, w1_send),
            masks, before, token, (made["gk"][0],),
        )
        return made["gs"][4]

    def gates_both(token):
        made["out"] = gates(
            attn_keep, attn_send, gate, gated, rinv, gain, made["gs"][1], token, made["gs"][0]
        )
        return made["out"][3]

    later_keep, later_send, total = scan(
        own, other, True, True, grads_keep, grads_send, gates_both
    )
    _, dk_keep, dv_keep, _ = made["gk"]
    _, _, dk_send, dv_send, _ = made["gs"]
    layer_out, grad_gate, grad_query, _ = made["out"]
    done = finish(0, dk_keep, dv_keep, k_keep, v_keep, later_keep, late_keep, seg, after)
    grad_keys, grad_values, grad_gain = finish(
        1, dk_send, dv_send, k_send, v_send, later_send, late_send, seg, after, (total[0],),
        tuple(done),
    )
    grad_gain = grad_gain.reshape(-1)
    return layer_out, grad_query, grad_keys, grad_values, grad_gate, grad_gain


def solution(mesh):
    in_specs = (P("ctx", "tp"),) * 5 + (P("tp"), P("ctx"))
    out_specs = (P("ctx", "tp"),) * 5 + (P("tp"),)
    return jax.shard_map(
        on_device, mesh=mesh, in_specs=in_specs, out_specs=out_specs, check_vma=False
    )
```

```python
import functools

import jax
import jax.numpy as jnp
from jax import lax
from jax.experimental import pallas as pl
from jax.experimental.pallas import tpu as pltpu
from jax.sharding import PartitionSpec as P

HD = 128
ATT = 8192
EPSILON = 1e-06
TOK = 512
BLOCK = 256
HEADS = 8
WIDE = HEADS * HD
GROUP = 4
GROUPS = HEADS // GROUP
SPAN = GROUP * HD
STATE_ROWS = HEADS * HD
QUARTER = 2 * HD
TILE = 16
F32 = jnp.float32
BF16 = jnp.bfloat16
VMEM_LIMIT = 16 * 1024 * 1024
VM = pl.BlockSpec(memory_space=pltpu.VMEM)
SM = pl.BlockSpec(memory_space=pltpu.SMEM)
ANY = pl.BlockSpec(memory_space=pl.ANY)


def dot(a, b, da, db):
    return lax.dot_general(a, b, (((da,), (db,)), ((), ())), preferred_element_type=F32)


def pair_diagonal(a, b, da, db):
    both = dot(a, b, da, db)
    return both[0:HD, 0:HD], both[HD : 2 * HD, HD : 2 * HD]


def diagonal(a, b):
    zero = jnp.zeros_like(a)
    return jnp.concatenate(
        [jnp.concatenate([a, zero], axis=1), jnp.concatenate([zero, b], axis=1)], axis=0
    )


def pair_columns(p):
    return pl.ds(pl.multiple_of(p * 2 * HD, 2 * HD), 2 * HD)


def vmem(shape, dtype):
    return pltpu.VMEM(shape, dtype)


def half_shape(dtype):
    return vmem((TOK, WIDE), dtype)


def far(dtype=BF16):
    return jax.ShapeDtypeStruct((TOK, 2 * WIDE), dtype)


def call(kernel, name, flops, near, outs, distant=(), scratch=(), aliases=None):
    near = [pltpu.with_memory_space_constraint(a, pltpu.VMEM) for a in near]
    distant = [pltpu.with_memory_space_constraint(a, pltpu.HBM) for a in distant]
    out_specs = [ANY if isinstance(o, jax.ShapeDtypeStruct) else VM for o in outs]

    def placed(*refs):
        where = lax.axis_index("ctx")
        kernel((where & 1, (where >> 1) & 3, where >> 3), *refs)

    return pl.pallas_call(
        placed,
        in_specs=[VM] * len(near) + [ANY] * len(distant),
        out_specs=out_specs,
        out_shape=list(outs),
        scratch_shapes=list(scratch),
        input_output_aliases=aliases or {},
        compiler_params=pltpu.CompilerParams(vmem_limit_bytes=VMEM_LIMIT),
        cost_estimate=pl.CostEstimate(
            flops=int(flops), bytes_accessed=int(flops / 300), transcendentals=0
        ),
        name=name,
    )(*near, *distant)


def base_column(ids, flip):
    return pl.multiple_of((ids[0] ^ flip) * WIDE, WIDE)


def head_columns(h):
    return pl.ds(pl.multiple_of(h * HD, HD), HD)


def head_rows(h, rows=HD):
    return pl.ds(pl.multiple_of(h * rows, rows), rows)


def span(start, width):
    return pl.ds(pl.multiple_of(start, width), width)


def store_half(source, base, target, sem):
    return pltpu.make_async_copy(source, target.at[:, span(base, WIDE)], sem)


def load(source, base, at, target, sem, width=SPAN):
    return pltpu.make_async_copy(
        source.at[:, span(base + at, width)], target.at[:, span(at, width)], sem
    )


def store(source, at, base, target, sem, width=SPAN):
    return pltpu.make_async_copy(
        source.at[:, span(at, width)], target.at[:, span(base, width)], sem
    )


def info_tile(low, high):
    row = lax.broadcasted_iota(jnp.int32, (TILE, HD), 0)
    return jnp.where(
        row < 8, jnp.broadcast_to(low, (TILE, HD)), jnp.broadcast_to(high, (TILE, HD))
    ).astype(BF16)


def split_tile(x):
    high = x.astype(BF16).astype(F32)
    return jnp.concatenate([high, x - high], axis=0).astype(BF16)


def joined_tile(tile):
    t = tile.astype(F32)
    return t[0:8] + t[8:16]


def split_ends(seg_ref):
    seg = seg_ref[...].astype(F32)
    return seg[:, 0:1], seg[:, BLOCK - 1 : BLOCK], seg[:, BLOCK : BLOCK + 1], seg[:, TOK - 1 : TOK]


def flag(cond):
    return jnp.where(cond, 1.0, 0.0)


def fill_last_mask(seg_ref, ref):
    seg = seg_ref[...].astype(F32)
    row = lax.broadcasted_iota(jnp.int32, (BLOCK, HD), 0).astype(F32)
    for _, t in BLOCKS:
        block = seg[:, t]
        same = jnp.sum(flag(block == block[:, BLOCK - 1 : BLOCK]), axis=1, keepdims=True)
        ref[t, :] = flag(row >= BLOCK - same).astype(BF16)


def fill_token_masks(seg_ref, col, before, after, first):
    start0, end0, start1, end1 = split_ends(seg_ref)
    wide = jnp.broadcast_to(col, (TOK, HD))
    for ref, ids in ((before, (start0, end0)), (after, (start1, end1)), (first, (start0, start1))):
        for n, t in BLOCKS:
            ref[t, :] = flag(wide[t] == ids[n]).astype(BF16)


BLOCKS = ((0, slice(0, BLOCK)), (1, slice(BLOCK, TOK)))
FINE = 2
FINE_SPAN = FINE * HD


def state_kernel(flip, ids, *refs):
    if flip:
        k_far, v_far, seg_far, k, v, out, early, seg, last, sems, seg_sem = refs
    else:
        seg, last, k_far, v_far, k, v, out, early, sems = refs
    base = base_column(ids, flip)
    copies = [
        [
            pltpu.make_async_copy(far_ref.at[t, span(base, WIDE)], ref.at[t, :], sems.at[m, n])
            for m, (far_ref, ref) in enumerate(((k_far, k), (v_far, v)))
        ]
        for n, t in BLOCKS
    ]
    for pair in copies:
        for c in pair:
            c.start()
    if flip:
        copy = pltpu.make_async_copy(seg_far, seg, seg_sem)
        copy.start()
        copy.wait()
        fill_last_mask(seg, last)
    start0, end0, _, end1 = split_ends(seg)
    join = flag(end0 == end1)
    out[STATE_ROWS : STATE_ROWS + TILE, :] = info_tile(start0, end1)
    for n, t in BLOCKS:
        for c in copies[n]:
            c.wait()
        mask = jnp.concatenate([last[t, :]] * 2, axis=1)
        rows = [
            (k[t, pair_columns(p)] * mask, v[t, pair_columns(p)]) for p in range(HEADS // 2)
        ]
        parts = [part for kp, vp in rows for part in pair_diagonal(kp, vp, 0, 0)]
        if n == 1:
            parts = [two + early[head_rows(h), :] * join for h, two in enumerate(parts)]
        for h, part in enumerate(parts):
            if n == 0:
                early[head_rows(h), :] = part
            else:
                out[head_rows(h), :] = part.astype(BF16)


def local_state(k, v, seg, seg_vmem=None, last=None):
    flip = seg_vmem is None
    outs = [
        half_shape(BF16), half_shape(BF16), vmem((STATE_ROWS + TILE, HD), BF16),
        vmem((STATE_ROWS, HD), F32),
    ]
    scratch = [pltpu.SemaphoreType.DMA((2, 2))]
    near, distant = [seg_vmem, last], [k, v]
    if flip:
        outs += [vmem((1, TOK), jnp.int32), vmem((TOK, HD), BF16)]
        scratch += [pltpu.SemaphoreType.DMA]
        near, distant = [], [k, v, seg]
    return call(
        functools.partial(state_kernel, int(flip)), "local_state", 1e9, near, outs, distant, scratch
    )


def fill_masks(seg_ref, m0, m1, *masks):
    seg = seg_ref[...].astype(F32)
    col = jnp.transpose(jnp.broadcast_to(seg, (8, TOK)))[:, 0:1]
    fill_token_masks(seg_ref, col, *masks)
    t = lax.broadcasted_iota(jnp.int32, (BLOCK, BLOCK), 0)
    s = lax.broadcasted_iota(jnp.int32, (BLOCK, BLOCK), 1)
    for start, ref in ((0, m0), (BLOCK, m1)):
        same = col[start : start + BLOCK] == seg[:, start : start + BLOCK]
        ref[...] = flag(same & (s <= t)).astype(BF16)


def masked(left, right, mask):
    return dot(left, right, 1, 1).astype(BF16) * mask[...]


def intra_kernel(flip, ids, *refs):
    if flip:
        k, v, m0, m1, first, _, q_far, q, attn, w0, w1, qt, token, sems = refs
    else:
        k, v, seg, _, q_far, q, attn, w0, w1, qt, token, m0, m1, before, after, first, sems = refs
    base = base_column(ids, flip)
    for g in range(GROUPS):
        load(q_far, base, g * SPAN, q, sems.at[g]).start()
    if not flip:
        fill_masks(seg, m0, m1, before, after, first)
    token[...] = jnp.zeros_like(token)

    def body(g):
        load(q_far, base, g * SPAN, q, sems.at[g]).wait()
        group = [g * GROUP + j for j in range(GROUP)]
        rows = [[ref[:, head_columns(h)] for ref in (q, k, v)] for h in group]
        flipped = [jnp.transpose(qh * first[...]) for qh, _, _ in rows]
        weights = [[masked(qh[t], kh[t], (m0, m1)[n]) for n, t in BLOCKS] for qh, kh, _ in rows]
        sums = [
            [dot(w[n], vh[t], 1, 0) for n, t in BLOCKS] for w, (_, _, vh) in zip(weights, rows)
        ]
        for h, turned, w, a in zip(group, flipped, weights, sums):
            qt[head_rows(h), :] = turned
            for n, t in BLOCKS:
                (w0, w1)[n][head_rows(h, BLOCK), :] = w[n]
                attn[t, head_columns(h)] = a[n]

    for g in range(GROUPS):
        body(g)


TOKEN = vmem((8, HD), F32)


def intra(k, v, q, after, seg=None, masks=None):
    outs = [
        half_shape(BF16),
        half_shape(F32),
        vmem((HEADS * BLOCK, BLOCK), BF16),
        vmem((HEADS * BLOCK, BLOCK), BF16),
        vmem((STATE_ROWS, TOK), BF16),
        TOKEN,
    ]
    if masks is None:
        near = [k, v, seg, after]
        outs += [vmem((BLOCK, BLOCK), BF16)] * 2 + [vmem((TOK, HD), BF16)] * 3
    else:
        near = [k, v, *masks, after]
    return call(
        functools.partial(intra_kernel, int(masks is not None)), "intra", 3e9, near, outs, [q],
        [pltpu.SemaphoreType.DMA((GROUPS,))],
    )


def sigmoid_parts(gi):
    bend = 0.5 * jnp.tanh(0.5 * gi.astype(F32))
    return 0.5 + bend, 0.5 - bend


def prepare_kernel(ids, _, go_far, gi_far, w, gi, token, go, sems):
    pairs = ((go_far, go), (gi_far, gi))
    for g in range(2 * GROUPS):
        for n, (far_ref, ref) in enumerate(pairs):
            load(far_ref, 0, g * SPAN, ref, sems.at[n, g]).start()
    token[...] = jnp.zeros_like(token)

    def body(g):
        for n, (far_ref, ref) in enumerate(pairs):
            load(far_ref, 0, g * SPAN, ref, sems.at[n, g]).wait()
        for j in range(GROUP):
            c = head_columns(g * GROUP + j)
            w[:, c] = go[:, c].astype(F32) * sigmoid_parts(gi[:, c])[0]

    for g in range(2 * GROUPS):
        body(g)


def prepare(after, go, gi):
    return call(
        prepare_kernel, "prepare", 3e9, [after],
        [vmem((TOK, 2 * WIDE), F32), vmem((TOK, 2 * WIDE), BF16), TOKEN], [go, gi],
        [pltpu.VMEM((TOK, 2 * WIDE), BF16), pltpu.SemaphoreType.DMA((2, 2 * GROUPS))],
    )


def cross_kernel(flip, ids, attn_in, q, s, early, w, before, seg, gain, *rest):
    if flip:
        squares_in, inners_in, attn, second, sums, squares, inners = rest
        squares[...] = squares_in[...]
        inners[...] = inners_in[...]
    else:
        attn, second, squares, inners = rest
        squares[...] = jnp.zeros_like(squares)
        inners[...] = jnp.zeros_like(inners)
    base = base_column(ids, flip)
    start0, end0, _, _ = split_ends(seg)
    join = flag(start0 == end0)

    def body(g):
        group = [g * GROUP + j for j in range(GROUP)]
        ones = [s[head_rows(h), :] for h in group]
        twos = [
            (early[head_rows(h), :] + one.astype(F32) * join).astype(BF16)
            for h, one in zip(group, ones)
        ]
        mask = jnp.concatenate([before[...]] * 2, axis=1)
        rows = [q[:, pair_columns(g * (GROUP // 2) + j)] * mask for j in range(GROUP // 2)]
        for n, t in BLOCKS:
            states = (ones, twos)[n]
            hops = []
            for j, qp in enumerate(rows):
                hop = dot(qp[t], diagonal(states[2 * j], states[2 * j + 1]), 1, 0)
                hops += [hop[:, 0:HD], hop[:, HD : 2 * HD]]
            sums = [attn_in[t, head_columns(h)] + hop for h, hop in zip(group, hops)]
            square, inner = squares[t, :], inners[t, :]
            for h, a in zip(group, sums):
                far_c = span(base + h * HD, HD)
                square = square + a * a
                inner = inner + w[t, far_c] * a * gain[:, far_c]
            squares[t, :] = square
            inners[t, :] = inner
            for h, a in zip(group, sums):
                attn[t, head_columns(h)] = a
        for h, two in zip(group, twos):
            second[head_rows(h), :] = two

    for g in range(GROUPS):
        body(g)
    if flip:
        ones = jnp.ones((8, HD), BF16)
        totals = []
        for x in (squares[...], inners[...]):
            high = x.astype(BF16)
            low = (x - high.astype(F32)).astype(BF16)
            totals.append(dot(ones, high, 1, 1) + dot(ones, low, 1, 1))
        row = lax.broadcasted_iota(jnp.int32, (8, TOK), 0)
        sums[...] = jnp.where(row < 4, totals[0], totals[1])


def cross(flip, attn, q, state, early, w, before, seg, gain, previous=()):
    total = vmem((TOK, HD), F32)
    outs = [half_shape(F32), vmem((STATE_ROWS, HD), BF16)]
    return call(
        functools.partial(cross_kernel, flip), "cross", 1.2e9,
        [attn, q, state, early, w, before, seg, gain, *previous],
        outs + ([vmem((8, TOK), F32)] if flip else [total, total]), (),
        [pltpu.VMEM((TOK, HD), F32)] * 2 if flip else [],
    )


def scales(sums, rinv_ref, back_ref):
    own, one, two, three = [r[...] for r in sums]
    total = (own + one) + (two + three)
    rinv = lax.rsqrt(total[0:1] * (1.0 / ATT) + EPSILON)
    back = rinv * rinv * rinv * total[4:5] * (1.0 / ATT)
    row = lax.broadcasted_iota(jnp.int32, (8, TOK), 0)
    both = jnp.where(
        row < 4, jnp.broadcast_to(rinv, (8, TOK)), jnp.broadcast_to(back, (8, TOK))
    )
    cols = jnp.transpose(both)
    rinv_ref[...] = jnp.broadcast_to(cols[:, 0:1], (TOK, HD))
    back_ref[...] = jnp.broadcast_to(cols[:, 4:5], (TOK, HD))


def grad_kernel(flip, ids, seg, attn, w, qt, gain, *rest):
    if flip:
        s0, s1, s2, s3, grad, out, late, rinv, back, gains = rest
        scales((s0, s1, s2, s3), rinv, back)
    else:
        rinv, back, grad, out, late, gains = rest
    base = base_column(ids, flip)
    start0, _, start1, end1 = split_ends(seg)
    join = flag(start0 == start1)
    out[STATE_ROWS : STATE_ROWS + TILE, :] = info_tile(8.0 - end1, 8.0 - start0)

    def body(g):
        group = [g * GROUP + j for j in range(GROUP)]
        turned = [qt[head_rows(g * (GROUP // 2) + j, 2 * HD), :] for j in range(GROUP // 2)]
        totals, rows = [], []
        for h in group:
            far_c = span(base + h * HD, HD)
            a = attn[:, head_columns(h)]
            gated = w[:, far_c] * rinv[...]
            totals.append(jnp.sum(gated * a, axis=0, keepdims=True))
            rows.append((gated * gain[:, far_c] - a * back[...]).astype(BF16))
        parts = []
        for j, qp in enumerate(turned):
            xp = jnp.concatenate(rows[2 * j : 2 * j + 2], axis=1)
            parts += zip(*[pair_diagonal(qp[:, t], xp[t], 1, 0) for _, t in BLOCKS])
        for h, total, x, (one, two) in zip(group, totals, rows, parts):
            gains[pl.ds(h, 1), :] = total
            grad[:, head_columns(h)] = x
            late[head_rows(h), :] = two
            out[head_rows(h), :] = (one + two * join).astype(BF16)

    for g in range(GROUPS):
        body(g)
    out[STATE_ROWS + TILE : STATE_ROWS + 2 * TILE, :] = split_tile(gains[...])


def grad_attn(flip, seg, attn, w, qt, gain, extra):
    outs = [
        half_shape(BF16), vmem((STATE_ROWS + 2 * TILE, HD), BF16), vmem((STATE_ROWS, HD), F32)
    ]
    if flip:
        outs += [vmem((TOK, HD), F32), vmem((TOK, HD), F32)]
    return call(
        functools.partial(grad_kernel, flip), "grad_attn", 1.2e9,
        [seg, attn, w, qt, gain, *extra], outs, (), [pltpu.VMEM((8, HD), F32)],
    )


def local_grads_kernel(flip, ids, q, k, v, grad, s0, s1, w0, w1, m0, m1, before, _, *rest):
    if flip:
        dq_keep, dq_far, dq, dk, dv, token, sems = rest
        keep_copy = store_half(dq_keep, base_column(ids, 0), dq_far, sems.at[1])
        keep_copy.start()
        first_copy = store(dq, 0, base_column(ids, 1), dq_far, sems.at[0])
    else:
        dq, dk, dv, token = rest
    token[...] = jnp.zeros_like(token)

    def body(g):
        group = [g * GROUP + j for j in range(GROUP)]
        rows = [[ref[:, head_columns(h)] for ref in (q, k, v, grad)] for h in group]
        states = [[ref[head_rows(h), :] for ref in (s0, s1)] for h in group]
        weights = [[ref[head_rows(h, BLOCK), :] for ref in (w0, w1)] for h in group]
        inner = [
            [masked(gh[t], vh[t], (m0, m1)[n]) for n, t in BLOCKS] for _, _, vh, gh in rows
        ]
        outs = []
        for (qh, kh, _, gh), state, w, d in zip(rows, states, weights, inner):
            cut = gh * before[...]
            outs.append(
                [
                    (
                        dot(d[n], kh[t], 1, 0) + dot(cut[t], state[n], 1, 1),
                        dot(d[n], qh[t], 0, 0),
                        dot(w[n], gh[t], 0, 0),
                    )
                    for n, t in BLOCKS
                ]
            )
        for h, blocks in zip(group, outs):
            c = head_columns(h)
            for (n, t), (x, y, z) in zip(BLOCKS, blocks):
                dq[t, c] = x.astype(BF16)
                dk[t, c] = y
                dv[t, c] = z
        if flip and g == 0:
            first_copy.start()

    for g in range(GROUPS):
        body(g)
    if flip:
        first_copy.wait()
        keep_copy.wait()


def local_grads(flip, q, k, v, g, states, weights, masks, before, after, dq_keep=()):
    near = [q, k, v, g, *states, *weights, *masks, before, after, *dq_keep]
    outs = [half_shape(BF16), half_shape(F32), half_shape(F32), TOKEN]
    return call(
        functools.partial(local_grads_kernel, flip), "local_grads", 5e9, near,
        [far()] * flip + outs, (), [pltpu.SemaphoreType.DMA((2,))] * flip,
    )


def gates_kernel(
    ids, keep, send, gi, w, rinv, gain, dq, _, dq_in, lo_far, gg_far, dq_far, token, lo, gg, sems,
    dq_sem
):
    token[...] = jnp.zeros_like(token)
    at = (GROUPS - 1) * SPAN
    copies = [store(dq, at, base_column(ids, 1) + at, dq_far, dq_sem)]
    copies[0].start()
    for flip, attn in enumerate((keep, send)):
        base = base_column(ids, flip)

        def body(g, flip=flip, attn=attn, base=base):
            for j in range(GROUP):
                h = g * GROUP + j
                far_c = span(base + h * HD, HD)
                out_c = head_columns(flip * HEADS + h)
                sig, other = sigmoid_parts(gi[:, far_c])
                scaled = attn[:, head_columns(h)] * rinv[...] * gain[:, far_c]
                lo[:, out_c] = (scaled * sig).astype(BF16)
                gg[:, out_c] = (scaled * w[:, far_c] * other).astype(BF16)
            at, to = flip * WIDE + g * SPAN, base + g * SPAN
            store(lo, at, to, lo_far, sems.at[0, flip, g]).start()
            store(gg, at, to, gg_far, sems.at[1, flip, g]).start()

        for g in range(GROUPS):
            body(g)
        for g in range(GROUPS):
            at, to = flip * WIDE + g * SPAN, base + g * SPAN
            copies.append(store(lo, at, to, lo_far, sems.at[0, flip, g]))
            copies.append(store(gg, at, to, gg_far, sems.at[1, flip, g]))
    for copy in copies:
        copy.wait()


def gates(keep, send, gi, w, rinv, gain, dq, after, dq_far):
    near = [keep, send, gi, w, rinv, gain, dq, after]
    return call(
        gates_kernel, "gates", 3e9, near, [far(), far(), far(), TOKEN], [dq_far],
        [
            pltpu.VMEM((TOK, 2 * WIDE), BF16),
            pltpu.VMEM((TOK, 2 * WIDE), BF16),
            pltpu.SemaphoreType.DMA((2, 2, GROUPS)),
            pltpu.SemaphoreType.DMA,
        ],
        {len(near): 2},
    )


def finish_kernel(flip, ids, dk_in, dv_in, k, v, later, late, seg, after, *rest):
    if flip:
        total, _, _, dk_far, dv_far, gain_far, dk, dv, sems, gain, gain_sem = rest
        core = ids[0]
        at = [pl.ds(pl.multiple_of(n * 8, 8), 8) for n in (core, 1 - core)]
        gain[at[0], :] = joined_tile(total[...])
        gain[at[1], :] = joined_tile(later[STATE_ROWS : STATE_ROWS + TILE, :])
        gain_copy = pltpu.make_async_copy(gain, gain_far, gain_sem)
        gain_copy.start()
    else:
        dk_far, dv_far, dk, dv, sems = rest
    base = base_column(ids, flip)
    _, _, start1, end1 = split_ends(seg)
    join = flag(start1 == end1)
    copies = []
    for g in range(HEADS // FINE):
        group = range(g * FINE, (g + 1) * FINE)
        states = []
        for h in group:
            one = later[head_rows(h), :]
            states.append(
                ((late[head_rows(h), :] + one.astype(F32) * join).astype(BF16), one)
            )
        mask = jnp.concatenate([after[...]] * 2, axis=1)
        kp, vp = k[:, pair_columns(g)] * mask, v[:, pair_columns(g)] * mask
        hops = ([], [])
        for n, t in BLOCKS:
            both = diagonal(states[0][n], states[1][n])
            x, y = dot(vp[t], both, 1, 1), dot(kp[t], both, 1, 0)
            hops[0].append((x[:, 0:HD], y[:, 0:HD]))
            hops[1].append((x[:, HD : 2 * HD], y[:, HD : 2 * HD]))
        sums = [
            [
                (dk_in[t, head_columns(h)] + hop[n][0], dv_in[t, head_columns(h)] + hop[n][1])
                for n, t in BLOCKS
            ]
            for h, hop in zip(group, hops)
        ]
        for h, blocks in zip(group, sums):
            for (_, t), (x, y) in zip(BLOCKS, blocks):
                dk[t, head_columns(h)] = x.astype(BF16)
                dv[t, head_columns(h)] = y.astype(BF16)
        for n, (ref, far_ref) in enumerate(((dk, dk_far), (dv, dv_far))):
            at = g * FINE_SPAN
            copy = store(ref, at, base + at, far_ref, sems.at[n, g], FINE_SPAN)
            copy.start()
            copies.append(copy)
    for copy in copies:
        copy.wait()
    if flip:
        gain_copy.wait()


def finish(flip, dk, dv, k, v, later, late, seg, after, total=(), done=()):
    near = [dk, dv, k, v, later, late, seg, after, *total]
    outs = [far(), far()]
    scratch = [
        pltpu.VMEM((TOK, WIDE), BF16),
        pltpu.VMEM((TOK, WIDE), BF16),
        pltpu.SemaphoreType.DMA((2, HEADS // FINE)),
    ]
    if flip:
        outs += [jax.ShapeDtypeStruct((TILE, HD), F32)]
        scratch += [pltpu.VMEM((TILE, HD), F32), pltpu.SemaphoreType.DMA]
    return call(
        functools.partial(finish_kernel, flip), "finish", 1.2e9, near, outs, done, scratch,
        {len(near): 0, len(near) + 1: 1} if flip else None,
    )


def place(ids, reverse):
    core, x, z = ids[0], ids[1], ids[2]
    return (1 - core, 3 - x, 3 - z) if reverse else (core, x, z)


def info_rows(ref, at):
    tile = ref[at : at + TILE, :].astype(F32)
    return tile[0:1], tile[8:9]


def sorted_cores(first_core, own, other):
    return jnp.where(first_core, own, other), jnp.where(first_core, other, own)


def quarter_rows(ids, m):
    return pl.ds(pl.multiple_of((ids[1] ^ m) * QUARTER, QUARTER), QUARTER)


def chip_kernel(reverse, gain, ids, own_ref, other_ref, *outs):
    vcore, _, _ = place(ids, reverse)
    first_core = vcore == 0
    low_own, high_own = info_rows(own_ref, STATE_ROWS)
    low_other, high_other = info_rows(other_ref, STATE_ROWS)
    low_a, _ = sorted_cores(first_core, low_own, low_other)
    high_a, high_b = sorted_cores(first_core, high_own, high_other)
    join = flag(high_a == high_b)
    own_weight = jnp.where(first_core, join, 1.0)
    other_weight = jnp.where(first_core, 1.0, join)
    for m, out in enumerate(outs):
        rows = quarter_rows(ids, m)
        total = own_ref[rows, :].astype(F32) * own_weight
        total = total + other_ref[rows, :].astype(F32) * other_weight
        out[0:QUARTER, :] = total.astype(BF16)
        out[QUARTER : QUARTER + TILE, :] = info_tile(low_a, high_b)
        if gain:
            at = slice(STATE_ROWS + TILE, STATE_ROWS + 2 * TILE)
            both = joined_tile(own_ref[at, :]) + joined_tile(other_ref[at, :])
            out[QUARTER + TILE : QUARTER + 2 * TILE, :] = split_tile(both)


def row_kernel(gain, ids, p0, p1, p2, p3, _, out):
    parts = (p0, p1, p2, p3)
    info = [info_rows(p, QUARTER) for p in parts]
    low = jnp.minimum(jnp.minimum(info[0][0], info[1][0]), jnp.minimum(info[2][0], info[3][0]))
    high = jnp.maximum(jnp.maximum(info[0][1], info[1][1]), jnp.maximum(info[2][1], info[3][1]))
    total = None
    for p, (_, own_high) in zip(parts, info):
        term = p[0:QUARTER, :].astype(F32) * flag(own_high == high)
        total = term if total is None else total + term
    out[0:QUARTER, :] = total.astype(BF16)
    out[QUARTER : QUARTER + TILE, :] = info_tile(low, high)
    if gain:
        g = [joined_tile(p[QUARTER + TILE : QUARTER + 2 * TILE, :]) for p in parts]
        out[QUARTER + TILE : QUARTER + 2 * TILE, :] = split_tile((g[0] + g[1]) + (g[2] + g[3]))


def entry_kernel(reverse, gain, ids, p0, p1, p2, p3, *rest):
    _, vx, vz = place(ids, reverse)
    parts = (p0, p1, p2, p3)
    outs = rest[-5 if gain else -4 :]
    if gain:
        rows = rest[1:4]
        earlier = [(vz ^ n) < vz for n in range(1, 4)]
    else:
        rows = rest[1:3]
        earlier = [vz >= 1, vz >= 2]
    info = [info_rows(p, QUARTER) for p in parts]
    row_high = [info_rows(t, QUARTER)[1] for t in rows]
    for m in range(4):
        low = info[m][0]
        total = jnp.zeros((QUARTER, HD), F32)
        for n in range(4):
            if n != m:
                weight = flag(info[n][1] == low) * flag((vx ^ n) < (vx ^ m))
                total = total + parts[n][0:QUARTER, :].astype(F32) * weight
        for row, high, before in zip(rows, row_high, earlier):
            weight = flag(high == low) * flag(before)
            total = total + row[0:QUARTER, :].astype(F32) * weight
        outs[m][...] = total.astype(BF16)
    if gain:
        g = [joined_tile(t[QUARTER + TILE : QUARTER + 2 * TILE, :]) for t in rest[0:4]]
        outs[4][...] = split_tile((g[0] + g[1]) + (g[2] + g[3]))


def device_kernel(reverse, gain, ids, own_ref, other_ref, e0, e1, e2, e3, _, *rest):
    keep, send = rest[-2:]
    vcore, _, _ = place(ids, reverse)
    first_core = vcore == 0
    low_own, high_own = info_rows(own_ref, STATE_ROWS)
    low_other, high_other = info_rows(other_ref, STATE_ROWS)
    low_a, low_b = sorted_cores(first_core, low_own, low_other)
    high_a, _ = sorted_cores(first_core, high_own, high_other)
    from_a = flag(high_a == low_b)
    from_chip = flag(low_a == low_b)
    for m, ref in enumerate((e0, e1, e2, e3)):
        rows = quarter_rows(ids, m)
        entry = ref[...].astype(F32)
        a = jnp.where(first_core, own_ref[rows, :].astype(F32), other_ref[rows, :].astype(F32))
        second = a * from_a + entry * from_chip
        keep[rows, :] = jnp.where(first_core, entry, second).astype(BF16)
        send[rows, :] = jnp.where(first_core, second, entry).astype(BF16)
    if gain:
        send[STATE_ROWS : STATE_ROWS + TILE, :] = rest[0][...]


def glue(kernel, name, rows, *args):
    return call(kernel, name, 5e8, args, [vmem((r, HD), BF16) for r in rows])


def swap(x, axis, size, bits):
    return lax.ppermute(x, axis, [(i, i ^ bits) for i in range(size)])


def chip_swap(x):
    return swap(x, "ctx", 32, 1)


def row_swap(x, m):
    return swap(x, "ctx", 32, m << 1)


def plane_swap(x, m):
    return swap(x, "ctx", 32, m << 3)


def plane_shift(x):
    return lax.ppermute(x, "ctx", [(i, (i + 8) % 32) for i in range(32)])


def scan(own, other, reverse, gain, beside_x, beside_z, beside_back):
    extra = TILE if gain else 0
    rows = QUARTER + TILE + extra
    sent = glue(
        functools.partial(chip_kernel, reverse, gain), "chip_sum", [rows] * 4, own, other
    )
    parts = [sent[0]] + [row_swap(sent[m], m) for m in range(1, 4)]
    token = beside_x(sent[0])
    total = glue(functools.partial(row_kernel, gain), "row_sum", [rows], *parts, token)[0]
    if gain:
        totals = [total] + [plane_swap(total, m) for m in range(1, 4)]
    else:
        totals = [total, plane_shift(total), plane_swap(total, 2)]
    token = beside_z(total)
    entries = glue(
        functools.partial(entry_kernel, reverse, gain),
        "entry",
        [QUARTER] * 4 + ([TILE] if gain else []),
        *parts,
        *totals,
        token,
    )
    tail = entries[4:]
    back = [entries[0]] + [row_swap(entries[m], m) for m in range(1, 4)]
    token = beside_back(entries[0])
    keep, send = glue(
        functools.partial(device_kernel, reverse, gain),
        "device_entry",
        [STATE_ROWS, STATE_ROWS + extra],
        own,
        other,
        *back,
        token,
        *tail,
    )
    return keep, chip_swap(send), tail


def on_device(query, keys, values, gate_input, grad_output, norm_gain, segment_ids):
    gain = norm_gain.reshape(1, -1)

    k_send, v_send, sent, early_send, seg, last = local_state(
        keys, values, segment_ids.reshape(1, TOK)
    )
    other = chip_swap(sent)
    k_keep, v_keep, own, early_keep = local_state(keys, values, None, seg, last)
    made = {}

    def intra_keep(token):
        made["keep"] = intra(k_keep, v_keep, query, token, seg=seg)
        return made["keep"][5]

    def intra_send(token):
        m0, m1, _, _, first = made["keep"][6:]
        made["send"] = intra(k_send, v_send, query, token, masks=(m0, m1, first))
        return made["send"][5]

    def prepare_both(token):
        made["gate"] = prepare(token, grad_output, gate_input)
        return made["gate"][2]

    state_keep, state_send, _ = scan(own, other, False, False, intra_keep, intra_send, prepare_both)
    q_keep, attn_keep, w0_keep, w1_keep, qt_keep, _, *masks, before, after, _ = made["keep"]
    q_send, attn_send, w0_send, w1_send, qt_send, _ = made["send"]
    gated, gate, _ = made["gate"]

    attn_keep, second_keep, *sums = cross(
        0, attn_keep, q_keep, state_keep, early_keep, gated, before, seg, gain
    )
    attn_send, second_send, sums = cross(
        1, attn_send, q_send, state_send, early_send, gated, before, seg, gain, sums
    )
    sums = [sums] + [swap(sums, "tp", 4, m) for m in range(1, 4)]

    g_send, sent, late_send, rinv, back = grad_attn(
        1, seg, attn_send, gated, qt_send, gain, sums
    )
    other = chip_swap(sent)
    g_keep, own, late_keep = grad_attn(0, seg, attn_keep, gated, qt_keep, gain, (rinv, back))

    def grads_keep(token):
        made["gk"] = local_grads(
            0, q_keep, k_keep, v_keep, g_keep, (state_keep, second_keep), (w0_keep, w1_keep),
            masks, before, token,
        )
        return made["gk"][3]

    def grads_send(token):
        made["gs"] = local_grads(
            1, q_send, k_send, v_send, g_send, (state_send, second_send), (w0_send, w1_send),
            masks, before, token, (made["gk"][0],),
        )
        return made["gs"][4]

    def gates_both(token):
        made["out"] = gates(
            attn_keep, attn_send, gate, gated, rinv, gain, made["gs"][1], token, made["gs"][0]
        )
        return made["out"][3]

    later_keep, later_send, total = scan(
        own, other, True, True, grads_keep, grads_send, gates_both
    )
    _, dk_keep, dv_keep, _ = made["gk"]
    _, _, dk_send, dv_send, _ = made["gs"]
    layer_out, grad_gate, grad_query, _ = made["out"]
    done = finish(0, dk_keep, dv_keep, k_keep, v_keep, later_keep, late_keep, seg, after)
    grad_keys, grad_values, grad_gain = finish(
        1, dk_send, dv_send, k_send, v_send, later_send, late_send, seg, after, (total[0],),
        tuple(done),
    )
    grad_gain = grad_gain.reshape(-1)
    return layer_out, grad_query, grad_keys, grad_values, grad_gate, grad_gain


def solution(mesh):
    in_specs = (P("ctx", "tp"),) * 5 + (P("tp"), P("ctx"))
    out_specs = (P("ctx", "tp"),) * 5 + (P("tp"),)
    return jax.shard_map(
        on_device, mesh=mesh, in_specs=in_specs, out_specs=out_specs, check_vma=False
    )
```

```python
import functools

import jax
import jax.numpy as jnp
from jax import lax
from jax.experimental import pallas as pl
from jax.experimental.pallas import tpu as pltpu
from jax.sharding import PartitionSpec as P

HD = 128
ATT = 8192
EPSILON = 1e-06
TOK = 512
BLOCK = 256
HEADS = 8
WIDE = HEADS * HD
GROUP = 4
GROUPS = HEADS // GROUP
SPAN = GROUP * HD
STATE_ROWS = HEADS * HD
QUARTER = 2 * HD
TILE = 16
F32 = jnp.float32
BF16 = jnp.bfloat16
VMEM_LIMIT = 16 * 1024 * 1024
VM = pl.BlockSpec(memory_space=pltpu.VMEM)
SM = pl.BlockSpec(memory_space=pltpu.SMEM)
ANY = pl.BlockSpec(memory_space=pl.ANY)


def dot(a, b, da, db):
    return lax.dot_general(a, b, (((da,), (db,)), ((), ())), preferred_element_type=F32)


def pair_diagonal(a, b, da, db):
    both = dot(a, b, da, db)
    return both[0:HD, 0:HD], both[HD : 2 * HD, HD : 2 * HD]


def diagonal(a, b):
    zero = jnp.zeros_like(a)
    return jnp.concatenate(
        [jnp.concatenate([a, zero], axis=1), jnp.concatenate([zero, b], axis=1)], axis=0
    )


def pair_columns(p):
    return pl.ds(pl.multiple_of(p * 2 * HD, 2 * HD), 2 * HD)


def vmem(shape, dtype):
    return pltpu.VMEM(shape, dtype)


def half_shape(dtype):
    return vmem((TOK, WIDE), dtype)


def far(dtype=BF16):
    return jax.ShapeDtypeStruct((TOK, 2 * WIDE), dtype)


def call(kernel, name, flops, near, outs, distant=(), scratch=(), aliases=None):
    near = [pltpu.with_memory_space_constraint(a, pltpu.VMEM) for a in near]
    distant = [pltpu.with_memory_space_constraint(a, pltpu.HBM) for a in distant]
    out_specs = [ANY if isinstance(o, jax.ShapeDtypeStruct) else VM for o in outs]

    def placed(*refs):
        where = lax.axis_index("ctx")
        kernel((where & 1, (where >> 1) & 3, where >> 3), *refs)

    return pl.pallas_call(
        placed,
        in_specs=[VM] * len(near) + [ANY] * len(distant),
        out_specs=out_specs,
        out_shape=list(outs),
        scratch_shapes=list(scratch),
        input_output_aliases=aliases or {},
        compiler_params=pltpu.CompilerParams(vmem_limit_bytes=VMEM_LIMIT),
        cost_estimate=pl.CostEstimate(
            flops=int(flops), bytes_accessed=int(flops / 300), transcendentals=0
        ),
        name=name,
    )(*near, *distant)


def base_column(ids, flip):
    return pl.multiple_of((ids[0] ^ flip) * WIDE, WIDE)


def head_columns(h):
    return pl.ds(pl.multiple_of(h * HD, HD), HD)


def head_rows(h, rows=HD):
    return pl.ds(pl.multiple_of(h * rows, rows), rows)


def span(start, width):
    return pl.ds(pl.multiple_of(start, width), width)


def store_half(source, base, target, sem):
    return pltpu.make_async_copy(source, target.at[:, span(base, WIDE)], sem)


def load(source, base, at, target, sem, width=SPAN):
    return pltpu.make_async_copy(
        source.at[:, span(base + at, width)], target.at[:, span(at, width)], sem
    )


def store(source, at, base, target, sem, width=SPAN):
    return pltpu.make_async_copy(
        source.at[:, span(at, width)], target.at[:, span(base, width)], sem
    )


def info_tile(low, high):
    row = lax.broadcasted_iota(jnp.int32, (TILE, HD), 0)
    return jnp.where(
        row < 8, jnp.broadcast_to(low, (TILE, HD)), jnp.broadcast_to(high, (TILE, HD))
    ).astype(BF16)


def split_tile(x):
    high = x.astype(BF16).astype(F32)
    return jnp.concatenate([high, x - high], axis=0).astype(BF16)


def joined_tile(tile):
    t = tile.astype(F32)
    return t[0:8] + t[8:16]


def split_ends(seg_ref):
    seg = seg_ref[...].astype(F32)
    return seg[:, 0:1], seg[:, BLOCK - 1 : BLOCK], seg[:, BLOCK : BLOCK + 1], seg[:, TOK - 1 : TOK]


def flag(cond):
    return jnp.where(cond, 1.0, 0.0)


def fill_last_mask(seg_ref, ref):
    seg = seg_ref[...].astype(F32)
    row = lax.broadcasted_iota(jnp.int32, (BLOCK, HD), 0).astype(F32)
    for _, t in BLOCKS:
        block = seg[:, t]
        same = jnp.sum(flag(block == block[:, BLOCK - 1 : BLOCK]), axis=1, keepdims=True)
        ref[t, :] = flag(row >= BLOCK - same).astype(BF16)


def fill_token_masks(seg_ref, col, before, after, first):
    start0, end0, start1, end1 = split_ends(seg_ref)
    wide = jnp.broadcast_to(col, (TOK, HD))
    for ref, ids in ((before, (start0, end0)), (after, (start1, end1)), (first, (start0, start1))):
        for n, t in BLOCKS:
            ref[t, :] = flag(wide[t] == ids[n]).astype(BF16)


BLOCKS = ((0, slice(0, BLOCK)), (1, slice(BLOCK, TOK)))
FINE = 2
FINE_SPAN = FINE * HD


def state_kernel(flip, ids, *refs):
    if flip:
        k_far, v_far, seg_far, k, v, out, early, seg, last, sems, seg_sem = refs
    else:
        seg, last, k_far, v_far, k, v, out, early, sems = refs
    base = base_column(ids, flip)
    copies = [
        [
            pltpu.make_async_copy(far_ref.at[t, span(base, WIDE)], ref.at[t, :], sems.at[m, n])
            for m, (far_ref, ref) in enumerate(((k_far, k), (v_far, v)))
        ]
        for n, t in BLOCKS
    ]
    for pair in copies:
        for c in pair:
            c.start()
    if flip:
        copy = pltpu.make_async_copy(seg_far, seg, seg_sem)
        copy.start()
        copy.wait()
        fill_last_mask(seg, last)
    start0, end0, _, end1 = split_ends(seg)
    join = flag(end0 == end1)
    out[STATE_ROWS : STATE_ROWS + TILE, :] = info_tile(start0, end1)
    for n, t in BLOCKS:
        for c in copies[n]:
            c.wait()
        mask = jnp.concatenate([last[t, :]] * 2, axis=1)
        rows = [
            (k[t, pair_columns(p)] * mask, v[t, pair_columns(p)]) for p in range(HEADS // 2)
        ]
        parts = [part for kp, vp in rows for part in pair_diagonal(kp, vp, 0, 0)]
        if n == 1:
            parts = [two + early[head_rows(h), :] * join for h, two in enumerate(parts)]
        for h, part in enumerate(parts):
            if n == 0:
                early[head_rows(h), :] = part
            else:
                out[head_rows(h), :] = part.astype(BF16)


def local_state(k, v, seg, seg_vmem=None, last=None):
    flip = seg_vmem is None
    outs = [
        half_shape(BF16), half_shape(BF16), vmem((STATE_ROWS + TILE, HD), BF16),
        vmem((STATE_ROWS, HD), F32),
    ]
    scratch = [pltpu.SemaphoreType.DMA((2, 2))]
    near, distant = [seg_vmem, last], [k, v]
    if flip:
        outs += [vmem((1, TOK), jnp.int32), vmem((TOK, HD), BF16)]
        scratch += [pltpu.SemaphoreType.DMA]
        near, distant = [], [k, v, seg]
    return call(
        functools.partial(state_kernel, int(flip)), "local_state", 1e9, near, outs, distant, scratch
    )


def fill_masks(seg_ref, m0, m1, *masks):
    seg = seg_ref[...].astype(F32)
    col = jnp.transpose(jnp.broadcast_to(seg, (8, TOK)))[:, 0:1]
    fill_token_masks(seg_ref, col, *masks)
    t = lax.broadcasted_iota(jnp.int32, (BLOCK, BLOCK), 0)
    s = lax.broadcasted_iota(jnp.int32, (BLOCK, BLOCK), 1)
    for start, ref in ((0, m0), (BLOCK, m1)):
        same = col[start : start + BLOCK] == seg[:, start : start + BLOCK]
        ref[...] = flag(same & (s <= t)).astype(BF16)


def masked(left, right, mask):
    return dot(left, right, 1, 1).astype(BF16) * mask[...]


def intra_kernel(flip, ids, *refs):
    if flip:
        k, v, m0, m1, first, _, q_far, q, attn, w0, w1, qt, token, sems = refs
    else:
        k, v, seg, _, q_far, q, attn, w0, w1, qt, token, m0, m1, before, after, first, sems = refs
    base = base_column(ids, flip)
    for g in range(GROUPS):
        load(q_far, base, g * SPAN, q, sems.at[g]).start()
    if not flip:
        fill_masks(seg, m0, m1, before, after, first)
    token[...] = jnp.zeros_like(token)

    def body(g):
        load(q_far, base, g * SPAN, q, sems.at[g]).wait()
        group = [g * GROUP + j for j in range(GROUP)]
        rows = [[ref[:, head_columns(h)] for ref in (q, k, v)] for h in group]
        flipped = [jnp.transpose(qh * first[...]) for qh, _, _ in rows]
        weights = [[masked(qh[t], kh[t], (m0, m1)[n]) for n, t in BLOCKS] for qh, kh, _ in rows]
        sums = [
            [dot(w[n], vh[t], 1, 0) for n, t in BLOCKS] for w, (_, _, vh) in zip(weights, rows)
        ]
        for h, turned, w, a in zip(group, flipped, weights, sums):
            qt[head_rows(h), :] = turned
            for n, t in BLOCKS:
                (w0, w1)[n][head_rows(h, BLOCK), :] = w[n]
                attn[t, head_columns(h)] = a[n]

    for g in range(GROUPS):
        body(g)


TOKEN = vmem((8, HD), F32)


def intra(k, v, q, after, seg=None, masks=None):
    outs = [
        half_shape(BF16),
        half_shape(F32),
        vmem((HEADS * BLOCK, BLOCK), BF16),
        vmem((HEADS * BLOCK, BLOCK), BF16),
        vmem((STATE_ROWS, TOK), BF16),
        TOKEN,
    ]
    if masks is None:
        near = [k, v, seg, after]
        outs += [vmem((BLOCK, BLOCK), BF16)] * 2 + [vmem((TOK, HD), BF16)] * 3
    else:
        near = [k, v, *masks, after]
    return call(
        functools.partial(intra_kernel, int(masks is not None)), "intra", 3e9, near, outs, [q],
        [pltpu.SemaphoreType.DMA((GROUPS,))],
    )


def sigmoid_parts(gi):
    bend = 0.5 * jnp.tanh(0.5 * gi.astype(F32))
    return 0.5 + bend, 0.5 - bend


def prepare_kernel(ids, _, go_far, gi_far, w, gi, token, go, sems):
    pairs = ((go_far, go), (gi_far, gi))
    for g in range(2 * GROUPS):
        for n, (far_ref, ref) in enumerate(pairs):
            load(far_ref, 0, g * SPAN, ref, sems.at[n, g]).start()
    token[...] = jnp.zeros_like(token)

    def body(g):
        for n, (far_ref, ref) in enumerate(pairs):
            load(far_ref, 0, g * SPAN, ref, sems.at[n, g]).wait()
        for j in range(GROUP):
            c = head_columns(g * GROUP + j)
            w[:, c] = go[:, c].astype(F32) * sigmoid_parts(gi[:, c])[0]

    for g in range(2 * GROUPS):
        body(g)


def prepare(after, go, gi):
    return call(
        prepare_kernel, "prepare", 3e9, [after],
        [vmem((TOK, 2 * WIDE), F32), vmem((TOK, 2 * WIDE), BF16), TOKEN], [go, gi],
        [pltpu.VMEM((TOK, 2 * WIDE), BF16), pltpu.SemaphoreType.DMA((2, 2 * GROUPS))],
    )


def cross_kernel(flip, ids, attn_in, q, s, early, w, before, seg, gain, *rest):
    if flip:
        squares_in, inners_in, attn, second, sums, squares, inners = rest
        squares[...] = squares_in[...]
        inners[...] = inners_in[...]
    else:
        attn, second, squares, inners = rest
        squares[...] = jnp.zeros_like(squares)
        inners[...] = jnp.zeros_like(inners)
    base = base_column(ids, flip)
    start0, end0, _, _ = split_ends(seg)
    join = flag(start0 == end0)

    def body(g):
        group = [g * GROUP + j for j in range(GROUP)]
        ones = [s[head_rows(h), :] for h in group]
        twos = [
            (early[head_rows(h), :] + one.astype(F32) * join).astype(BF16)
            for h, one in zip(group, ones)
        ]
        mask = jnp.concatenate([before[...]] * 2, axis=1)
        rows = [q[:, pair_columns(g * (GROUP // 2) + j)] * mask for j in range(GROUP // 2)]
        for n, t in BLOCKS:
            states = (ones, twos)[n]
            hops = []
            for j, qp in enumerate(rows):
                hop = dot(qp[t], diagonal(states[2 * j], states[2 * j + 1]), 1, 0)
                hops += [hop[:, 0:HD], hop[:, HD : 2 * HD]]
            sums = [attn_in[t, head_columns(h)] + hop for h, hop in zip(group, hops)]
            square, inner = squares[t, :], inners[t, :]
            for h, a in zip(group, sums):
                far_c = span(base + h * HD, HD)
                square = square + a * a
                inner = inner + w[t, far_c] * a * gain[:, far_c]
            squares[t, :] = square
            inners[t, :] = inner
            for h, a in zip(group, sums):
                attn[t, head_columns(h)] = a
        for h, two in zip(group, twos):
            second[head_rows(h), :] = two

    for g in range(GROUPS):
        body(g)
    if flip:
        ones = jnp.ones((8, HD), BF16)
        totals = []
        for x in (squares[...], inners[...]):
            high = x.astype(BF16)
            low = (x - high.astype(F32)).astype(BF16)
            totals.append(dot(ones, high, 1, 1) + dot(ones, low, 1, 1))
        row = lax.broadcasted_iota(jnp.int32, (8, HD), 0)
        for n in range(8):
            total = totals[n // 4][:, (n % 4) * HD : (n % 4 + 1) * HD]
            packed = total if n == 0 else jnp.where(row == n, total, packed)
        sums[...] = packed


def cross(flip, attn, q, state, early, w, before, seg, gain, previous=()):
    total = vmem((TOK, HD), F32)
    outs = [half_shape(F32), vmem((STATE_ROWS, HD), BF16)]
    return call(
        functools.partial(cross_kernel, flip), "cross", 1.2e9,
        [attn, q, state, early, w, before, seg, gain, *previous],
        outs + ([vmem((8, HD), F32)] if flip else [total, total]), (),
        [pltpu.VMEM((TOK, HD), F32)] * 2 if flip else [],
    )


def scales(sums, rinv_ref, back_ref):
    own, two, one, three = [r[...] for r in sums]
    total = (own + one) + (two + three)
    rinv = lax.rsqrt(total[0:4] * (1.0 / ATT) + EPSILON)
    back = rinv * rinv * rinv * total[4:8] * (1.0 / ATT)
    cols = jnp.transpose(jnp.concatenate([rinv, back], axis=0))
    for n in range(4):
        rinv_ref[n * HD : (n + 1) * HD, :] = jnp.broadcast_to(cols[:, n : n + 1], (HD, HD))
        back_ref[n * HD : (n + 1) * HD, :] = jnp.broadcast_to(cols[:, n + 4 : n + 5], (HD, HD))


def grad_kernel(flip, ids, seg, attn, w, qt, gain, *rest):
    if flip:
        s0, s1, s2, s3, grad, out, late, rinv, back, gains = rest
        scales((s0, s1, s2, s3), rinv, back)
    else:
        rinv, back, grad, out, late, gains = rest
    base = base_column(ids, flip)
    start0, _, start1, end1 = split_ends(seg)
    join = flag(start0 == start1)
    out[STATE_ROWS : STATE_ROWS + TILE, :] = info_tile(8.0 - end1, 8.0 - start0)

    def body(g):
        group = [g * GROUP + j for j in range(GROUP)]
        turned = [qt[head_rows(g * (GROUP // 2) + j, 2 * HD), :] for j in range(GROUP // 2)]
        totals, rows = [], []
        for h in group:
            far_c = span(base + h * HD, HD)
            a = attn[:, head_columns(h)]
            gated = w[:, far_c] * rinv[...]
            totals.append(jnp.sum(gated * a, axis=0, keepdims=True))
            rows.append((gated * gain[:, far_c] - a * back[...]).astype(BF16))
        parts = []
        for j, qp in enumerate(turned):
            xp = jnp.concatenate(rows[2 * j : 2 * j + 2], axis=1)
            parts += zip(*[pair_diagonal(qp[:, t], xp[t], 1, 0) for _, t in BLOCKS])
        for h, total, x, (one, two) in zip(group, totals, rows, parts):
            gains[pl.ds(h, 1), :] = total
            grad[:, head_columns(h)] = x
            late[head_rows(h), :] = two
            out[head_rows(h), :] = (one + two * join).astype(BF16)

    for g in range(GROUPS):
        body(g)
    out[STATE_ROWS + TILE : STATE_ROWS + 2 * TILE, :] = split_tile(gains[...])


def grad_attn(flip, seg, attn, w, qt, gain, extra):
    outs = [
        half_shape(BF16), vmem((STATE_ROWS + 2 * TILE, HD), BF16), vmem((STATE_ROWS, HD), F32)
    ]
    if flip:
        outs += [vmem((TOK, HD), F32), vmem((TOK, HD), F32)]
    return call(
        functools.partial(grad_kernel, flip), "grad_attn", 1.2e9,
        [seg, attn, w, qt, gain, *extra], outs, (), [pltpu.VMEM((8, HD), F32)],
    )


def local_grads_kernel(flip, ids, q, k, v, grad, s0, s1, w0, w1, m0, m1, before, _, *rest):
    if flip:
        dq_keep, dq_far, dq, dk, dv, token, sems = rest
        keep_copy = store_half(dq_keep, base_column(ids, 0), dq_far, sems.at[1])
        keep_copy.start()
        first_copy = store(dq, 0, base_column(ids, 1), dq_far, sems.at[0])
    else:
        dq, dk, dv, token = rest
    token[...] = jnp.zeros_like(token)

    def body(g):
        group = [g * GROUP + j for j in range(GROUP)]
        rows = [[ref[:, head_columns(h)] for ref in (q, k, v, grad)] for h in group]
        states = [[ref[head_rows(h), :] for ref in (s0, s1)] for h in group]
        weights = [[ref[head_rows(h, BLOCK), :] for ref in (w0, w1)] for h in group]
        inner = [
            [masked(gh[t], vh[t], (m0, m1)[n]) for n, t in BLOCKS] for _, _, vh, gh in rows
        ]
        outs = []
        for (qh, kh, _, gh), state, w, d in zip(rows, states, weights, inner):
            cut = gh * before[...]
            outs.append(
                [
                    (
                        dot(d[n], kh[t], 1, 0) + dot(cut[t], state[n], 1, 1),
                        dot(d[n], qh[t], 0, 0),
                        dot(w[n], gh[t], 0, 0),
                    )
                    for n, t in BLOCKS
                ]
            )
        for h, blocks in zip(group, outs):
            c = head_columns(h)
            for (n, t), (x, y, z) in zip(BLOCKS, blocks):
                dq[t, c] = x.astype(BF16)
                dk[t, c] = y
                dv[t, c] = z
        if flip and g == 0:
            first_copy.start()

    for g in range(GROUPS):
        body(g)
    if flip:
        first_copy.wait()
        keep_copy.wait()


def local_grads(flip, q, k, v, g, states, weights, masks, before, after, dq_keep=()):
    near = [q, k, v, g, *states, *weights, *masks, before, after, *dq_keep]
    outs = [half_shape(BF16), half_shape(F32), half_shape(F32), TOKEN]
    return call(
        functools.partial(local_grads_kernel, flip), "local_grads", 5e9, near,
        [far()] * flip + outs, (), [pltpu.SemaphoreType.DMA((2,))] * flip,
    )


def gates_kernel(
    ids, keep, send, gi, w, rinv, gain, dq, _, dq_in, lo_far, gg_far, dq_far, token, lo, gg, sems,
    dq_sem
):
    token[...] = jnp.zeros_like(token)
    at = (GROUPS - 1) * SPAN
    copies = [store(dq, at, base_column(ids, 1) + at, dq_far, dq_sem)]
    copies[0].start()
    for flip, attn in enumerate((keep, send)):
        base = base_column(ids, flip)

        def body(g, flip=flip, attn=attn, base=base):
            for j in range(GROUP):
                h = g * GROUP + j
                far_c = span(base + h * HD, HD)
                out_c = head_columns(flip * HEADS + h)
                sig, other = sigmoid_parts(gi[:, far_c])
                scaled = attn[:, head_columns(h)] * rinv[...] * gain[:, far_c]
                lo[:, out_c] = (scaled * sig).astype(BF16)
                gg[:, out_c] = (scaled * w[:, far_c] * other).astype(BF16)
            at, to = flip * WIDE + g * SPAN, base + g * SPAN
            store(lo, at, to, lo_far, sems.at[0, flip, g]).start()
            store(gg, at, to, gg_far, sems.at[1, flip, g]).start()

        for g in range(GROUPS):
            body(g)
        for g in range(GROUPS):
            at, to = flip * WIDE + g * SPAN, base + g * SPAN
            copies.append(store(lo, at, to, lo_far, sems.at[0, flip, g]))
            copies.append(store(gg, at, to, gg_far, sems.at[1, flip, g]))
    for copy in copies:
        copy.wait()


def gates(keep, send, gi, w, rinv, gain, dq, after, dq_far):
    near = [keep, send, gi, w, rinv, gain, dq, after]
    return call(
        gates_kernel, "gates", 3e9, near, [far(), far(), far(), TOKEN], [dq_far],
        [
            pltpu.VMEM((TOK, 2 * WIDE), BF16),
            pltpu.VMEM((TOK, 2 * WIDE), BF16),
            pltpu.SemaphoreType.DMA((2, 2, GROUPS)),
            pltpu.SemaphoreType.DMA,
        ],
        {len(near): 2},
    )


def finish_kernel(flip, ids, dk_in, dv_in, k, v, later, late, seg, after, *rest):
    if flip:
        total, _, _, dk_far, dv_far, gain_far, dk, dv, sems, gain, gain_sem = rest
        core = ids[0]
        at = [pl.ds(pl.multiple_of(n * 8, 8), 8) for n in (core, 1 - core)]
        gain[at[0], :] = joined_tile(total[...])
        gain[at[1], :] = joined_tile(later[STATE_ROWS : STATE_ROWS + TILE, :])
        gain_copy = pltpu.make_async_copy(gain, gain_far, gain_sem)
        gain_copy.start()
    else:
        dk_far, dv_far, dk, dv, sems = rest
    base = base_column(ids, flip)
    _, _, start1, end1 = split_ends(seg)
    join = flag(start1 == end1)
    copies = []
    for g in range(HEADS // FINE):
        group = range(g * FINE, (g + 1) * FINE)
        states = []
        for h in group:
            one = later[head_rows(h), :]
            states.append(
                ((late[head_rows(h), :] + one.astype(F32) * join).astype(BF16), one)
            )
        mask = jnp.concatenate([after[...]] * 2, axis=1)
        kp, vp = k[:, pair_columns(g)] * mask, v[:, pair_columns(g)] * mask
        hops = ([], [])
        for n, t in BLOCKS:
            both = diagonal(states[0][n], states[1][n])
            x, y = dot(vp[t], both, 1, 1), dot(kp[t], both, 1, 0)
            hops[0].append((x[:, 0:HD], y[:, 0:HD]))
            hops[1].append((x[:, HD : 2 * HD], y[:, HD : 2 * HD]))
        sums = [
            [
                (dk_in[t, head_columns(h)] + hop[n][0], dv_in[t, head_columns(h)] + hop[n][1])
                for n, t in BLOCKS
            ]
            for h, hop in zip(group, hops)
        ]
        for h, blocks in zip(group, sums):
            for (_, t), (x, y) in zip(BLOCKS, blocks):
                dk[t, head_columns(h)] = x.astype(BF16)
                dv[t, head_columns(h)] = y.astype(BF16)
        for n, (ref, far_ref) in enumerate(((dk, dk_far), (dv, dv_far))):
            at = g * FINE_SPAN
            copy = store(ref, at, base + at, far_ref, sems.at[n, g], FINE_SPAN)
            copy.start()
            copies.append(copy)
    for copy in copies:
        copy.wait()
    if flip:
        gain_copy.wait()


def finish(flip, dk, dv, k, v, later, late, seg, after, total=(), done=()):
    near = [dk, dv, k, v, later, late, seg, after, *total]
    outs = [far(), far()]
    scratch = [
        pltpu.VMEM((TOK, WIDE), BF16),
        pltpu.VMEM((TOK, WIDE), BF16),
        pltpu.SemaphoreType.DMA((2, HEADS // FINE)),
    ]
    if flip:
        outs += [jax.ShapeDtypeStruct((TILE, HD), F32)]
        scratch += [pltpu.VMEM((TILE, HD), F32), pltpu.SemaphoreType.DMA]
    return call(
        functools.partial(finish_kernel, flip), "finish", 1.2e9, near, outs, done, scratch,
        {len(near): 0, len(near) + 1: 1} if flip else None,
    )


def place(ids, reverse):
    core, x, z = ids[0], ids[1], ids[2]
    return (1 - core, 3 - x, 3 - z) if reverse else (core, x, z)


def info_rows(ref, at):
    tile = ref[at : at + TILE, :].astype(F32)
    return tile[0:1], tile[8:9]


def sorted_cores(first_core, own, other):
    return jnp.where(first_core, own, other), jnp.where(first_core, other, own)


def quarter_rows(ids, m):
    return pl.ds(pl.multiple_of((ids[1] ^ m) * QUARTER, QUARTER), QUARTER)


def chip_kernel(reverse, gain, ids, own_ref, other_ref, *outs):
    vcore, _, _ = place(ids, reverse)
    first_core = vcore == 0
    low_own, high_own = info_rows(own_ref, STATE_ROWS)
    low_other, high_other = info_rows(other_ref, STATE_ROWS)
    low_a, _ = sorted_cores(first_core, low_own, low_other)
    high_a, high_b = sorted_cores(first_core, high_own, high_other)
    join = flag(high_a == high_b)
    own_weight = jnp.where(first_core, join, 1.0)
    other_weight = jnp.where(first_core, 1.0, join)
    for m, out in enumerate(outs):
        rows = quarter_rows(ids, m)
        total = own_ref[rows, :].astype(F32) * own_weight
        total = total + other_ref[rows, :].astype(F32) * other_weight
        out[0:QUARTER, :] = total.astype(BF16)
        out[QUARTER : QUARTER + TILE, :] = info_tile(low_a, high_b)
        if gain:
            at = slice(STATE_ROWS + TILE, STATE_ROWS + 2 * TILE)
            both = joined_tile(own_ref[at, :]) + joined_tile(other_ref[at, :])
            out[QUARTER + TILE : QUARTER + 2 * TILE, :] = split_tile(both)


def row_kernel(gain, ids, p0, p2, p1, p3, _, out):
    parts = (p0, p1, p2, p3)
    info = [info_rows(p, QUARTER) for p in parts]
    low = jnp.minimum(jnp.minimum(info[0][0], info[1][0]), jnp.minimum(info[2][0], info[3][0]))
    high = jnp.maximum(jnp.maximum(info[0][1], info[1][1]), jnp.maximum(info[2][1], info[3][1]))
    total = None
    for p, (_, own_high) in zip(parts, info):
        term = p[0:QUARTER, :].astype(F32) * flag(own_high == high)
        total = term if total is None else total + term
    out[0:QUARTER, :] = total.astype(BF16)
    out[QUARTER : QUARTER + TILE, :] = info_tile(low, high)
    if gain:
        g = [joined_tile(p[QUARTER + TILE : QUARTER + 2 * TILE, :]) for p in parts]
        out[QUARTER + TILE : QUARTER + 2 * TILE, :] = split_tile((g[0] + g[1]) + (g[2] + g[3]))


def entry_kernel(reverse, gain, ids, p0, p2, p1, p3, *rest):
    _, vx, vz = place(ids, reverse)
    parts = (p0, p1, p2, p3)
    outs = rest[-5 if gain else -4 :]
    if gain:
        rows = rest[1:4]
        earlier = [(vz ^ n) < vz for n in FAR_FIRST[1:]]
    else:
        rows = rest[1:3]
        earlier = [vz >= 2, vz >= 1]
    info = [info_rows(p, QUARTER) for p in parts]
    row_high = [info_rows(t, QUARTER)[1] for t in rows]
    for m in range(4):
        low = info[m][0]
        total = jnp.zeros((QUARTER, HD), F32)
        for n in range(4):
            if n != m:
                weight = flag(info[n][1] == low) * flag((vx ^ n) < (vx ^ m))
                total = total + parts[n][0:QUARTER, :].astype(F32) * weight
        for row, high, before in zip(rows, row_high, earlier):
            weight = flag(high == low) * flag(before)
            total = total + row[0:QUARTER, :].astype(F32) * weight
        outs[m][...] = total.astype(BF16)
    if gain:
        tiles = [joined_tile(t[QUARTER + TILE : QUARTER + 2 * TILE, :]) for t in rest[0:4]]
        g = [tiles[m] for m in FAR_FIRST]
        outs[4][...] = split_tile((g[0] + g[1]) + (g[2] + g[3]))


def device_kernel(reverse, gain, ids, own_ref, other_ref, e0, e2, e1, e3, _, *rest):
    keep, send = rest[-2:]
    vcore, _, _ = place(ids, reverse)
    first_core = vcore == 0
    low_own, high_own = info_rows(own_ref, STATE_ROWS)
    low_other, high_other = info_rows(other_ref, STATE_ROWS)
    low_a, low_b = sorted_cores(first_core, low_own, low_other)
    high_a, _ = sorted_cores(first_core, high_own, high_other)
    from_a = flag(high_a == low_b)
    from_chip = flag(low_a == low_b)
    for m, ref in enumerate((e0, e1, e2, e3)):
        rows = quarter_rows(ids, m)
        entry = ref[...].astype(F32)
        a = jnp.where(first_core, own_ref[rows, :].astype(F32), other_ref[rows, :].astype(F32))
        second = a * from_a + entry * from_chip
        keep[rows, :] = jnp.where(first_core, entry, second).astype(BF16)
        send[rows, :] = jnp.where(first_core, second, entry).astype(BF16)
    if gain:
        send[STATE_ROWS : STATE_ROWS + TILE, :] = rest[0][...]


def glue(kernel, name, rows, *args):
    return call(kernel, name, 5e8, args, [vmem((r, HD), BF16) for r in rows])


def swap(x, axis, size, bits):
    return lax.ppermute(x, axis, [(i, i ^ bits) for i in range(size)])


FAR_FIRST = (0, 2, 1, 3)


def swap_all(arrays, send):
    return [arrays[0]] + [send(arrays[m], m) for m in FAR_FIRST[1:]]


def chip_swap(x):
    return swap(x, "ctx", 32, 1)


def row_swap(x, m):
    return swap(x, "ctx", 32, m << 1)


def plane_swap(x, m):
    return swap(x, "ctx", 32, m << 3)


def plane_shift(x):
    return lax.ppermute(x, "ctx", [(i, (i + 8) % 32) for i in range(32)])


def scan(own, other, reverse, gain, beside_x, beside_z, beside_back):
    extra = TILE if gain else 0
    rows = QUARTER + TILE + extra
    sent = glue(
        functools.partial(chip_kernel, reverse, gain), "chip_sum", [rows] * 4, own, other
    )
    parts = swap_all(sent, row_swap)
    token = beside_x(sent[0])
    total = glue(functools.partial(row_kernel, gain), "row_sum", [rows], *parts, token)[0]
    if gain:
        totals = swap_all([total] * 4, plane_swap)
    else:
        second = plane_swap(total, 2)
        totals = [total, second, plane_shift(total)]
    token = beside_z(total)
    entries = glue(
        functools.partial(entry_kernel, reverse, gain),
        "entry",
        [QUARTER] * 4 + ([TILE] if gain else []),
        *parts,
        *totals,
        token,
    )
    tail = entries[4:]
    back = swap_all(entries, row_swap)
    token = beside_back(entries[0])
    keep, send = glue(
        functools.partial(device_kernel, reverse, gain),
        "device_entry",
        [STATE_ROWS, STATE_ROWS + extra],
        own,
        other,
        *back,
        token,
        *tail,
    )
    return keep, chip_swap(send), tail


def on_device(query, keys, values, gate_input, grad_output, norm_gain, segment_ids):
    gain = norm_gain.reshape(1, -1)

    k_send, v_send, sent, early_send, seg, last = local_state(
        keys, values, segment_ids.reshape(1, TOK)
    )
    other = chip_swap(sent)
    k_keep, v_keep, own, early_keep = local_state(keys, values, None, seg, last)
    made = {}

    def intra_keep(token):
        made["keep"] = intra(k_keep, v_keep, query, token, seg=seg)
        return made["keep"][5]

    def intra_send(token):
        m0, m1, _, _, first = made["keep"][6:]
        made["send"] = intra(k_send, v_send, query, token, masks=(m0, m1, first))
        return made["send"][5]

    def prepare_both(token):
        made["gate"] = prepare(token, grad_output, gate_input)
        return made["gate"][2]

    state_keep, state_send, _ = scan(own, other, False, False, intra_keep, intra_send, prepare_both)
    q_keep, attn_keep, w0_keep, w1_keep, qt_keep, _, *masks, before, after, _ = made["keep"]
    q_send, attn_send, w0_send, w1_send, qt_send, _ = made["send"]
    gated, gate, _ = made["gate"]

    attn_keep, second_keep, *sums = cross(
        0, attn_keep, q_keep, state_keep, early_keep, gated, before, seg, gain
    )
    attn_send, second_send, sums = cross(
        1, attn_send, q_send, state_send, early_send, gated, before, seg, gain, sums
    )
    sums = swap_all([sums] * 4, lambda x, m: swap(x, "tp", 4, m))

    g_send, sent, late_send, rinv, back = grad_attn(
        1, seg, attn_send, gated, qt_send, gain, sums
    )
    other = chip_swap(sent)
    g_keep, own, late_keep = grad_attn(0, seg, attn_keep, gated, qt_keep, gain, (rinv, back))

    def grads_keep(token):
        made["gk"] = local_grads(
            0, q_keep, k_keep, v_keep, g_keep, (state_keep, second_keep), (w0_keep, w1_keep),
            masks, before, token,
        )
        return made["gk"][3]

    def grads_send(token):
        made["gs"] = local_grads(
            1, q_send, k_send, v_send, g_send, (state_send, second_send), (w0_send, w1_send),
            masks, before, token, (made["gk"][0],),
        )
        return made["gs"][4]

    def gates_both(token):
        made["out"] = gates(
            attn_keep, attn_send, gate, gated, rinv, gain, made["gs"][1], token, made["gs"][0]
        )
        return made["out"][3]

    later_keep, later_send, total = scan(
        own, other, True, True, grads_keep, grads_send, gates_both
    )
    _, dk_keep, dv_keep, _ = made["gk"]
    _, _, dk_send, dv_send, _ = made["gs"]
    layer_out, grad_gate, grad_query, _ = made["out"]
    done = finish(0, dk_keep, dv_keep, k_keep, v_keep, later_keep, late_keep, seg, after)
    grad_keys, grad_values, grad_gain = finish(
        1, dk_send, dv_send, k_send, v_send, later_send, late_send, seg, after, (total[0],),
        tuple(done),
    )
    grad_gain = grad_gain.reshape(-1)
    return layer_out, grad_query, grad_keys, grad_values, grad_gate, grad_gain


def solution(mesh):
    in_specs = (P("ctx", "tp"),) * 5 + (P("tp"), P("ctx"))
    out_specs = (P("ctx", "tp"),) * 5 + (P("tp"),)
    return jax.shard_map(
        on_device, mesh=mesh, in_specs=in_specs, out_specs=out_specs, check_vma=False
    )
```

```python
import functools

import jax
import jax.numpy as jnp
from jax import lax
from jax.experimental import pallas as pl
from jax.experimental.pallas import tpu as pltpu
from jax.sharding import PartitionSpec as P

HD = 128
ATT = 8192
EPSILON = 1e-06
TOK = 512
BLOCK = 256
HEADS = 8
WIDE = HEADS * HD
GROUP = 4
GROUPS = HEADS // GROUP
SPAN = GROUP * HD
STATE_ROWS = HEADS * HD
QUARTER = 2 * HD
TILE = 16
F32 = jnp.float32
BF16 = jnp.bfloat16
VMEM_LIMIT = 16 * 1024 * 1024
VM = pl.BlockSpec(memory_space=pltpu.VMEM)
SM = pl.BlockSpec(memory_space=pltpu.SMEM)
ANY = pl.BlockSpec(memory_space=pl.ANY)


def dot(a, b, da, db):
    return lax.dot_general(a, b, (((da,), (db,)), ((), ())), preferred_element_type=F32)


def pair_diagonal(a, b, da, db):
    both = dot(a, b, da, db)
    return both[0:HD, 0:HD], both[HD : 2 * HD, HD : 2 * HD]


def diagonal(a, b):
    zero = jnp.zeros_like(a)
    return jnp.concatenate(
        [jnp.concatenate([a, zero], axis=1), jnp.concatenate([zero, b], axis=1)], axis=0
    )


def pair_columns(p):
    return pl.ds(pl.multiple_of(p * 2 * HD, 2 * HD), 2 * HD)


def vmem(shape, dtype):
    return pltpu.VMEM(shape, dtype)


def half_shape(dtype):
    return vmem((TOK, WIDE), dtype)


def far(dtype=BF16):
    return jax.ShapeDtypeStruct((TOK, 2 * WIDE), dtype)


def call(kernel, name, flops, near, outs, distant=(), scratch=(), aliases=None):
    near = [pltpu.with_memory_space_constraint(a, pltpu.VMEM) for a in near]
    distant = [pltpu.with_memory_space_constraint(a, pltpu.HBM) for a in distant]
    out_specs = [ANY if isinstance(o, jax.ShapeDtypeStruct) else VM for o in outs]

    def placed(*refs):
        where = lax.axis_index("ctx")
        kernel((where & 1, (where >> 1) & 3, where >> 3), *refs)

    return pl.pallas_call(
        placed,
        in_specs=[VM] * len(near) + [ANY] * len(distant),
        out_specs=out_specs,
        out_shape=list(outs),
        scratch_shapes=list(scratch),
        input_output_aliases=aliases or {},
        compiler_params=pltpu.CompilerParams(vmem_limit_bytes=VMEM_LIMIT),
        cost_estimate=pl.CostEstimate(
            flops=int(flops), bytes_accessed=int(flops / 300), transcendentals=0
        ),
        name=name,
    )(*near, *distant)


def base_column(ids, flip):
    return pl.multiple_of((ids[0] ^ flip) * WIDE, WIDE)


def head_columns(h):
    return pl.ds(pl.multiple_of(h * HD, HD), HD)


def head_rows(h, rows=HD):
    return pl.ds(pl.multiple_of(h * rows, rows), rows)


def span(start, width):
    return pl.ds(pl.multiple_of(start, width), width)


def store_half(source, base, target, sem):
    return pltpu.make_async_copy(source, target.at[:, span(base, WIDE)], sem)


def load(source, base, at, target, sem, width=SPAN):
    return pltpu.make_async_copy(
        source.at[:, span(base + at, width)], target.at[:, span(at, width)], sem
    )


def store(source, at, base, target, sem, width=SPAN):
    return pltpu.make_async_copy(
        source.at[:, span(at, width)], target.at[:, span(base, width)], sem
    )


def info_tile(low, high):
    row = lax.broadcasted_iota(jnp.int32, (TILE, HD), 0)
    return jnp.where(
        row < 8, jnp.broadcast_to(low, (TILE, HD)), jnp.broadcast_to(high, (TILE, HD))
    ).astype(BF16)


def split_tile(x):
    high = x.astype(BF16).astype(F32)
    return jnp.concatenate([high, x - high], axis=0).astype(BF16)


def joined_tile(tile):
    t = tile.astype(F32)
    return t[0:8] + t[8:16]


def split_ends(seg_ref):
    seg = seg_ref[...].astype(F32)
    return seg[:, 0:1], seg[:, BLOCK - 1 : BLOCK], seg[:, BLOCK : BLOCK + 1], seg[:, TOK - 1 : TOK]


def flag(cond):
    return jnp.where(cond, 1.0, 0.0)


def fill_last_mask(seg_ref, ref):
    seg = seg_ref[...].astype(F32)
    row = lax.broadcasted_iota(jnp.int32, (BLOCK, HD), 0).astype(F32)
    for _, t in BLOCKS:
        block = seg[:, t]
        same = jnp.sum(flag(block == block[:, BLOCK - 1 : BLOCK]), axis=1, keepdims=True)
        ref[t, :] = flag(row >= BLOCK - same).astype(BF16)


def fill_token_masks(seg_ref, col, before, after, first):
    start0, end0, start1, end1 = split_ends(seg_ref)
    wide = jnp.broadcast_to(col, (TOK, HD))
    for ref, ids in ((before, (start0, end0)), (after, (start1, end1)), (first, (start0, start1))):
        for n, t in BLOCKS:
            ref[t, :] = flag(wide[t] == ids[n]).astype(BF16)


BLOCKS = ((0, slice(0, BLOCK)), (1, slice(BLOCK, TOK)))
FINE = 2
FINE_SPAN = FINE * HD


def state_kernel(flip, ids, *refs):
    if flip:
        k_far, v_far, seg_far, k, v, out, early, seg, last, sems, seg_sem = refs
    else:
        seg, last, k_far, v_far, k, v, out, early, sems = refs
    base = base_column(ids, flip)
    copies = [
        [
            pltpu.make_async_copy(far_ref.at[t, span(base, WIDE)], ref.at[t, :], sems.at[m, n])
            for m, (far_ref, ref) in enumerate(((k_far, k), (v_far, v)))
        ]
        for n, t in BLOCKS
    ]
    for pair in copies:
        for c in pair:
            c.start()
    if flip:
        copy = pltpu.make_async_copy(seg_far, seg, seg_sem)
        copy.start()
        copy.wait()
        fill_last_mask(seg, last)
    start0, end0, _, end1 = split_ends(seg)
    join = flag(end0 == end1)
    out[STATE_ROWS : STATE_ROWS + TILE, :] = info_tile(start0, end1)
    for n, t in BLOCKS:
        for c in copies[n]:
            c.wait()
        mask = jnp.concatenate([last[t, :]] * 2, axis=1)
        rows = [
            (k[t, pair_columns(p)] * mask, v[t, pair_columns(p)]) for p in range(HEADS // 2)
        ]
        parts = [part for kp, vp in rows for part in pair_diagonal(kp, vp, 0, 0)]
        if n == 1:
            parts = [two + early[head_rows(h), :] * join for h, two in enumerate(parts)]
        for h, part in enumerate(parts):
            if n == 0:
                early[head_rows(h), :] = part
            else:
                out[head_rows(h), :] = part.astype(BF16)


def local_state(k, v, seg, seg_vmem=None, last=None):
    flip = seg_vmem is None
    outs = [
        half_shape(BF16), half_shape(BF16), vmem((STATE_ROWS + TILE, HD), BF16),
        vmem((STATE_ROWS, HD), F32),
    ]
    scratch = [pltpu.SemaphoreType.DMA((2, 2))]
    near, distant = [seg_vmem, last], [k, v]
    if flip:
        outs += [vmem((1, TOK), jnp.int32), vmem((TOK, HD), BF16)]
        scratch += [pltpu.SemaphoreType.DMA]
        near, distant = [], [k, v, seg]
    return call(
        functools.partial(state_kernel, int(flip)), "local_state", 1e9, near, outs, distant, scratch
    )


def fill_masks(seg_ref, m0, m1, *masks):
    seg = seg_ref[...].astype(F32)
    col = jnp.transpose(jnp.broadcast_to(seg, (8, TOK)))[:, 0:1]
    fill_token_masks(seg_ref, col, *masks)
    t = lax.broadcasted_iota(jnp.int32, (BLOCK, BLOCK), 0)
    s = lax.broadcasted_iota(jnp.int32, (BLOCK, BLOCK), 1)
    for start, ref in ((0, m0), (BLOCK, m1)):
        same = col[start : start + BLOCK] == seg[:, start : start + BLOCK]
        ref[...] = flag(same & (s <= t)).astype(BF16)


def masked(left, right, mask):
    return dot(left, right, 1, 1).astype(BF16) * mask[...]


def intra_kernel(flip, ids, *refs):
    if flip:
        k, v, m0, m1, first, _, q_far, q, attn, w0, w1, qt, token, sems = refs
    else:
        k, v, seg, _, q_far, q, attn, w0, w1, qt, token, m0, m1, before, after, first, sems = refs
    base = base_column(ids, flip)
    for g in range(GROUPS):
        load(q_far, base, g * SPAN, q, sems.at[g]).start()
    if not flip:
        fill_masks(seg, m0, m1, before, after, first)
    token[...] = jnp.zeros_like(token)

    def body(g):
        load(q_far, base, g * SPAN, q, sems.at[g]).wait()
        group = [g * GROUP + j for j in range(GROUP)]
        rows = [[ref[:, head_columns(h)] for ref in (q, k, v)] for h in group]
        flipped = [jnp.transpose(qh * first[...]) for qh, _, _ in rows]
        weights = [[masked(qh[t], kh[t], (m0, m1)[n]) for n, t in BLOCKS] for qh, kh, _ in rows]
        sums = [
            [dot(w[n], vh[t], 1, 0) for n, t in BLOCKS] for w, (_, _, vh) in zip(weights, rows)
        ]
        for h, turned, w, a in zip(group, flipped, weights, sums):
            qt[head_rows(h), :] = turned
            for n, t in BLOCKS:
                (w0, w1)[n][head_rows(h, BLOCK), :] = w[n]
                attn[t, head_columns(h)] = a[n]

    for g in range(GROUPS):
        body(g)


TOKEN = vmem((8, HD), F32)


def intra(k, v, q, after, seg=None, masks=None):
    outs = [
        half_shape(BF16),
        half_shape(F32),
        vmem((HEADS * BLOCK, BLOCK), BF16),
        vmem((HEADS * BLOCK, BLOCK), BF16),
        vmem((STATE_ROWS, TOK), BF16),
        TOKEN,
    ]
    if masks is None:
        near = [k, v, seg, after]
        outs += [vmem((BLOCK, BLOCK), BF16)] * 2 + [vmem((TOK, HD), BF16)] * 3
    else:
        near = [k, v, *masks, after]
    return call(
        functools.partial(intra_kernel, int(masks is not None)), "intra", 3e9, near, outs, [q],
        [pltpu.SemaphoreType.DMA((GROUPS,))],
    )


def sigmoid_parts(gi):
    bend = 0.5 * jnp.tanh(0.5 * gi.astype(F32))
    return 0.5 + bend, 0.5 - bend


def prepare_kernel(ids, _, go_far, gi_far, w, gi, token, go, sems):
    pairs = ((go_far, go), (gi_far, gi))
    for g in range(2 * GROUPS):
        for n, (far_ref, ref) in enumerate(pairs):
            load(far_ref, 0, g * SPAN, ref, sems.at[n, g]).start()
    token[...] = jnp.zeros_like(token)

    def body(g):
        for n, (far_ref, ref) in enumerate(pairs):
            load(far_ref, 0, g * SPAN, ref, sems.at[n, g]).wait()
        for j in range(GROUP):
            c = head_columns(g * GROUP + j)
            w[:, c] = go[:, c].astype(F32) * sigmoid_parts(gi[:, c])[0]

    for g in range(2 * GROUPS):
        body(g)


def prepare(after, go, gi):
    return call(
        prepare_kernel, "prepare", 3e9, [after],
        [vmem((TOK, 2 * WIDE), F32), vmem((TOK, 2 * WIDE), BF16), TOKEN], [go, gi],
        [pltpu.VMEM((TOK, 2 * WIDE), BF16), pltpu.SemaphoreType.DMA((2, 2 * GROUPS))],
    )


def cross_kernel(flip, ids, attn_in, q, s, early, w, before, seg, gain, *rest):
    if flip:
        squares_in, inners_in, attn, second, sums, squares, inners = rest
        squares[...] = squares_in[...]
        inners[...] = inners_in[...]
    else:
        attn, second, squares, inners = rest
        squares[...] = jnp.zeros_like(squares)
        inners[...] = jnp.zeros_like(inners)
    base = base_column(ids, flip)
    start0, end0, _, _ = split_ends(seg)
    join = flag(start0 == end0)

    def body(g):
        group = [g * GROUP + j for j in range(GROUP)]
        ones = [s[head_rows(h), :] for h in group]
        twos = [
            (early[head_rows(h), :] + one.astype(F32) * join).astype(BF16)
            for h, one in zip(group, ones)
        ]
        mask = jnp.concatenate([before[...]] * 2, axis=1)
        rows = [q[:, pair_columns(g * (GROUP // 2) + j)] * mask for j in range(GROUP // 2)]
        for n, t in BLOCKS:
            states = (ones, twos)[n]
            hops = []
            for j, qp in enumerate(rows):
                hop = dot(qp[t], diagonal(states[2 * j], states[2 * j + 1]), 1, 0)
                hops += [hop[:, 0:HD], hop[:, HD : 2 * HD]]
            sums = [attn_in[t, head_columns(h)] + hop for h, hop in zip(group, hops)]
            square, inner = squares[t, :], inners[t, :]
            for h, a in zip(group, sums):
                far_c = span(base + h * HD, HD)
                square = square + a * a
                inner = inner + w[t, far_c] * a * gain[:, far_c]
            squares[t, :] = square
            inners[t, :] = inner
            for h, a in zip(group, sums):
                attn[t, head_columns(h)] = a
        for h, two in zip(group, twos):
            second[head_rows(h), :] = two

    for g in range(GROUPS):
        body(g)
    if flip:
        ones = jnp.ones((8, HD), BF16)
        totals = []
        for x in (squares[...], inners[...]):
            high = x.astype(BF16)
            low = (x - high.astype(F32)).astype(BF16)
            totals.append(dot(ones, high, 1, 1) + dot(ones, low, 1, 1))
        row = lax.broadcasted_iota(jnp.int32, (8, HD), 0)
        for n in range(8):
            total = totals[n // 4][:, (n % 4) * HD : (n % 4 + 1) * HD]
            packed = total if n == 0 else jnp.where(row == n, total, packed)
        sums[...] = packed


def cross(flip, attn, q, state, early, w, before, seg, gain, previous=()):
    total = vmem((TOK, HD), F32)
    outs = [half_shape(F32), vmem((STATE_ROWS, HD), BF16)]
    return call(
        functools.partial(cross_kernel, flip), "cross", 1.2e9,
        [attn, q, state, early, w, before, seg, gain, *previous],
        outs + ([vmem((8, HD), F32)] if flip else [total, total]), (),
        [pltpu.VMEM((TOK, HD), F32)] * 2 if flip else [],
    )


def scales(sums, rinv_ref, back_ref):
    own, two, three, one = [r[...] for r in sums]
    total = (own + one) + (two + three)
    rinv = lax.rsqrt(total[0:4] * (1.0 / ATT) + EPSILON)
    back = rinv * rinv * rinv * total[4:8] * (1.0 / ATT)
    cols = jnp.transpose(jnp.concatenate([rinv, back], axis=0))
    for n in range(4):
        rinv_ref[n * HD : (n + 1) * HD, :] = jnp.broadcast_to(cols[:, n : n + 1], (HD, HD))
        back_ref[n * HD : (n + 1) * HD, :] = jnp.broadcast_to(cols[:, n + 4 : n + 5], (HD, HD))


def grad_kernel(flip, ids, seg, attn, w, qt, gain, *rest):
    if flip:
        s0, s1, s2, s3, grad, out, late, rinv, back, gains = rest
        scales((s0, s1, s2, s3), rinv, back)
    else:
        rinv, back, grad, out, late, gains = rest
    base = base_column(ids, flip)
    start0, _, start1, end1 = split_ends(seg)
    join = flag(start0 == start1)
    out[STATE_ROWS : STATE_ROWS + TILE, :] = info_tile(8.0 - end1, 8.0 - start0)

    def body(g):
        group = [g * GROUP + j for j in range(GROUP)]
        turned = [qt[head_rows(g * (GROUP // 2) + j, 2 * HD), :] for j in range(GROUP // 2)]
        totals, rows = [], []
        for h in group:
            far_c = span(base + h * HD, HD)
            a = attn[:, head_columns(h)]
            gated = w[:, far_c] * rinv[...]
            totals.append(jnp.sum(gated * a, axis=0, keepdims=True))
            rows.append((gated * gain[:, far_c] - a * back[...]).astype(BF16))
        parts = []
        for j, qp in enumerate(turned):
            xp = jnp.concatenate(rows[2 * j : 2 * j + 2], axis=1)
            parts += zip(*[pair_diagonal(qp[:, t], xp[t], 1, 0) for _, t in BLOCKS])
        for h, total, x, (one, two) in zip(group, totals, rows, parts):
            gains[pl.ds(h, 1), :] = total
            grad[:, head_columns(h)] = x
            late[head_rows(h), :] = two
            out[head_rows(h), :] = (one + two * join).astype(BF16)

    for g in range(GROUPS):
        body(g)
    out[STATE_ROWS + TILE : STATE_ROWS + 2 * TILE, :] = split_tile(gains[...])


def grad_attn(flip, seg, attn, w, qt, gain, extra):
    outs = [
        half_shape(BF16), vmem((STATE_ROWS + 2 * TILE, HD), BF16), vmem((STATE_ROWS, HD), F32)
    ]
    if flip:
        outs += [vmem((TOK, HD), F32), vmem((TOK, HD), F32)]
    return call(
        functools.partial(grad_kernel, flip), "grad_attn", 1.2e9,
        [seg, attn, w, qt, gain, *extra], outs, (), [pltpu.VMEM((8, HD), F32)],
    )


def local_grads_kernel(flip, ids, q, k, v, grad, s0, s1, w0, w1, m0, m1, before, _, *rest):
    if flip:
        dq_keep, dq_far, dq, dk, dv, token, sems = rest
        keep_copy = store_half(dq_keep, base_column(ids, 0), dq_far, sems.at[1])
        keep_copy.start()
        first_copy = store(dq, 0, base_column(ids, 1), dq_far, sems.at[0])
    else:
        dq, dk, dv, token = rest
    token[...] = jnp.zeros_like(token)

    def body(g):
        group = [g * GROUP + j for j in range(GROUP)]
        rows = [[ref[:, head_columns(h)] for ref in (q, k, v, grad)] for h in group]
        states = [[ref[head_rows(h), :] for ref in (s0, s1)] for h in group]
        weights = [[ref[head_rows(h, BLOCK), :] for ref in (w0, w1)] for h in group]
        inner = [
            [masked(gh[t], vh[t], (m0, m1)[n]) for n, t in BLOCKS] for _, _, vh, gh in rows
        ]
        outs = []
        for (qh, kh, _, gh), state, w, d in zip(rows, states, weights, inner):
            cut = gh * before[...]
            outs.append(
                [
                    (
                        dot(d[n], kh[t], 1, 0) + dot(cut[t], state[n], 1, 1),
                        dot(d[n], qh[t], 0, 0),
                        dot(w[n], gh[t], 0, 0),
                    )
                    for n, t in BLOCKS
                ]
            )
        for h, blocks in zip(group, outs):
            c = head_columns(h)
            for (n, t), (x, y, z) in zip(BLOCKS, blocks):
                dq[t, c] = x.astype(BF16)
                dk[t, c] = y
                dv[t, c] = z
        if flip and g == 0:
            first_copy.start()

    for g in range(GROUPS):
        body(g)
    if flip:
        first_copy.wait()
        keep_copy.wait()


def local_grads(flip, q, k, v, g, states, weights, masks, before, after, dq_keep=()):
    near = [q, k, v, g, *states, *weights, *masks, before, after, *dq_keep]
    outs = [half_shape(BF16), half_shape(F32), half_shape(F32), TOKEN]
    return call(
        functools.partial(local_grads_kernel, flip), "local_grads", 5e9, near,
        [far()] * flip + outs, (), [pltpu.SemaphoreType.DMA((2,))] * flip,
    )


def gates_kernel(
    ids, keep, send, gi, w, rinv, gain, dq, _, dq_in, lo_far, gg_far, dq_far, token, lo, gg, sems,
    dq_sem
):
    token[...] = jnp.zeros_like(token)
    at = (GROUPS - 1) * SPAN
    copies = [store(dq, at, base_column(ids, 1) + at, dq_far, dq_sem)]
    copies[0].start()
    for flip, attn in enumerate((keep, send)):
        base = base_column(ids, flip)

        def body(g, flip=flip, attn=attn, base=base):
            for j in range(GROUP):
                h = g * GROUP + j
                far_c = span(base + h * HD, HD)
                out_c = head_columns(flip * HEADS + h)
                sig, other = sigmoid_parts(gi[:, far_c])
                scaled = attn[:, head_columns(h)] * rinv[...] * gain[:, far_c]
                lo[:, out_c] = (scaled * sig).astype(BF16)
                gg[:, out_c] = (scaled * w[:, far_c] * other).astype(BF16)
            at, to = flip * WIDE + g * SPAN, base + g * SPAN
            store(lo, at, to, lo_far, sems.at[0, flip, g]).start()
            store(gg, at, to, gg_far, sems.at[1, flip, g]).start()

        for g in range(GROUPS):
            body(g)
        for g in range(GROUPS):
            at, to = flip * WIDE + g * SPAN, base + g * SPAN
            copies.append(store(lo, at, to, lo_far, sems.at[0, flip, g]))
            copies.append(store(gg, at, to, gg_far, sems.at[1, flip, g]))
    for copy in copies:
        copy.wait()


def gates(keep, send, gi, w, rinv, gain, dq, after, dq_far):
    near = [keep, send, gi, w, rinv, gain, dq, after]
    return call(
        gates_kernel, "gates", 3e9, near, [far(), far(), far(), TOKEN], [dq_far],
        [
            pltpu.VMEM((TOK, 2 * WIDE), BF16),
            pltpu.VMEM((TOK, 2 * WIDE), BF16),
            pltpu.SemaphoreType.DMA((2, 2, GROUPS)),
            pltpu.SemaphoreType.DMA,
        ],
        {len(near): 2},
    )


def finish_kernel(flip, ids, dk_in, dv_in, k, v, later, late, seg, after, *rest):
    if flip:
        total, _, _, dk_far, dv_far, gain_far, dk, dv, sems, gain, gain_sem = rest
        core = ids[0]
        at = [pl.ds(pl.multiple_of(n * 8, 8), 8) for n in (core, 1 - core)]
        gain[at[0], :] = joined_tile(total[...])
        gain[at[1], :] = joined_tile(later[STATE_ROWS : STATE_ROWS + TILE, :])
        gain_copy = pltpu.make_async_copy(gain, gain_far, gain_sem)
        gain_copy.start()
    else:
        dk_far, dv_far, dk, dv, sems = rest
    base = base_column(ids, flip)
    _, _, start1, end1 = split_ends(seg)
    join = flag(start1 == end1)
    copies = []
    for g in range(HEADS // FINE):
        group = range(g * FINE, (g + 1) * FINE)
        states = []
        for h in group:
            one = later[head_rows(h), :]
            states.append(
                ((late[head_rows(h), :] + one.astype(F32) * join).astype(BF16), one)
            )
        mask = jnp.concatenate([after[...]] * 2, axis=1)
        kp, vp = k[:, pair_columns(g)] * mask, v[:, pair_columns(g)] * mask
        hops = ([], [])
        for n, t in BLOCKS:
            both = diagonal(states[0][n], states[1][n])
            x, y = dot(vp[t], both, 1, 1), dot(kp[t], both, 1, 0)
            hops[0].append((x[:, 0:HD], y[:, 0:HD]))
            hops[1].append((x[:, HD : 2 * HD], y[:, HD : 2 * HD]))
        sums = [
            [
                (dk_in[t, head_columns(h)] + hop[n][0], dv_in[t, head_columns(h)] + hop[n][1])
                for n, t in BLOCKS
            ]
            for h, hop in zip(group, hops)
        ]
        for h, blocks in zip(group, sums):
            for (_, t), (x, y) in zip(BLOCKS, blocks):
                dk[t, head_columns(h)] = x.astype(BF16)
                dv[t, head_columns(h)] = y.astype(BF16)
        for n, (ref, far_ref) in enumerate(((dk, dk_far), (dv, dv_far))):
            at = g * FINE_SPAN
            copy = store(ref, at, base + at, far_ref, sems.at[n, g], FINE_SPAN)
            copy.start()
            copies.append(copy)
    for copy in copies:
        copy.wait()
    if flip:
        gain_copy.wait()


def finish(flip, dk, dv, k, v, later, late, seg, after, total=(), done=()):
    near = [dk, dv, k, v, later, late, seg, after, *total]
    outs = [far(), far()]
    scratch = [
        pltpu.VMEM((TOK, WIDE), BF16),
        pltpu.VMEM((TOK, WIDE), BF16),
        pltpu.SemaphoreType.DMA((2, HEADS // FINE)),
    ]
    if flip:
        outs += [jax.ShapeDtypeStruct((TILE, HD), F32)]
        scratch += [pltpu.VMEM((TILE, HD), F32), pltpu.SemaphoreType.DMA]
    return call(
        functools.partial(finish_kernel, flip), "finish", 1.2e9, near, outs, done, scratch,
        {len(near): 0, len(near) + 1: 1} if flip else None,
    )


def place(ids, reverse):
    core, x, z = ids[0], ids[1], ids[2]
    return (1 - core, 3 - x, 3 - z) if reverse else (core, x, z)


def info_rows(ref, at):
    tile = ref[at : at + TILE, :].astype(F32)
    return tile[0:1], tile[8:9]


def sorted_cores(first_core, own, other):
    return jnp.where(first_core, own, other), jnp.where(first_core, other, own)


def quarter_rows(ids, m):
    return pl.ds(pl.multiple_of((ids[1] ^ m) * QUARTER, QUARTER), QUARTER)


def chip_kernel(reverse, gain, ids, own_ref, other_ref, *outs):
    vcore, _, _ = place(ids, reverse)
    first_core = vcore == 0
    low_own, high_own = info_rows(own_ref, STATE_ROWS)
    low_other, high_other = info_rows(other_ref, STATE_ROWS)
    low_a, _ = sorted_cores(first_core, low_own, low_other)
    high_a, high_b = sorted_cores(first_core, high_own, high_other)
    join = flag(high_a == high_b)
    own_weight = jnp.where(first_core, join, 1.0)
    other_weight = jnp.where(first_core, 1.0, join)
    for m, out in enumerate(outs):
        rows = quarter_rows(ids, m)
        total = own_ref[rows, :].astype(F32) * own_weight
        total = total + other_ref[rows, :].astype(F32) * other_weight
        out[0:QUARTER, :] = total.astype(BF16)
        out[QUARTER : QUARTER + TILE, :] = info_tile(low_a, high_b)
        if gain:
            at = slice(STATE_ROWS + TILE, STATE_ROWS + 2 * TILE)
            both = joined_tile(own_ref[at, :]) + joined_tile(other_ref[at, :])
            out[QUARTER + TILE : QUARTER + 2 * TILE, :] = split_tile(both)


def row_kernel(gain, ids, p0, p2, p3, p1, _, out):
    parts = (p0, p1, p2, p3)
    info = [info_rows(p, QUARTER) for p in parts]
    low = jnp.minimum(jnp.minimum(info[0][0], info[1][0]), jnp.minimum(info[2][0], info[3][0]))
    high = jnp.maximum(jnp.maximum(info[0][1], info[1][1]), jnp.maximum(info[2][1], info[3][1]))
    total = None
    for p, (_, own_high) in zip(parts, info):
        term = p[0:QUARTER, :].astype(F32) * flag(own_high == high)
        total = term if total is None else total + term
    out[0:QUARTER, :] = total.astype(BF16)
    out[QUARTER : QUARTER + TILE, :] = info_tile(low, high)
    if gain:
        g = [joined_tile(p[QUARTER + TILE : QUARTER + 2 * TILE, :]) for p in parts]
        out[QUARTER + TILE : QUARTER + 2 * TILE, :] = split_tile((g[0] + g[1]) + (g[2] + g[3]))


def entry_kernel(reverse, gain, ids, p0, p2, p3, p1, *rest):
    _, vx, vz = place(ids, reverse)
    parts = (p0, p1, p2, p3)
    outs = rest[-5 if gain else -4 :]
    if gain:
        rows = rest[1:4]
        earlier = [(vz ^ n) < vz for n in FAR_FIRST[1:]]
    else:
        rows = rest[1:3]
        earlier = [vz >= 2, vz >= 1]
    info = [info_rows(p, QUARTER) for p in parts]
    row_high = [info_rows(t, QUARTER)[1] for t in rows]
    for m in range(4):
        low = info[m][0]
        total = jnp.zeros((QUARTER, HD), F32)
        for n in range(4):
            if n != m:
                weight = flag(info[n][1] == low) * flag((vx ^ n) < (vx ^ m))
                total = total + parts[n][0:QUARTER, :].astype(F32) * weight
        for row, high, before in zip(rows, row_high, earlier):
            weight = flag(high == low) * flag(before)
            total = total + row[0:QUARTER, :].astype(F32) * weight
        outs[m][...] = total.astype(BF16)
    if gain:
        tiles = [joined_tile(t[QUARTER + TILE : QUARTER + 2 * TILE, :]) for t in rest[0:4]]
        g = [tiles[FAR_FIRST.index(m)] for m in range(4)]
        outs[4][...] = split_tile((g[0] + g[1]) + (g[2] + g[3]))


def device_kernel(reverse, gain, ids, own_ref, other_ref, e0, e2, e3, e1, _, *rest):
    keep, send = rest[-2:]
    vcore, _, _ = place(ids, reverse)
    first_core = vcore == 0
    low_own, high_own = info_rows(own_ref, STATE_ROWS)
    low_other, high_other = info_rows(other_ref, STATE_ROWS)
    low_a, low_b = sorted_cores(first_core, low_own, low_other)
    high_a, _ = sorted_cores(first_core, high_own, high_other)
    from_a = flag(high_a == low_b)
    from_chip = flag(low_a == low_b)
    for m, ref in enumerate((e0, e1, e2, e3)):
        rows = quarter_rows(ids, m)
        entry = ref[...].astype(F32)
        a = jnp.where(first_core, own_ref[rows, :].astype(F32), other_ref[rows, :].astype(F32))
        second = a * from_a + entry * from_chip
        keep[rows, :] = jnp.where(first_core, entry, second).astype(BF16)
        send[rows, :] = jnp.where(first_core, second, entry).astype(BF16)
    if gain:
        send[STATE_ROWS : STATE_ROWS + TILE, :] = rest[0][...]


def glue(kernel, name, rows, *args):
    return call(kernel, name, 5e8, args, [vmem((r, HD), BF16) for r in rows])


def swap(x, axis, size, bits):
    return lax.ppermute(x, axis, [(i, i ^ bits) for i in range(size)])


FAR_FIRST = (0, 2, 3, 1)


def swap_all(arrays, send):
    return [arrays[0]] + [send(arrays[m], m) for m in FAR_FIRST[1:]]


def chip_swap(x):
    return swap(x, "ctx", 32, 1)


def row_swap(x, m):
    return swap(x, "ctx", 32, m << 1)


def plane_swap(x, m):
    return swap(x, "ctx", 32, m << 3)


def plane_shift(x):
    return lax.ppermute(x, "ctx", [(i, (i + 8) % 32) for i in range(32)])


def scan(own, other, reverse, gain, beside_x, beside_z, beside_back):
    extra = TILE if gain else 0
    rows = QUARTER + TILE + extra
    sent = glue(
        functools.partial(chip_kernel, reverse, gain), "chip_sum", [rows] * 4, own, other
    )
    parts = swap_all(sent, row_swap)
    token = beside_x(sent[0])
    total = glue(functools.partial(row_kernel, gain), "row_sum", [rows], *parts, token)[0]
    if gain:
        totals = swap_all([total] * 4, plane_swap)
    else:
        second = plane_swap(total, 2)
        totals = [total, second, plane_shift(total)]
    token = beside_z(total)
    entries = glue(
        functools.partial(entry_kernel, reverse, gain),
        "entry",
        [QUARTER] * 4 + ([TILE] if gain else []),
        *parts,
        *totals,
        token,
    )
    tail = entries[4:]
    back = swap_all(entries, row_swap)
    token = beside_back(entries[0])
    keep, send = glue(
        functools.partial(device_kernel, reverse, gain),
        "device_entry",
        [STATE_ROWS, STATE_ROWS + extra],
        own,
        other,
        *back,
        token,
        *tail,
    )
    return keep, chip_swap(send), tail


def on_device(query, keys, values, gate_input, grad_output, norm_gain, segment_ids):
    gain = norm_gain.reshape(1, -1)

    k_send, v_send, sent, early_send, seg, last = local_state(
        keys, values, segment_ids.reshape(1, TOK)
    )
    other = chip_swap(sent)
    k_keep, v_keep, own, early_keep = local_state(keys, values, None, seg, last)
    made = {}

    def intra_keep(token):
        made["keep"] = intra(k_keep, v_keep, query, token, seg=seg)
        return made["keep"][5]

    def intra_send(token):
        m0, m1, _, _, first = made["keep"][6:]
        made["send"] = intra(k_send, v_send, query, token, masks=(m0, m1, first))
        return made["send"][5]

    def prepare_both(token):
        made["gate"] = prepare(token, grad_output, gate_input)
        return made["gate"][2]

    state_keep, state_send, _ = scan(own, other, False, False, intra_keep, intra_send, prepare_both)
    q_keep, attn_keep, w0_keep, w1_keep, qt_keep, _, *masks, before, after, _ = made["keep"]
    q_send, attn_send, w0_send, w1_send, qt_send, _ = made["send"]
    gated, gate, _ = made["gate"]

    attn_keep, second_keep, *sums = cross(
        0, attn_keep, q_keep, state_keep, early_keep, gated, before, seg, gain
    )
    attn_send, second_send, sums = cross(
        1, attn_send, q_send, state_send, early_send, gated, before, seg, gain, sums
    )
    sums = swap_all([sums] * 4, lambda x, m: swap(x, "tp", 4, m))

    g_send, sent, late_send, rinv, back = grad_attn(
        1, seg, attn_send, gated, qt_send, gain, sums
    )
    other = chip_swap(sent)
    g_keep, own, late_keep = grad_attn(0, seg, attn_keep, gated, qt_keep, gain, (rinv, back))

    def grads_keep(token):
        made["gk"] = local_grads(
            0, q_keep, k_keep, v_keep, g_keep, (state_keep, second_keep), (w0_keep, w1_keep),
            masks, before, token,
        )
        return made["gk"][3]

    def grads_send(token):
        made["gs"] = local_grads(
            1, q_send, k_send, v_send, g_send, (state_send, second_send), (w0_send, w1_send),
            masks, before, token, (made["gk"][0],),
        )
        return made["gs"][4]

    def gates_both(token):
        made["out"] = gates(
            attn_keep, attn_send, gate, gated, rinv, gain, made["gs"][1], token, made["gs"][0]
        )
        return made["out"][3]

    later_keep, later_send, total = scan(
        own, other, True, True, grads_keep, grads_send, gates_both
    )
    _, dk_keep, dv_keep, _ = made["gk"]
    _, _, dk_send, dv_send, _ = made["gs"]
    layer_out, grad_gate, grad_query, _ = made["out"]
    done = finish(0, dk_keep, dv_keep, k_keep, v_keep, later_keep, late_keep, seg, after)
    grad_keys, grad_values, grad_gain = finish(
        1, dk_send, dv_send, k_send, v_send, later_send, late_send, seg, after, (total[0],),
        tuple(done),
    )
    grad_gain = grad_gain.reshape(-1)
    return layer_out, grad_query, grad_keys, grad_values, grad_gate, grad_gain


def solution(mesh):
    in_specs = (P("ctx", "tp"),) * 5 + (P("tp"), P("ctx"))
    out_specs = (P("ctx", "tp"),) * 5 + (P("tp"),)
    return jax.shard_map(
        on_device, mesh=mesh, in_specs=in_specs, out_specs=out_specs, check_vma=False
    )
```
